128 devices in a mesh: stream: 32 (over z, x, core), span: 4 (over y).
Axes of the slice: x: 4, y: 4, z: 4, core: 2. Of those that a mesh axis runs over, the one named last changes fastest.
Arguments:
- q_now: float32 [5, 512, 128, 128], P(None, 'stream', 'span'), may hold values from -4 to 4
- q_prev: float32 [5, 512, 128, 128], P(None, 'stream', 'span'), may hold values from -4 to 4
- jacobians: float32 [3, 5, 5], replicated, may hold values from -2.5 to 2.5
- fractions: float32 [3, 128, 4096], P(None, ('stream', 'span')), may hold values from 0 to 0.9
- send_blocks: int32 [128, 4096], P(('stream', 'span')), may hold values from -1 to 8191, as said below
- recv_blocks: int32 [128, 4096], P(('stream', 'span')), may hold values from -1 to 8191, as said below
Outputs:
- q_next: float32 [5, 512, 128, 128], P(None, 'stream', 'span')
The draws below stay inside these ranges and needn't reach their ends.
Inputs may be any that keep to these rules, and one draw needn't show every extreme that they name: In each row of send_blocks, the 32 slots to one destination hold valid brick indices first and -1 after them; a device sends only to devices whose streamwise rank differs from its own by at most 2, and to the device whose rank differs from its own by 64, which always receives exactly 32 valid slots from it; the busiest receivers get several times the mean. recv_blocks[r, s * 32 + k] is -1 exactly where send_blocks[s, r * 32 + k] is; the valid entries of one row are distinct.
All inputs are finite; a program needn't handle non-finite values.
Results may differ from the reference program's by a relative error of at most 0.0003.
Values sent between devices are 32-bit elements; how exact they have to be, the bound alone decides.
A program may use at most 192 MiB of HBM per device.

```python
import jax
import jax.numpy as jnp
from jax import lax

CX = 16
CY = 32
CZ = 128
SLOT = 32
RANKS = 128
BLOCKS_DEV = 8192
NX = 512
NY = 128
NZ = 128
N_STREAM = 32
N_SPAN = 4


def field_values(key):
    shape = (5, NX, NY, NZ)
    values = jnp.clip(jax.random.normal(key, shape, jnp.float32), -4.0, 4.0)
    return values


def draw_q_now(key, part):
    return field_values(jax.random.fold_in(key, 21))


def draw_q_prev(key, part):
    return field_values(jax.random.fold_in(key, 22))


def donor_tables(key):
    ranks = jnp.arange(RANKS, dtype=jnp.int32)
    stream_rank = ranks // N_SPAN
    source_row = stream_rank[:, None]
    target_row = stream_rank[None, :]
    near = jnp.abs(source_row - target_row) <= 2
    opposite = (ranks[:, None] - ranks[None, :]) % RANKS == RANKS // 2
    base = jax.random.randint(jax.random.fold_in(key, 11), (RANKS, RANKS), 0, SLOT + 1)
    level = jnp.left_shift(jnp.int32(1), jax.random.randint(jax.random.fold_in(key, 12), (1, RANKS), 0, 4))
    counts = jnp.minimum(SLOT, base * level // 4)
    busiest = jax.random.randint(jax.random.fold_in(key, 13), (), 0, RANKS)
    counts = jnp.where(ranks[None, :] == busiest, SLOT, counts)
    counts = jnp.where(near, counts, 0)
    counts = jnp.where(opposite, SLOT, counts)
    live = jnp.arange(SLOT)[None, None, :] < counts[:, :, None]
    half_x = CX // 2
    face_depth = jax.random.randint(jax.random.fold_in(key, 16), (RANKS, RANKS, SLOT), 0, 2)
    anywhere_x = jax.random.randint(jax.random.fold_in(key, 17), (RANKS, RANKS, SLOT), 0, half_x)
    upstream = (source_row < target_row)[:, :, None]
    downstream = (source_row > target_row)[:, :, None]
    brick_x = jnp.where(upstream, half_x - 1 - face_depth, jnp.where(downstream, face_depth, anywhere_x))
    brick_y = jax.random.randint(jax.random.fold_in(key, 18), (RANKS, RANKS, SLOT), 0, CY // 2)
    brick_z = jax.random.randint(jax.random.fold_in(key, 19), (RANKS, RANKS, SLOT), 0, CZ // 2)
    picks = (brick_x * (CY // 2) + brick_y) * (CZ // 2) + brick_z
    sending = jnp.where(live, picks, -1).reshape(RANKS, RANKS * SLOT)
    row_keys = jax.random.split(jax.random.fold_in(key, 15), RANKS)
    orders = jax.vmap(lambda row_key: jax.random.permutation(row_key, BLOCKS_DEV)[:RANKS * SLOT])(row_keys)
    live_back = live.transpose(1, 0, 2).reshape(RANKS, RANKS * SLOT)
    receiving = jnp.where(live_back, orders, -1)
    return (sending.astype(jnp.int32), receiving.astype(jnp.int32))


def draw_send_blocks(key, part):
    return donor_tables(jax.random.fold_in(key, 7))[0]


def draw_recv_blocks(key, part):
    return donor_tables(jax.random.fold_in(key, 7))[1]


def levels(own_key, dims, pieces, least, high):
    gain, own = 1.0, jax.random.fold_in(own_key, 6)
    for dim, parts in pieces:
        steps = jnp.exp(jax.random.uniform(jax.random.fold_in(own, dim), (parts,), jnp.float32, least / len(pieces), high / len(pieces)))
        gain = gain * jnp.repeat(steps, dims[dim] // parts).reshape([-1 if axis == dim else 1 for axis in range(len(dims))])
    return gain


def gaussian(key, shape, spread, limit, held_as=jnp.bfloat16):
    result = spread * jax.random.normal(key, shape, jnp.float32)
    return jnp.clip(result, min=-limit, max=limit).astype(held_as)


def setup_inputs(seed: int = 0) -> dict:
    key_of = jax.random.split(jax.random.key(seed), 7)
    q_now = draw_q_now(jax.random.fold_in(key_of[6], 71), 0)
    q_prev = draw_q_prev(jax.random.fold_in(key_of[6], 71), 0)
    jacobians = gaussian(key_of[2], (3, 5, 5), 5 ** -0.5, 2.5, jnp.float32)
    fractions = jnp.clip(0.9 * jax.random.uniform(key_of[3], (3, RANKS, RANKS * SLOT), jnp.float32) ** levels(key_of[3], (3, RANKS, RANKS * SLOT), ((1, 128),), -0.2, 0.2), 0.0, 0.9)
    send_blocks = draw_send_blocks(jax.random.fold_in(key_of[6], 71), 0)
    recv_blocks = draw_recv_blocks(jax.random.fold_in(key_of[6], 71), 0)
    return dict(q_now=q_now, q_prev=q_prev, jacobians=jacobians, fractions=fractions, send_blocks=send_blocks, recv_blocks=recv_blocks)


FILTER_WEIGHTS = [1.0, -10.0, 45.0, -120.0, 210.0, -252.0, 210.0, -120.0, 45.0, -10.0, 1.0]
SIGMA = 0.6


def interpolate(values, fractions):
    slots = values.shape[1]
    cube = values.reshape(2, 2, 2, 10, slots)
    shift_x = fractions[0]
    shift_y = fractions[1]
    shift_z = fractions[2]
    lower = (1.0 - shift_x) * cube[0] + shift_x * cube[1]
    cube = jnp.stack([lower, cube[1]], 0)
    lower = (1.0 - shift_y) * cube[:, 0] + shift_y * cube[:, 1]
    cube = jnp.stack([lower, cube[:, 1]], 1)
    lower = (1.0 - shift_z) * cube[:, :, 0] + shift_z * cube[:, :, 1]
    cube = jnp.stack([lower, cube[:, :, 1]], 2)
    return cube.reshape(80, slots)


def place(bricks, values, targets):
    total = bricks.shape[1]
    where = jnp.where(targets >= 0, targets, total).astype(jnp.int32)
    return bricks.at[:, where].set(values, mode="drop")


def fourth(ext, axis):
    size = ext.shape[axis]

    def part(shift):
        return lax.slice_in_dim(ext, 2 + shift, size - 2 + shift, axis=axis)

    return (8.0 * (part(1) - part(-1)) - (part(2) - part(-2))) / 12.0


def rates(ext, jacobians):
    slope_x = fourth(ext[:, :, 2:-2, 2:-2], 1)
    slope_y = fourth(ext[:, 2:-2, :, 2:-2], 2)
    slope_z = fourth(ext[:, 2:-2, 2:-2, :], 3)
    high = lax.Precision.HIGHEST
    total = jnp.einsum("vw,wxyz->vxyz", jacobians[0], slope_x, precision=high)
    total = total + jnp.einsum("vw,wxyz->vxyz", jacobians[1], slope_y, precision=high)
    total = total + jnp.einsum("vw,wxyz->vxyz", jacobians[2], slope_z, precision=high)
    return -total


def tenth(ext, axis):
    size = ext.shape[axis]
    total = FILTER_WEIGHTS[0] * lax.slice_in_dim(ext, 0, size - 10, axis=axis)
    for offset in range(1, 11):
        total = total + FILTER_WEIGHTS[offset] * lax.slice_in_dim(ext, offset, size - 10 + offset, axis=axis)
    return total


def smooth(ext):
    along_x = tenth(ext[:, :, 5:-5, 5:-5], 1)
    along_y = tenth(ext[:, 5:-5, :, 5:-5], 2)
    along_z = tenth(ext[:, 5:-5, 5:-5, :], 3)
    centre = ext[:, 5:-5, 5:-5, 5:-5]
    return centre + (SIGMA / 1024.0) * (along_x + along_y + along_z)


def reference(q_now, q_prev, jacobians, fractions, send_blocks, recv_blocks):
    fields = jnp.concatenate([q_now, q_prev], 0)
    split = fields.reshape(10, N_STREAM, CX // 2, 2, N_SPAN, CY // 2, 2, CZ // 2, 2)
    bricks = split.transpose(1, 4, 3, 6, 8, 0, 2, 5, 7).reshape(RANKS, 80, BLOCKS_DEV)
    donors = jax.vmap(lambda brick, picks: brick[:, jnp.maximum(picks, 0).astype(jnp.int32)])(bricks, send_blocks)
    donors = donors.reshape(RANKS, 80, RANKS, SLOT).transpose(2, 1, 0, 3).reshape(RANKS, 80, RANKS * SLOT)
    fresh = jax.vmap(interpolate)(donors, fractions.transpose(1, 0, 2))
    bricks = jax.vmap(place)(bricks, fresh, recv_blocks)
    split = bricks.reshape(N_STREAM, N_SPAN, 2, 2, 2, 10, CX // 2, CY // 2, CZ // 2)
    fields = split.transpose(5, 0, 6, 2, 1, 7, 3, 8, 4).reshape(10, NX, NY, NZ)
    current = fields[:5]
    older = fields[5:]
    ext = jnp.pad(current, ((0, 0), (2, 2), (2, 2), (2, 2)))
    rhs = rates(ext, jacobians)
    pre = (4.0 * current - older + rhs) / 3.0
    return smooth(jnp.pad(pre, ((0, 0), (5, 5), (5, 5), (5, 5))))
```

```python
import functools

import jax
import jax.numpy as jnp
from jax import lax
from jax.experimental import pallas as pl
from jax.experimental.pallas import tpu as pltpu
from jax.sharding import PartitionSpec as P

MESH = pl.DeviceIdType.MESH
F32 = jnp.float32
VARS = 5
CHANS = 10
SLOT = 32
REACH = 2
GROUPS = 2 * REACH + 1
CX, CY, CZ = 16, 32, 128
BX, BY = CX // 2, CY // 2
ROW = 2 * CHANS
BRICK = 2 * ROW
ROWS = BX * CY * ROW
PAD = 8
WY = CY + 2 * PAD
NEAR, FAR = 2, 5
SCALE = 0.6 / 1024.0
TAPS = (-252.0, 210.0, -120.0, 45.0, -10.0, 1.0)


def lanes(shape):
    return lax.broadcasted_iota(jnp.int32, shape, len(shape) - 1)


def window_start(i, n_stream):
    return jnp.minimum(jnp.maximum(i - REACH, 0), n_stream - GROUPS)


def pack_kernel(n_stream, n_span, send_hbm, now_ref, prev_ref, packed_ref, sending_ref, picks, sem):
    i = lax.axis_index("stream")
    j = lax.axis_index("span")
    first = window_start(i, n_stream)
    far = lax.rem(i + n_stream // 2, n_stream)
    near_count = GROUPS * n_span
    copies = [
        pltpu.make_async_copy(send_hbm.at[pl.ds(first, GROUPS)], picks.at[pl.ds(0, GROUPS)], sem.at[0]),
        pltpu.make_async_copy(send_hbm.at[pl.ds(far, 1)], picks.at[pl.ds(GROUPS, 1)], sem.at[1]),
    ]
    for copy in copies:
        copy.start()

    def relayout(xb, carry):
        for dx in range(2):
            for tile in range(CY // 8):
                base = xb * (CY * ROW) + tile * 8 * ROW + dx * CHANS
                for c in range(VARS):
                    packed_ref[pl.ds(base + c, 8, ROW), :] = now_ref[c, 2 * xb + dx, tile * 8:tile * 8 + 8, :]
                    packed_ref[pl.ds(base + VARS + c, 8, ROW), :] = prev_ref[c, 2 * xb + dx, tile * 8:tile * 8 + 8, :]
        return carry

    lax.fori_loop(0, BX, relayout, 0)
    for copy in copies:
        copy.wait()
    half = lanes((ROW, 128)) < 64
    pair = lanes((BRICK, 128)) // 2
    chunk = 8

    def pack(p, carry):
        row = p // n_span
        start = jnp.where(p < near_count, lax.rem(p, n_span), j) * SLOT

        def some(head, total):
            def more(total):
                for k in range(head, head + chunk):
                    brick = jnp.maximum(picks[row, 0, start + k], 0)
                    base = pl.multiple_of((brick >> 6) * BRICK, 8)
                    shift = (2 * k - 2 * (brick & 63)) & 127
                    moved = pltpu.roll(packed_ref[pl.ds(base, BRICK), :], shift, 1)
                    total = jnp.where(pair == k, moved, total)
                return total
            return lax.cond(picks[row, 0, start + head] >= 0, more, lambda total: total, total)

        total = jnp.zeros((BRICK, 128), F32)
        for head in range(0, SLOT, chunk):
            total = some(head, total)
        sending_ref[p] = jnp.where(half, total[:ROW], pltpu.roll(total[ROW:], 64, 1))
        return carry

    lax.fori_loop(0, near_count + 1, pack, 0)


def exchange_kernel(n_stream, n_span, frac_ref, sending, fresh_ref, arrived, send_sem, recv_sem):
    i = lax.axis_index("stream")
    j = lax.axis_index("span")
    first = window_start(i, n_stream)
    far = lax.rem(i + n_stream // 2, n_stream)
    near_count = GROUPS * n_span
    far_slot = near_count

    def is_partner(g, jp):
        t = first + g
        return (t >= i - REACH) & (t <= i + REACH) & ((t != i) | (jp != j))

    barrier = pltpu.get_barrier_semaphore()
    for g in range(GROUPS):
        for jp in range(n_span):
            @pl.when(is_partner(g, jp))
            def _():
                pl.semaphore_signal(barrier, inc=1, device_id=(first + g, jp), device_id_type=MESH)
    pl.semaphore_signal(barrier, inc=1, device_id=(far, j), device_id_type=MESH)

    rows_near = jnp.minimum(i + REACH, n_stream - 1) - jnp.maximum(i - REACH, 0) + 1
    pl.semaphore_wait(barrier, rows_near * n_span)

    def far_copy():
        return pltpu.make_async_remote_copy(
            src_ref=sending.at[far_slot], dst_ref=arrived.at[far_slot],
            send_sem=send_sem.at[far_slot], recv_sem=recv_sem.at[far_slot],
            device_id=(far, j), device_id_type=MESH,
        )

    far_copy().start()

    def near_copy(p):
        g = p // n_span
        jp = lax.rem(p, n_span)
        t = first + g
        slot = (i - window_start(t, n_stream)) * n_span + j
        slot = jnp.minimum(jnp.maximum(slot, 0), near_count - 1)
        return pltpu.make_async_remote_copy(
            src_ref=sending.at[p], dst_ref=arrived.at[slot],
            send_sem=send_sem.at[p], recv_sem=recv_sem.at[slot],
            device_id=(t, jp), device_id_type=MESH,
        )

    def arrival(p):
        return pltpu.make_async_remote_copy(
            src_ref=sending.at[p], dst_ref=arrived.at[p],
            send_sem=send_sem.at[p], recv_sem=recv_sem.at[p],
            device_id=(first + p // n_span, lax.rem(p, n_span)), device_id_type=MESH,
        )

    def send(p, carry):
        g = p // n_span
        jp = lax.rem(p, n_span)
        t = first + g

        @pl.when(is_partner(g, jp))
        def _():
            near_copy(p).start()

        return carry

    lax.fori_loop(0, near_count, send, 0)
    own = (i - first) * n_span + j
    arrived[own] = sending[own]

    near_frac = [frac_ref[d, pl.ds(first, GROUPS), :] for d in range(3)]
    far_frac = [frac_ref[d, pl.ds(far, 1), :] for d in range(3)]
    table = jnp.concatenate([part for d in range(3) for part in (near_frac[d], far_frac[d])], 0)

    def spread(which):
        source = lax.broadcasted_iota(jnp.int32, (128, 128), 0)
        wanted = which * SLOT + lax.rem(lanes((128, 128)), 64) // 2
        chosen = jnp.where(source == wanted, 1.0, 0.0).astype(F32)
        return jnp.dot(table, chosen, precision=lax.Precision.HIGHEST, preferred_element_type=F32)

    spreads = [spread(jp) for jp in range(n_span)]
    far_spread = spread(j)
    even = lanes((CHANS, 128)) % 2 == 0
    low_half = lanes((CHANS, 128)) < 64

    def finish(p, fx, fy, fz):
        block = arrived[p]
        upper = block[CHANS:]
        lower = (1.0 - fx) * block[:CHANS] + fx * upper
        done = []
        for v in (lower, upper):
            v = jnp.where(low_half, (1.0 - fy) * v + fy * pltpu.roll(v, 64, 1), v)
            v = jnp.where(even, (1.0 - fz) * v + fz * pltpu.roll(v, 127, 1), v)
            done.append(v)
        both = jnp.concatenate(done, 0)
        fresh_ref[p, 0:ROW, :] = both
        fresh_ref[p, ROW:BRICK, :] = pltpu.roll(both, 64, 1)

    for p in range(near_count):
        g, jp = p // n_span, p % n_span

        @pl.when(is_partner(g, jp))
        def _():
            arrival(p).wait()

        finish(p, *(spreads[jp][6 * d + g:6 * d + g + 1] for d in range(3)))
    far_copy().wait()
    finish(far_slot, *(far_spread[6 * d + GROUPS:6 * d + GROUPS + 1] for d in range(3)))


def place_kernel(n_stream, n_span, recv_hbm, packed_hbm, fresh_ref, now_ref, prev_ref, targets, work, sem):
    i = lax.axis_index("stream")
    j = lax.axis_index("span")
    first = window_start(i, n_stream)
    far = lax.rem(i + n_stream // 2, n_stream)
    near_count = GROUPS * n_span
    copies = [
        pltpu.make_async_copy(recv_hbm.at[pl.ds(first, GROUPS)], targets.at[pl.ds(0, GROUPS)], sem.at[0]),
        pltpu.make_async_copy(recv_hbm.at[pl.ds(far, 1)], targets.at[pl.ds(GROUPS, 1)], sem.at[1]),
        pltpu.make_async_copy(packed_hbm, work, sem.at[2]),
    ]
    for copy in copies:
        copy.start()
    for copy in copies:
        copy.wait()
    pair = lanes((BRICK, 128)) // 2
    chunk = 8

    def put(p, carry):
        row = p // n_span
        start = jnp.where(p < near_count, lax.rem(p, n_span), j) * SLOT
        for head in range(0, SLOT, chunk):
            @pl.when(targets[row, 0, start + head] >= 0)
            def _():
                block = fresh_ref[p]
                for k in range(head, head + chunk):
                    target = targets[row, 0, start + k]
                    brick = jnp.maximum(target, 0)
                    column = lax.rem(brick, 64)
                    base = pl.multiple_of((brick // 64) * BRICK, 8)
                    shift = lax.rem(2 * column - 2 * k + 128, 128)
                    moved = pltpu.roll(block, shift, 1)
                    mark = jnp.where(target >= 0, column, -1)
                    pltpu.store(work.at[pl.ds(base, BRICK), :], moved, mask=pair == mark)
        return carry

    lax.fori_loop(0, near_count + 1, put, 0)

    def relayout(xb, carry):
        for dx in range(2):
            for tile in range(CY // 8):
                base = xb * (CY * ROW) + tile * 8 * ROW + dx * CHANS
                for c in range(VARS):
                    now_ref[c, 2 * xb + dx, tile * 8:tile * 8 + 8, :] = work[pl.ds(base + c, 8, ROW), :]
                    prev_ref[c, 2 * xb + dx, tile * 8:tile * 8 + 8, :] = work[pl.ds(base + VARS + c, 8, ROW), :]
        return carry

    lax.fori_loop(0, BX, relayout, 0)


def band(entries):
    source = lax.rem(lax.broadcasted_iota(jnp.int32, (2 * CZ, CZ), 0), CZ)
    away = source - lanes((2 * CZ, CZ))
    total = jnp.zeros((2 * CZ, CZ), F32)
    for offset, weight in entries:
        total = jnp.where(away == offset, weight, total)
    return total.astype(jnp.bfloat16)


def along_z(values, matrix):
    high = values.astype(jnp.bfloat16)
    low = (values - high.astype(F32)).astype(jnp.bfloat16)
    both = jnp.concatenate([high, low], 1)
    return jnp.dot(both, matrix, preferred_element_type=F32)


def advance_kernel(
    n_stream, n_span, jac, q_hbm, old_ref, out_ref,
    wide, pre, y_near_out, y_near_in, y_far_out, y_far_in,
    load_sem, near_send, near_recv, far_send, far_recv,
):
    i = lax.axis_index("stream")
    j = lax.axis_index("span")
    has = (i > 0, i < n_stream - 1, j > 0, j < n_span - 1)
    ids = ((i - 1, j), (i + 1, j), (i, j - 1), (i, j + 1))

    barrier = pltpu.get_barrier_semaphore()
    for side in range(4):
        @pl.when(has[side])
        def _():
            pl.semaphore_signal(barrier, inc=1, device_id=ids[side], device_id_type=MESH)

    load = pltpu.make_async_copy(q_hbm, wide.at[:, NEAR:NEAR + CX, PAD:PAD + CY, :], load_sem)
    load.start()

    for ref, width in ((wide, NEAR), (pre, FAR)):
        planes = CX + 2 * width

        @pl.when(~has[0])
        def _():
            ref[:, 0:width, :, :] = jnp.zeros((VARS, width, WY, CZ), F32)

        @pl.when(~has[1])
        def _():
            ref[:, width + CX:planes, :, :] = jnp.zeros((VARS, width, WY, CZ), F32)

        @pl.when(~has[2])
        def _():
            ref[:, width:width + CX, 0:PAD, :] = jnp.zeros((VARS, CX, PAD, CZ), F32)

        @pl.when(~has[3])
        def _():
            ref[:, width:width + CX, PAD + CY:WY, :] = jnp.zeros((VARS, CX, PAD, CZ), F32)

    load.wait()

    def column(ref, width, c, x, y):
        planes = CX + 2 * width
        flat = ref.reshape(VARS * planes * WY, CZ)
        return flat, pl.ds((c * planes + width + x) * WY + PAD + y, 8, WY)

    def pack(ref, out, width, side):
        for c in range(VARS):
            for m in range(width):
                for x in range(0, CX, 8):
                    flat, rows = column(ref, width, c, x, m if side == 2 else CY - width + m)
                    out[side - 2, c, m, x:x + 8, :] = flat[rows, :]

    def unpack(ref, held, width, side):
        for c in range(VARS):
            for m in range(width):
                for x in range(0, CX, 8):
                    flat, rows = column(ref, width, c, x, m - width if side == 2 else CY + m)
                    flat[rows, :] = held[side - 2, c, m, x:x + 8, :]

    def copy(ref, out, held, width, side, send, recv):
        if side == 0:
            src = ref.at[:, width:2 * width, PAD:PAD + CY, :]
            dst = ref.at[:, width + CX:2 * width + CX, PAD:PAD + CY, :]
        elif side == 1:
            src = ref.at[:, CX:width + CX, PAD:PAD + CY, :]
            dst = ref.at[:, 0:width, PAD:PAD + CY, :]
        else:
            src = out.at[side - 2]
            dst = held.at[3 - side]
        return pltpu.make_async_remote_copy(
            src_ref=src, dst_ref=dst, send_sem=send.at[side], recv_sem=recv.at[side ^ 1],
            device_id=ids[side], device_id_type=MESH,
        )

    def near(side):
        return copy(wide, y_near_out, y_near_in, NEAR, side, near_send, near_recv)

    def far(side):
        return copy(pre, y_far_out, y_far_in, FAR, side, far_send, far_recv)

    def start(make, side):
        @pl.when(has[side])
        def _():
            make(side).start()

    def finish_recv(make, side):
        @pl.when(has[side])
        def _():
            make(side ^ 1).wait_recv()

    def finish_send(make, side):
        @pl.when(has[side])
        def _():
            make(side).wait_send()

    expected = sum(jnp.where(flag, 1, 0) for flag in has)
    pl.semaphore_wait(barrier, expected)
    start(near, 0)
    start(near, 1)
    for side in (2, 3):
        pack(wide, y_near_out, NEAR, side)
        start(near, side)

    slope = band(((1, 8.0), (-1, -8.0), (2, -1.0), (-2, 1.0)))

    def base_plane(x, carry):
        q = wide[:, NEAR + x, PAD:PAD + CY, :]
        dz = along_z(q.reshape(VARS * CY, CZ), slope).reshape(VARS, CY, CZ) * (-1.0 / 36.0)
        for v in range(VARS):
            total = (4.0 * q[v] - old_ref[v, x]) * (1.0 / 3.0)
            for w in range(VARS):
                total = total + jac[50 + 5 * v + w] * dz[w]
            pre[v, FAR + x, PAD:PAD + CY, :] = total
        return carry

    lax.fori_loop(0, CX, base_plane, 0)

    for side in range(4):
        finish_recv(near, side)

    for side in (2, 3):
        @pl.when(has[side])
        def _():
            unpack(wide, y_near_in, NEAR, side)

    def rate_plane(x, carry):
        for tile in range(CY // 8):
            y = PAD + 8 * tile
            dx, dy = [], []
            for w in range(VARS):
                def at(sx, sy):
                    return wide[w, NEAR + x + sx, y + sy:y + sy + 8, :]

                dx.append((at(1, 0) - at(-1, 0)) * (-8.0 / 36.0) + (at(2, 0) - at(-2, 0)) * (1.0 / 36.0))
                dy.append((at(0, 1) - at(0, -1)) * (-8.0 / 36.0) + (at(0, 2) - at(0, -2)) * (1.0 / 36.0))
            for v in range(VARS):
                total = pre[v, FAR + x, y:y + 8, :]
                for w in range(VARS):
                    total = total + jac[5 * v + w] * dx[w]
                    total = total + jac[25 + 5 * v + w] * dy[w]
                pre[v, FAR + x, y:y + 8, :] = total
        return carry

    lax.fori_loop(0, FAR, rate_plane, 0)
    start(far, 0)
    lax.fori_loop(CX - FAR, CX, rate_plane, 0)
    start(far, 1)
    lax.fori_loop(FAR, CX - FAR, rate_plane, 0)
    for side in (2, 3):
        pack(pre, y_far_out, FAR, side)
        start(far, side)

    tenth = band(tuple((o, TAPS[abs(o)]) for o in range(-5, 6)))

    def filter_y(x, c, tile):
        y = PAD + 8 * tile

        def at(sy):
            return pre[c, FAR + x, y + sy:y + sy + 8, :]

        total = (TAPS[0] * SCALE) * at(0)
        for m in range(1, 6):
            total = total + (TAPS[m] * SCALE) * (at(m) + at(-m))
        return total

    def first_plane(x, carry):
        p = pre[:, FAR + x, PAD:PAD + CY, :]
        fz = along_z(p.reshape(VARS * CY, CZ), tenth).reshape(VARS, CY, CZ)
        total = p + SCALE * fz
        for c in range(VARS):
            for tile in range(CY // 8):
                part = total[c, 8 * tile:8 * tile + 8]
                if tile in (1, 2):
                    part = part + filter_y(x, c, tile)
                out_ref[c, x, 8 * tile:8 * tile + 8, :] = part
        return carry

    lax.fori_loop(0, CX, first_plane, 0)

    def filter_x(x, carry):
        for c in range(VARS):
            for tile in range(CY // 8):
                y = PAD + 8 * tile

                def at(sx):
                    return pre[c, FAR + x + sx, y:y + 8, :]

                total = out_ref[c, x, 8 * tile:8 * tile + 8, :] + (TAPS[0] * SCALE) * at(0)
                for m in range(1, 6):
                    total = total + (TAPS[m] * SCALE) * (at(m) + at(-m))
                out_ref[c, x, 8 * tile:8 * tile + 8, :] = total
        return carry

    lax.fori_loop(FAR, CX - FAR, filter_x, 0)
    for side in (0, 1):
        finish_recv(far, side)
    lax.fori_loop(0, FAR, filter_x, 0)
    lax.fori_loop(CX - FAR, CX, filter_x, 0)
    for side in (2, 3):
        finish_recv(far, side)

        @pl.when(has[side])
        def _():
            unpack(pre, y_far_in, FAR, side)

    def edge_plane(x, carry):
        for c in range(VARS):
            for tile in (0, CY // 8 - 1):
                rows = pl.ds(8 * tile, 8)
                out_ref[c, x, rows, :] = out_ref[c, x, rows, :] + filter_y(x, c, tile)
        return carry

    lax.fori_loop(0, CX, edge_plane, 0)
    for side in range(4):
        finish_send(near, side)
        finish_send(far, side)


def per_device(n_stream, n_span, q_now, q_prev, jacobians, fractions, send_blocks, recv_blocks):
    vmem = pl.BlockSpec(memory_space=pltpu.VMEM)
    anywhere = pl.BlockSpec(memory_space=pl.ANY)
    slots = GROUPS * n_span + 1
    width = n_span * SLOT
    sending = send_blocks.reshape(n_stream, 1, width)
    receiving = recv_blocks.reshape(n_stream, 1, width)
    offsets = fractions.reshape(3, n_stream, width)
    limit = 48 * 1024 * 1024
    packed, leaving = pl.pallas_call(
        functools.partial(pack_kernel, n_stream, n_span),
        name="pack",
        out_shape=(
            jax.ShapeDtypeStruct((ROWS, CZ), F32),
            jax.ShapeDtypeStruct((slots, ROW, 128), F32),
        ),
        in_specs=[anywhere, vmem, vmem],
        out_specs=(vmem, vmem),
        scratch_shapes=[
            pltpu.SMEM((GROUPS + 1, 1, width), jnp.int32),
            pltpu.SemaphoreType.DMA((2,)),
        ],
        compiler_params=pltpu.CompilerParams(vmem_limit_bytes=limit),
    )(sending, q_now, q_prev)
    fresh = pl.pallas_call(
        functools.partial(exchange_kernel, n_stream, n_span),
        name="exchange",
        out_shape=jax.ShapeDtypeStruct((slots, BRICK, 128), F32),
        in_specs=[vmem, vmem],
        out_specs=vmem,
        scratch_shapes=[
            pltpu.VMEM((slots, ROW, 128), F32),
            pltpu.SemaphoreType.DMA((slots,)),
            pltpu.SemaphoreType.DMA((slots,)),
        ],
        compiler_params=pltpu.CompilerParams(
            collective_id=0, has_side_effects=True, vmem_limit_bytes=limit
        ),
    )(offsets, leaving)
    shape = jax.ShapeDtypeStruct(q_now.shape, F32)
    now, older = pl.pallas_call(
        functools.partial(place_kernel, n_stream, n_span),
        name="place",
        out_shape=(shape, shape),
        in_specs=[anywhere, anywhere, vmem],
        out_specs=(vmem, vmem),
        scratch_shapes=[
            pltpu.SMEM((GROUPS + 1, 1, width), jnp.int32),
            pltpu.VMEM((ROWS, CZ), F32),
            pltpu.SemaphoreType.DMA((3,)),
        ],
        compiler_params=pltpu.CompilerParams(vmem_limit_bytes=limit),
    )(receiving, packed, fresh)
    return pl.pallas_call(
        functools.partial(advance_kernel, n_stream, n_span),
        name="advance",
        out_shape=shape,
        in_specs=[pl.BlockSpec(memory_space=pltpu.SMEM), anywhere, vmem],
        out_specs=vmem,
        scratch_shapes=[
            pltpu.VMEM((VARS, CX + 2 * NEAR, WY, CZ), F32),
            pltpu.VMEM((VARS, CX + 2 * FAR, WY, CZ), F32),
            pltpu.VMEM((2, VARS, NEAR, CX, CZ), F32),
            pltpu.VMEM((2, VARS, NEAR, CX, CZ), F32),
            pltpu.VMEM((2, VARS, FAR, CX, CZ), F32),
            pltpu.VMEM((2, VARS, FAR, CX, CZ), F32),
            pltpu.SemaphoreType.DMA,
            pltpu.SemaphoreType.DMA((4,)),
            pltpu.SemaphoreType.DMA((4,)),
            pltpu.SemaphoreType.DMA((4,)),
            pltpu.SemaphoreType.DMA((4,)),
        ],
        compiler_params=pltpu.CompilerParams(
            collective_id=1, has_side_effects=True, vmem_limit_bytes=limit
        ),
    )(jacobians.reshape(-1), now, older)


def solution(mesh):
    in_specs = (
        P(None, "stream", "span", None),
        P(None, "stream", "span", None),
        P(),
        P(None, ("stream", "span"), None),
        P(("stream", "span"), None),
        P(("stream", "span"), None),
    )
    out_specs = P(None, "stream", "span", None)
    body = functools.partial(per_device, mesh.shape["stream"], mesh.shape["span"])
    return jax.shard_map(
        body, mesh=mesh, in_specs=in_specs, out_specs=out_specs, check_vma=False
    )
```

```python
import functools

import jax
import jax.numpy as jnp
from jax import lax
from jax.experimental import pallas as pl
from jax.experimental.pallas import tpu as pltpu
from jax.sharding import PartitionSpec as P

MESH = pl.DeviceIdType.MESH
F32 = jnp.float32
VARS = 5
CHANS = 10
SLOT = 32
REACH = 2
GROUPS = 2 * REACH + 1
CX, CY, CZ = 16, 32, 128
BX, BY = CX // 2, CY // 2
ROW = 2 * CHANS
BRICK = 2 * ROW
ROWS = BX * CY * ROW
PAD = 8
WY = CY + 2 * PAD
NEAR, FAR = 2, 5
SCALE = 0.6 / 1024.0
TAPS = (-252.0, 210.0, -120.0, 45.0, -10.0, 1.0)


def lanes(shape):
    return lax.broadcasted_iota(jnp.int32, shape, len(shape) - 1)


def window_start(i, n_stream):
    return jnp.minimum(jnp.maximum(i - REACH, 0), n_stream - GROUPS)


def exchange_kernel(
    n_stream, n_span, send_hbm, frac_ref, now_ref, prev_ref, packed_ref, fresh_ref,
    picks, sending, arrived, pick_sem, send_sem, recv_sem,
):
    i = lax.axis_index("stream")
    j = lax.axis_index("span")
    first = window_start(i, n_stream)
    far = lax.rem(i + n_stream // 2, n_stream)
    near_count = GROUPS * n_span
    far_slot = near_count

    def is_partner(g, jp):
        t = first + g
        return (t >= i - REACH) & (t <= i + REACH) & ((t != i) | (jp != j))

    barrier = pltpu.get_barrier_semaphore()
    for g in range(GROUPS):
        for jp in range(n_span):
            @pl.when(is_partner(g, jp))
            def _():
                pl.semaphore_signal(barrier, inc=1, device_id=(first + g, jp), device_id_type=MESH)
    pl.semaphore_signal(barrier, inc=1, device_id=(far, j), device_id_type=MESH)

    near_picks = pltpu.make_async_copy(
        send_hbm.at[pl.ds(first, GROUPS)], picks.at[pl.ds(0, GROUPS)], pick_sem.at[0]
    )
    far_picks = pltpu.make_async_copy(
        send_hbm.at[pl.ds(far, 1)], picks.at[pl.ds(GROUPS, 1)], pick_sem.at[1]
    )
    near_picks.start()
    far_picks.start()

    def relayout(xb, carry):
        for dx in range(2):
            for tile in range(CY // 8):
                base = xb * (CY * ROW) + tile * 8 * ROW + dx * CHANS
                for c in range(VARS):
                    packed_ref[pl.ds(base + c, 8, ROW), :] = now_ref[c, 2 * xb + dx, tile * 8:tile * 8 + 8, :]
                    packed_ref[pl.ds(base + VARS + c, 8, ROW), :] = prev_ref[c, 2 * xb + dx, tile * 8:tile * 8 + 8, :]
        return carry

    lax.fori_loop(0, BX, relayout, 0)
    near_picks.wait()
    far_picks.wait()

    rows_near = jnp.minimum(i + REACH, n_stream - 1) - jnp.maximum(i - REACH, 0) + 1
    pl.semaphore_wait(barrier, rows_near * n_span)

    half = lanes((ROW, 128)) < 64
    pair = lanes((BRICK, 128)) // 2

    def pack(row, start):
        total = jnp.zeros((BRICK, 128), F32)
        for k in range(SLOT):
            brick = jnp.maximum(picks[row, 0, start + k], 0)
            base = (brick >> 6) * BRICK
            moved = pltpu.roll(packed_ref[pl.ds(base, BRICK), :], (2 * k - 2 * (brick & 63)) & 127, 1)
            total = jnp.where(pair == k, moved, total)
        return jnp.where(half, total[:ROW], pltpu.roll(total[ROW:], 64, 1))

    my_far_slot = far_slot
    sending[far_slot] = pack(GROUPS, j * SLOT)

    def far_copy():
        return pltpu.make_async_remote_copy(
            src_ref=sending.at[far_slot], dst_ref=arrived.at[my_far_slot],
            send_sem=send_sem.at[far_slot], recv_sem=recv_sem.at[far_slot],
            device_id=(far, j), device_id_type=MESH,
        )

    far_copy().start()

    def near_copy(p):
        g = p // n_span
        jp = lax.rem(p, n_span)
        t = first + g
        slot = (i - window_start(t, n_stream)) * n_span + j
        slot = jnp.minimum(jnp.maximum(slot, 0), near_count - 1)
        return pltpu.make_async_remote_copy(
            src_ref=sending.at[p], dst_ref=arrived.at[slot],
            send_sem=send_sem.at[p], recv_sem=recv_sem.at[slot],
            device_id=(t, jp), device_id_type=MESH,
        )

    def arrival(p):
        return pltpu.make_async_remote_copy(
            src_ref=sending.at[p], dst_ref=arrived.at[p],
            send_sem=send_sem.at[p], recv_sem=recv_sem.at[p],
            device_id=(first + p // n_span, lax.rem(p, n_span)), device_id_type=MESH,
        )

    def send(p, carry):
        g = p // n_span
        jp = lax.rem(p, n_span)
        t = first + g

        @pl.when((t >= i - REACH) & (t <= i + REACH))
        def _():
            sending[p] = pack(g, jp * SLOT)

        @pl.when(is_partner(g, jp))
        def _():
            near_copy(p).start()

        return carry

    lax.fori_loop(0, near_count, send, 0)
    own = (i - first) * n_span + j
    arrived[own] = sending[own]

    near_frac = [frac_ref[d, pl.ds(first, GROUPS), :] for d in range(3)]
    far_frac = [frac_ref[d, pl.ds(far, 1), :] for d in range(3)]
    table = jnp.concatenate([part for d in range(3) for part in (near_frac[d], far_frac[d])], 0)

    def spread(which):
        source = lax.broadcasted_iota(jnp.int32, (128, 128), 0)
        wanted = which * SLOT + lax.rem(lanes((128, 128)), 64) // 2
        chosen = jnp.where(source == wanted, 1.0, 0.0).astype(F32)
        return jnp.dot(table, chosen, precision=lax.Precision.HIGHEST, preferred_element_type=F32)

    spreads = [spread(jp) for jp in range(n_span)]
    far_spread = spread(j)
    even = lanes((CHANS, 128)) % 2 == 0
    low_half = lanes((CHANS, 128)) < 64

    def finish(p, fx, fy, fz):
        block = arrived[p]
        upper = block[CHANS:]
        lower = (1.0 - fx) * block[:CHANS] + fx * upper
        done = []
        for v in (lower, upper):
            v = jnp.where(low_half, (1.0 - fy) * v + fy * pltpu.roll(v, 64, 1), v)
            v = jnp.where(even, (1.0 - fz) * v + fz * pltpu.roll(v, 127, 1), v)
            done.append(v)
        both = jnp.concatenate(done, 0)
        fresh_ref[p, 0:ROW, :] = both
        fresh_ref[p, ROW:BRICK, :] = pltpu.roll(both, 64, 1)

    for p in range(near_count):
        g, jp = p // n_span, p % n_span

        @pl.when(is_partner(g, jp))
        def _():
            arrival(p).wait()

        finish(p, *(spreads[jp][6 * d + g:6 * d + g + 1] for d in range(3)))
    far_copy().wait()
    finish(far_slot, *(far_spread[6 * d + GROUPS:6 * d + GROUPS + 1] for d in range(3)))


def place_kernel(n_stream, n_span, recv_hbm, packed_hbm, fresh_ref, now_ref, prev_ref, targets, work, sem):
    i = lax.axis_index("stream")
    j = lax.axis_index("span")
    first = window_start(i, n_stream)
    far = lax.rem(i + n_stream // 2, n_stream)
    near_count = GROUPS * n_span
    copies = [
        pltpu.make_async_copy(recv_hbm.at[pl.ds(first, GROUPS)], targets.at[pl.ds(0, GROUPS)], sem.at[0]),
        pltpu.make_async_copy(recv_hbm.at[pl.ds(far, 1)], targets.at[pl.ds(GROUPS, 1)], sem.at[1]),
        pltpu.make_async_copy(packed_hbm, work, sem.at[2]),
    ]
    for copy in copies:
        copy.start()
    for copy in copies:
        copy.wait()
    pair = lanes((BRICK, 128)) // 2
    chunk = 8

    def put(p, carry):
        row = p // n_span
        start = jnp.where(p < near_count, lax.rem(p, n_span), j) * SLOT
        for head in range(0, SLOT, chunk):
            @pl.when(targets[row, 0, start + head] >= 0)
            def _():
                block = fresh_ref[p]
                for k in range(head, head + chunk):
                    target = targets[row, 0, start + k]
                    brick = jnp.maximum(target, 0)
                    column = lax.rem(brick, 64)
                    base = pl.multiple_of((brick // 64) * BRICK, 8)
                    shift = lax.rem(2 * column - 2 * k + 128, 128)
                    moved = pltpu.roll(block, shift, 1)
                    mark = jnp.where(target >= 0, column, -1)
                    pltpu.store(work.at[pl.ds(base, BRICK), :], moved, mask=pair == mark)
        return carry

    lax.fori_loop(0, near_count + 1, put, 0)

    def relayout(xb, carry):
        for dx in range(2):
            for tile in range(CY // 8):
                base = xb * (CY * ROW) + tile * 8 * ROW + dx * CHANS
                for c in range(VARS):
                    now_ref[c, 2 * xb + dx, tile * 8:tile * 8 + 8, :] = work[pl.ds(base + c, 8, ROW), :]
                    prev_ref[c, 2 * xb + dx, tile * 8:tile * 8 + 8, :] = work[pl.ds(base + VARS + c, 8, ROW), :]
        return carry

    lax.fori_loop(0, BX, relayout, 0)


def band(entries):
    source = lax.rem(lax.broadcasted_iota(jnp.int32, (2 * CZ, CZ), 0), CZ)
    away = source - lanes((2 * CZ, CZ))
    total = jnp.zeros((2 * CZ, CZ), F32)
    for offset, weight in entries:
        total = jnp.where(away == offset, weight, total)
    return total.astype(jnp.bfloat16)


def along_z(values, matrix):
    high = values.astype(jnp.bfloat16)
    low = (values - high.astype(F32)).astype(jnp.bfloat16)
    both = jnp.concatenate([high, low], 1)
    return jnp.dot(both, matrix, preferred_element_type=F32)


def advance_kernel(
    n_stream, n_span, jac, q_hbm, old_ref, out_ref,
    wide, pre, y_near_out, y_near_in, y_far_out, y_far_in,
    load_sem, near_send, near_recv, far_send, far_recv,
):
    i = lax.axis_index("stream")
    j = lax.axis_index("span")
    has = (i > 0, i < n_stream - 1, j > 0, j < n_span - 1)
    ids = ((i - 1, j), (i + 1, j), (i, j - 1), (i, j + 1))

    barrier = pltpu.get_barrier_semaphore()
    for side in range(4):
        @pl.when(has[side])
        def _():
            pl.semaphore_signal(barrier, inc=1, device_id=ids[side], device_id_type=MESH)

    load = pltpu.make_async_copy(q_hbm, wide.at[:, NEAR:NEAR + CX, PAD:PAD + CY, :], load_sem)
    load.start()

    for ref, width in ((wide, NEAR), (pre, FAR)):
        planes = CX + 2 * width

        @pl.when(~has[0])
        def _():
            ref[:, 0:width, :, :] = jnp.zeros((VARS, width, WY, CZ), F32)

        @pl.when(~has[1])
        def _():
            ref[:, width + CX:planes, :, :] = jnp.zeros((VARS, width, WY, CZ), F32)

        @pl.when(~has[2])
        def _():
            ref[:, width:width + CX, 0:PAD, :] = jnp.zeros((VARS, CX, PAD, CZ), F32)

        @pl.when(~has[3])
        def _():
            ref[:, width:width + CX, PAD + CY:WY, :] = jnp.zeros((VARS, CX, PAD, CZ), F32)

    load.wait()

    def column(ref, width, c, x, y):
        planes = CX + 2 * width
        flat = ref.reshape(VARS * planes * WY, CZ)
        return flat, pl.ds((c * planes + width + x) * WY + PAD + y, 8, WY)

    def pack(ref, out, width, side):
        for c in range(VARS):
            for m in range(width):
                for x in range(0, CX, 8):
                    flat, rows = column(ref, width, c, x, m if side == 2 else CY - width + m)
                    out[side - 2, c, m, x:x + 8, :] = flat[rows, :]

    def unpack(ref, held, width, side):
        for c in range(VARS):
            for m in range(width):
                for x in range(0, CX, 8):
                    flat, rows = column(ref, width, c, x, m - width if side == 2 else CY + m)
                    flat[rows, :] = held[side - 2, c, m, x:x + 8, :]

    def copy(ref, out, held, width, side, send, recv):
        if side == 0:
            src = ref.at[:, width:2 * width, PAD:PAD + CY, :]
            dst = ref.at[:, width + CX:2 * width + CX, PAD:PAD + CY, :]
        elif side == 1:
            src = ref.at[:, CX:width + CX, PAD:PAD + CY, :]
            dst = ref.at[:, 0:width, PAD:PAD + CY, :]
        else:
            src = out.at[side - 2]
            dst = held.at[3 - side]
        return pltpu.make_async_remote_copy(
            src_ref=src, dst_ref=dst, send_sem=send.at[side], recv_sem=recv.at[side ^ 1],
            device_id=ids[side], device_id_type=MESH,
        )

    def near(side):
        return copy(wide, y_near_out, y_near_in, NEAR, side, near_send, near_recv)

    def far(side):
        return copy(pre, y_far_out, y_far_in, FAR, side, far_send, far_recv)

    def start(make, side):
        @pl.when(has[side])
        def _():
            make(side).start()

    def finish_recv(make, side):
        @pl.when(has[side])
        def _():
            make(side ^ 1).wait_recv()

    def finish_send(make, side):
        @pl.when(has[side])
        def _():
            make(side).wait_send()

    expected = sum(jnp.where(flag, 1, 0) for flag in has)
    pl.semaphore_wait(barrier, expected)
    start(near, 0)
    start(near, 1)
    for side in (2, 3):
        pack(wide, y_near_out, NEAR, side)
        start(near, side)

    slope = band(((1, 8.0), (-1, -8.0), (2, -1.0), (-2, 1.0)))

    def base_plane(x, carry):
        q = wide[:, NEAR + x, PAD:PAD + CY, :]
        dz = along_z(q.reshape(VARS * CY, CZ), slope).reshape(VARS, CY, CZ) * (-1.0 / 36.0)
        for v in range(VARS):
            total = (4.0 * q[v] - old_ref[v, x]) * (1.0 / 3.0)
            for w in range(VARS):
                total = total + jac[50 + 5 * v + w] * dz[w]
            pre[v, FAR + x, PAD:PAD + CY, :] = total
        return carry

    lax.fori_loop(0, CX, base_plane, 0)

    for side in range(4):
        finish_recv(near, side)

    for side in (2, 3):
        @pl.when(has[side])
        def _():
            unpack(wide, y_near_in, NEAR, side)

    def rate_plane(x, carry):
        for tile in range(CY // 8):
            y = PAD + 8 * tile
            dx, dy = [], []
            for w in range(VARS):
                def at(sx, sy):
                    return wide[w, NEAR + x + sx, y + sy:y + sy + 8, :]

                dx.append((at(1, 0) - at(-1, 0)) * (-8.0 / 36.0) + (at(2, 0) - at(-2, 0)) * (1.0 / 36.0))
                dy.append((at(0, 1) - at(0, -1)) * (-8.0 / 36.0) + (at(0, 2) - at(0, -2)) * (1.0 / 36.0))
            for v in range(VARS):
                total = pre[v, FAR + x, y:y + 8, :]
                for w in range(VARS):
                    total = total + jac[5 * v + w] * dx[w]
                    total = total + jac[25 + 5 * v + w] * dy[w]
                pre[v, FAR + x, y:y + 8, :] = total
        return carry

    lax.fori_loop(0, FAR, rate_plane, 0)
    start(far, 0)
    lax.fori_loop(CX - FAR, CX, rate_plane, 0)
    start(far, 1)
    lax.fori_loop(FAR, CX - FAR, rate_plane, 0)
    for side in (2, 3):
        pack(pre, y_far_out, FAR, side)
        start(far, side)

    tenth = band(tuple((o, TAPS[abs(o)]) for o in range(-5, 6)))

    def filter_y(x, c, tile):
        y = PAD + 8 * tile

        def at(sy):
            return pre[c, FAR + x, y + sy:y + sy + 8, :]

        total = (TAPS[0] * SCALE) * at(0)
        for m in range(1, 6):
            total = total + (TAPS[m] * SCALE) * (at(m) + at(-m))
        return total

    def first_plane(x, carry):
        p = pre[:, FAR + x, PAD:PAD + CY, :]
        fz = along_z(p.reshape(VARS * CY, CZ), tenth).reshape(VARS, CY, CZ)
        total = p + SCALE * fz
        for c in range(VARS):
            for tile in range(CY // 8):
                part = total[c, 8 * tile:8 * tile + 8]
                if tile in (1, 2):
                    part = part + filter_y(x, c, tile)
                out_ref[c, x, 8 * tile:8 * tile + 8, :] = part
        return carry

    lax.fori_loop(0, CX, first_plane, 0)

    def filter_x(x, carry):
        for c in range(VARS):
            for tile in range(CY // 8):
                y = PAD + 8 * tile

                def at(sx):
                    return pre[c, FAR + x + sx, y:y + 8, :]

                total = out_ref[c, x, 8 * tile:8 * tile + 8, :] + (TAPS[0] * SCALE) * at(0)
                for m in range(1, 6):
                    total = total + (TAPS[m] * SCALE) * (at(m) + at(-m))
                out_ref[c, x, 8 * tile:8 * tile + 8, :] = total
        return carry

    lax.fori_loop(FAR, CX - FAR, filter_x, 0)
    for side in (0, 1):
        finish_recv(far, side)
    lax.fori_loop(0, FAR, filter_x, 0)
    lax.fori_loop(CX - FAR, CX, filter_x, 0)
    for side in (2, 3):
        finish_recv(far, side)

        @pl.when(has[side])
        def _():
            unpack(pre, y_far_in, FAR, side)

    def edge_plane(x, carry):
        for c in range(VARS):
            for tile in (0, CY // 8 - 1):
                rows = pl.ds(8 * tile, 8)
                out_ref[c, x, rows, :] = out_ref[c, x, rows, :] + filter_y(x, c, tile)
        return carry

    lax.fori_loop(0, CX, edge_plane, 0)
    for side in range(4):
        finish_send(near, side)
        finish_send(far, side)


def per_device(n_stream, n_span, q_now, q_prev, jacobians, fractions, send_blocks, recv_blocks):
    vmem = pl.BlockSpec(memory_space=pltpu.VMEM)
    anywhere = pl.BlockSpec(memory_space=pl.ANY)
    slots = GROUPS * n_span + 1
    width = n_span * SLOT
    sending = send_blocks.reshape(n_stream, 1, width)
    receiving = recv_blocks.reshape(n_stream, 1, width)
    offsets = fractions.reshape(3, n_stream, width)
    limit = 48 * 1024 * 1024
    packed, fresh = pl.pallas_call(
        functools.partial(exchange_kernel, n_stream, n_span),
        name="exchange",
        out_shape=(
            jax.ShapeDtypeStruct((ROWS, CZ), F32),
            jax.ShapeDtypeStruct((slots, BRICK, 128), F32),
        ),
        in_specs=[anywhere, vmem, vmem, vmem],
        out_specs=(vmem, vmem),
        scratch_shapes=[
            pltpu.SMEM((GROUPS + 1, 1, width), jnp.int32),
            pltpu.VMEM((slots, ROW, 128), F32),
            pltpu.VMEM((slots, ROW, 128), F32),
            pltpu.SemaphoreType.DMA((2,)),
            pltpu.SemaphoreType.DMA((slots,)),
            pltpu.SemaphoreType.DMA((slots,)),
        ],
        compiler_params=pltpu.CompilerParams(
            collective_id=0, has_side_effects=True, vmem_limit_bytes=limit
        ),
    )(sending, offsets, q_now, q_prev)
    shape = jax.ShapeDtypeStruct(q_now.shape, F32)
    now, older = pl.pallas_call(
        functools.partial(place_kernel, n_stream, n_span),
        name="place",
        out_shape=(shape, shape),
        in_specs=[anywhere, anywhere, vmem],
        out_specs=(vmem, vmem),
        scratch_shapes=[
            pltpu.SMEM((GROUPS + 1, 1, width), jnp.int32),
            pltpu.VMEM((ROWS, CZ), F32),
            pltpu.SemaphoreType.DMA((3,)),
        ],
        compiler_params=pltpu.CompilerParams(vmem_limit_bytes=limit),
    )(receiving, packed, fresh)
    return pl.pallas_call(
        functools.partial(advance_kernel, n_stream, n_span),
        name="advance",
        out_shape=shape,
        in_specs=[pl.BlockSpec(memory_space=pltpu.SMEM), anywhere, vmem],
        out_specs=vmem,
        scratch_shapes=[
            pltpu.VMEM((VARS, CX + 2 * NEAR, WY, CZ), F32),
            pltpu.VMEM((VARS, CX + 2 * FAR, WY, CZ), F32),
            pltpu.VMEM((2, VARS, NEAR, CX, CZ), F32),
            pltpu.VMEM((2, VARS, NEAR, CX, CZ), F32),
            pltpu.VMEM((2, VARS, FAR, CX, CZ), F32),
            pltpu.VMEM((2, VARS, FAR, CX, CZ), F32),
            pltpu.SemaphoreType.DMA,
            pltpu.SemaphoreType.DMA((4,)),
            pltpu.SemaphoreType.DMA((4,)),
            pltpu.SemaphoreType.DMA((4,)),
            pltpu.SemaphoreType.DMA((4,)),
        ],
        compiler_params=pltpu.CompilerParams(
            collective_id=1, has_side_effects=True, vmem_limit_bytes=limit
        ),
    )(jacobians.reshape(-1), now, older)


def solution(mesh):
    in_specs = (
        P(None, "stream", "span", None),
        P(None, "stream", "span", None),
        P(),
        P(None, ("stream", "span"), None),
        P(("stream", "span"), None),
        P(("stream", "span"), None),
    )
    out_specs = P(None, "stream", "span", None)
    body = functools.partial(per_device, mesh.shape["stream"], mesh.shape["span"])
    return jax.shard_map(
        body, mesh=mesh, in_specs=in_specs, out_specs=out_specs, check_vma=False
    )
```

```python
import functools

import jax
import jax.numpy as jnp
from jax import lax
from jax.experimental import pallas as pl
from jax.experimental.pallas import tpu as pltpu
from jax.sharding import PartitionSpec as P

MESH = pl.DeviceIdType.MESH
F32 = jnp.float32
VARS = 5
CHANS = 10
SLOT = 32
REACH = 2
GROUPS = 2 * REACH + 1
CX, CY, CZ = 16, 32, 128
BX, BY = CX // 2, CY // 2
ROW = 2 * CHANS
BRICK = 2 * ROW
ROWS = BX * CY * ROW
PAD = 8
WY = CY + 2 * PAD
NEAR, FAR = 2, 5
SCALE = 0.6 / 1024.0
TAPS = (-252.0, 210.0, -120.0, 45.0, -10.0, 1.0)


def lanes(shape):
    return lax.broadcasted_iota(jnp.int32, shape, len(shape) - 1)


def window_start(i, n_stream):
    return jnp.minimum(jnp.maximum(i - REACH, 0), n_stream - GROUPS)


def exchange_kernel(
    n_stream, n_span, send_hbm, frac_ref, now_ref, prev_ref, packed_ref, fresh_ref,
    picks, sending, arrived, pick_sem, send_sem, recv_sem,
):
    i = lax.axis_index("stream")
    j = lax.axis_index("span")
    first = window_start(i, n_stream)
    far = lax.rem(i + n_stream // 2, n_stream)
    near_count = GROUPS * n_span
    far_slot = near_count

    def is_partner(g, jp):
        t = first + g
        return (t >= i - REACH) & (t <= i + REACH) & ((t != i) | (jp != j))

    barrier = pltpu.get_barrier_semaphore()
    for g in range(GROUPS):
        for jp in range(n_span):
            @pl.when(is_partner(g, jp))
            def _():
                pl.semaphore_signal(barrier, inc=1, device_id=(first + g, jp), device_id_type=MESH)
    pl.semaphore_signal(barrier, inc=1, device_id=(far, j), device_id_type=MESH)

    near_picks = pltpu.make_async_copy(
        send_hbm.at[pl.ds(first, GROUPS)], picks.at[pl.ds(0, GROUPS)], pick_sem.at[0]
    )
    far_picks = pltpu.make_async_copy(
        send_hbm.at[pl.ds(far, 1)], picks.at[pl.ds(GROUPS, 1)], pick_sem.at[1]
    )
    near_picks.start()
    far_picks.start()

    def relayout(xb, carry):
        for dx in range(2):
            for tile in range(CY // 8):
                base = xb * (CY * ROW) + tile * 8 * ROW + dx * CHANS
                for c in range(VARS):
                    packed_ref[pl.ds(base + c, 8, ROW), :] = now_ref[c, 2 * xb + dx, tile * 8:tile * 8 + 8, :]
                    packed_ref[pl.ds(base + VARS + c, 8, ROW), :] = prev_ref[c, 2 * xb + dx, tile * 8:tile * 8 + 8, :]
        return carry

    lax.fori_loop(0, BX, relayout, 0)
    near_picks.wait()
    far_picks.wait()

    rows_near = jnp.minimum(i + REACH, n_stream - 1) - jnp.maximum(i - REACH, 0) + 1
    pl.semaphore_wait(barrier, rows_near * n_span)

    half = lanes((ROW, 128)) < 64
    pair = lanes((BRICK, 128)) // 2

    def pack(p, row, start):
        total = jnp.zeros((BRICK, 128), F32)
        for k in range(SLOT):
            brick = jnp.maximum(picks[row, 0, start + k], 0)
            moved = pltpu.roll(
                packed_ref[pl.ds((brick >> 6) * BRICK, BRICK), :], (2 * k - 2 * (brick & 63)) & 127, 1
            )
            total = jnp.where(pair == k, moved, total)
        sending[p] = jnp.where(half, total[:ROW], pltpu.roll(total[ROW:], 64, 1))

    def far_copy():
        return pltpu.make_async_remote_copy(
            src_ref=sending.at[far_slot], dst_ref=arrived.at[far_slot],
            send_sem=send_sem.at[far_slot], recv_sem=recv_sem.at[far_slot],
            device_id=(far, j), device_id_type=MESH,
        )

    def near_copy(p, g, jp):
        t = first + g
        slot = (i - window_start(t, n_stream)) * n_span + j
        slot = jnp.minimum(jnp.maximum(slot, 0), near_count - 1)
        return pltpu.make_async_remote_copy(
            src_ref=sending.at[p], dst_ref=arrived.at[slot],
            send_sem=send_sem.at[p], recv_sem=recv_sem.at[slot],
            device_id=(t, jp), device_id_type=MESH,
        )

    def arrival(p):
        return pltpu.make_async_remote_copy(
            src_ref=sending.at[p], dst_ref=arrived.at[p],
            send_sem=send_sem.at[p], recv_sem=recv_sem.at[p],
            device_id=(first + p // n_span, p % n_span), device_id_type=MESH,
        )

    pack(far_slot, GROUPS, j * SLOT)
    far_copy().start()

    def send(n, carry):
        turn = n // 2
        g = jnp.where(n == 2 * turn, turn, GROUPS - 1 - turn)
        t = first + g

        @pl.when((t >= i - REACH) & (t <= i + REACH))
        def _():
            for jp in range(n_span):
                pack(g * n_span + jp, g, jp * SLOT)
            for jp in range(n_span):
                @pl.when((t != i) | (jp != j))
                def _():
                    near_copy(g * n_span + jp, g, jp).start()

        return carry

    lax.fori_loop(0, GROUPS, send, 0)
    own = (i - first) * n_span + j
    arrived[own] = sending[own]

    near_frac = [frac_ref[d, pl.ds(first, GROUPS), :] for d in range(3)]
    far_frac = [frac_ref[d, pl.ds(far, 1), :] for d in range(3)]
    table = jnp.concatenate([part for d in range(3) for part in (near_frac[d], far_frac[d])], 0)

    def spread(which):
        source = lax.broadcasted_iota(jnp.int32, (128, 128), 0)
        wanted = which * SLOT + lax.rem(lanes((128, 128)), 64) // 2
        chosen = jnp.where(source == wanted, 1.0, 0.0).astype(F32)
        return jnp.dot(table, chosen, precision=lax.Precision.HIGHEST, preferred_element_type=F32)

    spreads = [spread(jp) for jp in range(n_span)]
    far_spread = spread(j)
    even = lanes((CHANS, 128)) % 2 == 0
    low_half = lanes((CHANS, 128)) < 64

    def finish(p, fx, fy, fz):
        block = arrived[p]
        upper = block[CHANS:]
        lower = (1.0 - fx) * block[:CHANS] + fx * upper
        done = []
        for v in (lower, upper):
            v = jnp.where(low_half, (1.0 - fy) * v + fy * pltpu.roll(v, 64, 1), v)
            v = jnp.where(even, (1.0 - fz) * v + fz * pltpu.roll(v, 127, 1), v)
            done.append(v)
        both = jnp.concatenate(done, 0)
        fresh_ref[p, 0:ROW, :] = both
        fresh_ref[p, ROW:BRICK, :] = pltpu.roll(both, 64, 1)

    for p in range(near_count):
        @pl.when(is_partner(p // n_span, p % n_span))
        def _():
            arrival(p).wait_recv()

    far_copy().wait_recv()
    for p in range(near_count):
        g, jp = p // n_span, p % n_span
        finish(p, *(spreads[jp][6 * d + g:6 * d + g + 1] for d in range(3)))
    finish(far_slot, *(far_spread[6 * d + GROUPS:6 * d + GROUPS + 1] for d in range(3)))
    for p in range(near_count):
        @pl.when(is_partner(p // n_span, p % n_span))
        def _():
            arrival(p).wait_send()

    far_copy().wait_send()


def place_kernel(n_stream, n_span, recv_hbm, packed_hbm, fresh_ref, now_ref, prev_ref, targets, work, sem):
    i = lax.axis_index("stream")
    j = lax.axis_index("span")
    first = window_start(i, n_stream)
    far = lax.rem(i + n_stream // 2, n_stream)
    near_count = GROUPS * n_span
    copies = [
        pltpu.make_async_copy(recv_hbm.at[pl.ds(first, GROUPS)], targets.at[pl.ds(0, GROUPS)], sem.at[0]),
        pltpu.make_async_copy(recv_hbm.at[pl.ds(far, 1)], targets.at[pl.ds(GROUPS, 1)], sem.at[1]),
        pltpu.make_async_copy(packed_hbm, work, sem.at[2]),
    ]
    for copy in copies:
        copy.start()
    for copy in copies:
        copy.wait()
    pair = lanes((BRICK, 128)) // 2

    def put(p, row, start):
        block = fresh_ref[p]
        for k in range(SLOT):
            target = targets[row, 0, start + k]
            brick = jnp.maximum(target, 0)
            column = brick & 63
            moved = pltpu.roll(block, (2 * column - 2 * k) & 127, 1)
            mark = jnp.where(target >= 0, column, -1)
            base = pl.multiple_of((brick >> 6) * BRICK, 8)
            pltpu.store(work.at[pl.ds(base, BRICK), :], moved, mask=pair == mark)

    def put_group(g, carry):
        for jp in range(n_span):
            put(g * n_span + jp, g, jp * SLOT)
        return carry

    lax.fori_loop(0, GROUPS, put_group, 0)
    put(near_count, GROUPS, j * SLOT)

    def relayout(xb, carry):
        for dx in range(2):
            for tile in range(CY // 8):
                base = xb * (CY * ROW) + tile * 8 * ROW + dx * CHANS
                for c in range(VARS):
                    now_ref[c, 2 * xb + dx, tile * 8:tile * 8 + 8, :] = work[pl.ds(base + c, 8, ROW), :]
                    prev_ref[c, 2 * xb + dx, tile * 8:tile * 8 + 8, :] = work[pl.ds(base + VARS + c, 8, ROW), :]
        return carry

    lax.fori_loop(0, BX, relayout, 0)


def band(entries):
    source = lax.rem(lax.broadcasted_iota(jnp.int32, (2 * CZ, CZ), 0), CZ)
    away = source - lanes((2 * CZ, CZ))
    total = jnp.zeros((2 * CZ, CZ), F32)
    for offset, weight in entries:
        total = jnp.where(away == offset, weight, total)
    return total.astype(jnp.bfloat16)


def along_z(values, matrix):
    high = values.astype(jnp.bfloat16)
    low = (values - high.astype(F32)).astype(jnp.bfloat16)
    both = jnp.concatenate([high, low], 1)
    return jnp.dot(both, matrix, preferred_element_type=F32)


def advance_kernel(
    n_stream, n_span, jac, q_hbm, old_ref, out_ref,
    wide, pre, y_near_out, y_near_in, y_far_out, y_far_in,
    load_sem, near_send, near_recv, far_send, far_recv,
):
    i = lax.axis_index("stream")
    j = lax.axis_index("span")
    has = (i > 0, i < n_stream - 1, j > 0, j < n_span - 1)
    ids = ((i - 1, j), (i + 1, j), (i, j - 1), (i, j + 1))

    barrier = pltpu.get_barrier_semaphore()
    for side in range(4):
        @pl.when(has[side])
        def _():
            pl.semaphore_signal(barrier, inc=1, device_id=ids[side], device_id_type=MESH)

    load = pltpu.make_async_copy(q_hbm, wide.at[:, NEAR:NEAR + CX, PAD:PAD + CY, :], load_sem)
    load.start()

    for ref, width in ((wide, NEAR), (pre, FAR)):
        planes = CX + 2 * width

        @pl.when(~has[0])
        def _():
            ref[:, 0:width, :, :] = jnp.zeros((VARS, width, WY, CZ), F32)

        @pl.when(~has[1])
        def _():
            ref[:, width + CX:planes, :, :] = jnp.zeros((VARS, width, WY, CZ), F32)

        @pl.when(~has[2])
        def _():
            ref[:, width:width + CX, 0:PAD, :] = jnp.zeros((VARS, CX, PAD, CZ), F32)

        @pl.when(~has[3])
        def _():
            ref[:, width:width + CX, PAD + CY:WY, :] = jnp.zeros((VARS, CX, PAD, CZ), F32)

    load.wait()

    def column(ref, width, c, x, y):
        planes = CX + 2 * width
        flat = ref.reshape(VARS * planes * WY, CZ)
        return flat, pl.ds((c * planes + width + x) * WY + PAD + y, 8, WY)

    def pack(ref, out, width, side):
        for c in range(VARS):
            for m in range(width):
                for x in range(0, CX, 8):
                    flat, rows = column(ref, width, c, x, m if side == 2 else CY - width + m)
                    out[side - 2, c, m, x:x + 8, :] = flat[rows, :]

    def unpack(ref, held, width, side):
        for c in range(VARS):
            for m in range(width):
                for x in range(0, CX, 8):
                    flat, rows = column(ref, width, c, x, m - width if side == 2 else CY + m)
                    flat[rows, :] = held[side - 2, c, m, x:x + 8, :]

    def copy(ref, out, held, width, side, send, recv):
        if side == 0:
            src = ref.at[:, width:2 * width, PAD:PAD + CY, :]
            dst = ref.at[:, width + CX:2 * width + CX, PAD:PAD + CY, :]
        elif side == 1:
            src = ref.at[:, CX:width + CX, PAD:PAD + CY, :]
            dst = ref.at[:, 0:width, PAD:PAD + CY, :]
        else:
            src = out.at[side - 2]
            dst = held.at[3 - side]
        return pltpu.make_async_remote_copy(
            src_ref=src, dst_ref=dst, send_sem=send.at[side], recv_sem=recv.at[side ^ 1],
            device_id=ids[side], device_id_type=MESH,
        )

    def near(side):
        return copy(wide, y_near_out, y_near_in, NEAR, side, near_send, near_recv)

    def far(side):
        return copy(pre, y_far_out, y_far_in, FAR, side, far_send, far_recv)

    def start(make, side):
        @pl.when(has[side])
        def _():
            make(side).start()

    def finish_recv(make, side):
        @pl.when(has[side])
        def _():
            make(side ^ 1).wait_recv()

    def finish_send(make, side):
        @pl.when(has[side])
        def _():
            make(side).wait_send()

    expected = sum(jnp.where(flag, 1, 0) for flag in has)
    pl.semaphore_wait(barrier, expected)
    start(near, 0)
    start(near, 1)
    for side in (2, 3):
        pack(wide, y_near_out, NEAR, side)
        start(near, side)

    slope = band(((1, 8.0), (-1, -8.0), (2, -1.0), (-2, 1.0)))

    def base_plane(x, carry):
        q = wide[:, NEAR + x, PAD:PAD + CY, :]
        dz = along_z(q.reshape(VARS * CY, CZ), slope).reshape(VARS, CY, CZ) * (-1.0 / 36.0)
        for v in range(VARS):
            total = (4.0 * q[v] - old_ref[v, x]) * (1.0 / 3.0)
            for w in range(VARS):
                total = total + jac[50 + 5 * v + w] * dz[w]
            pre[v, FAR + x, PAD:PAD + CY, :] = total
        return carry

    lax.fori_loop(0, CX, base_plane, 0)

    for side in range(4):
        finish_recv(near, side)

    for side in (2, 3):
        @pl.when(has[side])
        def _():
            unpack(wide, y_near_in, NEAR, side)

    def rate_plane(x, carry):
        for tile in range(CY // 8):
            y = PAD + 8 * tile
            dx, dy = [], []
            for w in range(VARS):
                def at(sx, sy):
                    return wide[w, NEAR + x + sx, y + sy:y + sy + 8, :]

                dx.append((at(1, 0) - at(-1, 0)) * (-8.0 / 36.0) + (at(2, 0) - at(-2, 0)) * (1.0 / 36.0))
                dy.append((at(0, 1) - at(0, -1)) * (-8.0 / 36.0) + (at(0, 2) - at(0, -2)) * (1.0 / 36.0))
            for v in range(VARS):
                total = pre[v, FAR + x, y:y + 8, :]
                for w in range(VARS):
                    total = total + jac[5 * v + w] * dx[w]
                    total = total + jac[25 + 5 * v + w] * dy[w]
                pre[v, FAR + x, y:y + 8, :] = total
        return carry

    lax.fori_loop(0, FAR, rate_plane, 0)
    start(far, 0)
    lax.fori_loop(CX - FAR, CX, rate_plane, 0)
    start(far, 1)
    lax.fori_loop(FAR, CX - FAR, rate_plane, 0)
    for side in (2, 3):
        pack(pre, y_far_out, FAR, side)
        start(far, side)

    tenth = band(tuple((o, TAPS[abs(o)]) for o in range(-5, 6)))

    def filter_y(x, c, tile):
        y = PAD + 8 * tile

        def at(sy):
            return pre[c, FAR + x, y + sy:y + sy + 8, :]

        total = (TAPS[0] * SCALE) * at(0)
        for m in range(1, 6):
            total = total + (TAPS[m] * SCALE) * (at(m) + at(-m))
        return total

    def first_plane(x, carry):
        p = pre[:, FAR + x, PAD:PAD + CY, :]
        fz = along_z(p.reshape(VARS * CY, CZ), tenth).reshape(VARS, CY, CZ)
        total = p + SCALE * fz
        for c in range(VARS):
            for tile in range(CY // 8):
                part = total[c, 8 * tile:8 * tile + 8]
                if tile in (1, 2):
                    part = part + filter_y(x, c, tile)
                out_ref[c, x, 8 * tile:8 * tile + 8, :] = part
        return carry

    lax.fori_loop(0, CX, first_plane, 0)

    def filter_x(x, carry):
        for c in range(VARS):
            for tile in range(CY // 8):
                y = PAD + 8 * tile

                def at(sx):
                    return pre[c, FAR + x + sx, y:y + 8, :]

                total = out_ref[c, x, 8 * tile:8 * tile + 8, :] + (TAPS[0] * SCALE) * at(0)
                for m in range(1, 6):
                    total = total + (TAPS[m] * SCALE) * (at(m) + at(-m))
                out_ref[c, x, 8 * tile:8 * tile + 8, :] = total
        return carry

    lax.fori_loop(FAR, CX - FAR, filter_x, 0)
    for side in (0, 1):
        finish_recv(far, side)
    lax.fori_loop(0, FAR, filter_x, 0)
    lax.fori_loop(CX - FAR, CX, filter_x, 0)
    for side in (2, 3):
        finish_recv(far, side)

        @pl.when(has[side])
        def _():
            unpack(pre, y_far_in, FAR, side)

    def edge_plane(x, carry):
        for c in range(VARS):
            for tile in (0, CY // 8 - 1):
                rows = pl.ds(8 * tile, 8)
                out_ref[c, x, rows, :] = out_ref[c, x, rows, :] + filter_y(x, c, tile)
        return carry

    lax.fori_loop(0, CX, edge_plane, 0)
    for side in range(4):
        finish_send(near, side)
        finish_send(far, side)


def per_device(n_stream, n_span, q_now, q_prev, jacobians, fractions, send_blocks, recv_blocks):
    vmem = pl.BlockSpec(memory_space=pltpu.VMEM)
    anywhere = pl.BlockSpec(memory_space=pl.ANY)
    slots = GROUPS * n_span + 1
    width = n_span * SLOT
    sending = send_blocks.reshape(n_stream, 1, width)
    receiving = recv_blocks.reshape(n_stream, 1, width)
    offsets = fractions.reshape(3, n_stream, width)
    limit = 48 * 1024 * 1024
    packed, fresh = pl.pallas_call(
        functools.partial(exchange_kernel, n_stream, n_span),
        name="exchange",
        out_shape=(
            jax.ShapeDtypeStruct((ROWS, CZ), F32),
            jax.ShapeDtypeStruct((slots, BRICK, 128), F32),
        ),
        in_specs=[anywhere, vmem, vmem, vmem],
        out_specs=(vmem, vmem),
        scratch_shapes=[
            pltpu.SMEM((GROUPS + 1, 1, width), jnp.int32),
            pltpu.VMEM((slots, ROW, 128), F32),
            pltpu.VMEM((slots, ROW, 128), F32),
            pltpu.SemaphoreType.DMA((2,)),
            pltpu.SemaphoreType.DMA((slots,)),
            pltpu.SemaphoreType.DMA((slots,)),
        ],
        compiler_params=pltpu.CompilerParams(
            collective_id=0, has_side_effects=True, vmem_limit_bytes=limit
        ),
    )(sending, offsets, q_now, q_prev)
    shape = jax.ShapeDtypeStruct(q_now.shape, F32)
    now, older = pl.pallas_call(
        functools.partial(place_kernel, n_stream, n_span),
        name="place",
        out_shape=(shape, shape),
        in_specs=[anywhere, anywhere, vmem],
        out_specs=(vmem, vmem),
        scratch_shapes=[
            pltpu.SMEM((GROUPS + 1, 1, width), jnp.int32),
            pltpu.VMEM((ROWS, CZ), F32),
            pltpu.SemaphoreType.DMA((3,)),
        ],
        compiler_params=pltpu.CompilerParams(vmem_limit_bytes=limit),
    )(receiving, packed, fresh)
    return pl.pallas_call(
        functools.partial(advance_kernel, n_stream, n_span),
        name="advance",
        out_shape=shape,
        in_specs=[pl.BlockSpec(memory_space=pltpu.SMEM), anywhere, vmem],
        out_specs=vmem,
        scratch_shapes=[
            pltpu.VMEM((VARS, CX + 2 * NEAR, WY, CZ), F32),
            pltpu.VMEM((VARS, CX + 2 * FAR, WY, CZ), F32),
            pltpu.VMEM((2, VARS, NEAR, CX, CZ), F32),
            pltpu.VMEM((2, VARS, NEAR, CX, CZ), F32),
            pltpu.VMEM((2, VARS, FAR, CX, CZ), F32),
            pltpu.VMEM((2, VARS, FAR, CX, CZ), F32),
            pltpu.SemaphoreType.DMA,
            pltpu.SemaphoreType.DMA((4,)),
            pltpu.SemaphoreType.DMA((4,)),
            pltpu.SemaphoreType.DMA((4,)),
            pltpu.SemaphoreType.DMA((4,)),
        ],
        compiler_params=pltpu.CompilerParams(
            collective_id=1, has_side_effects=True, vmem_limit_bytes=limit
        ),
    )(jacobians.reshape(-1), now, older)


def solution(mesh):
    in_specs = (
        P(None, "stream", "span", None),
        P(None, "stream", "span", None),
        P(),
        P(None, ("stream", "span"), None),
        P(("stream", "span"), None),
        P(("stream", "span"), None),
    )
    out_specs = P(None, "stream", "span", None)
    body = functools.partial(per_device, mesh.shape["stream"], mesh.shape["span"])
    return jax.shard_map(
        body, mesh=mesh, in_specs=in_specs, out_specs=out_specs, check_vma=False
    )
```

```python
import functools

import jax
import jax.numpy as jnp
from jax import lax
from jax.experimental import pallas as pl
from jax.experimental.pallas import tpu as pltpu
from jax.sharding import PartitionSpec as P

MESH = pl.DeviceIdType.MESH
F32 = jnp.float32
VARS = 5
CHANS = 10
SLOT = 32
REACH = 2
PARTS = 4
EARLY = 2
GROUPS = 2 * REACH + 1
CX, CY, CZ = 16, 32, 128
BX, BY = CX // 2, CY // 2
ROW = 2 * CHANS
BRICK = 2 * ROW
ROWS = BX * CY * ROW
PAD = 8
WY = CY + 2 * PAD
NEAR, FAR = 2, 5
SCALE = 0.6 / 1024.0
TAPS = (-252.0, 210.0, -120.0, 45.0, -10.0, 1.0)


def lanes(shape):
    return lax.broadcasted_iota(jnp.int32, shape, len(shape) - 1)


def window_start(i, n_stream):
    return jnp.minimum(jnp.maximum(i - REACH, 0), n_stream - GROUPS)


def exchange_kernel(
    n_stream, n_span, send_hbm, frac_hbm, now_hbm, prev_hbm, packed_ref, fresh_ref,
    picks, frac_ref, now_ref, prev_ref, sending, arrived, pick_sem, load_sem, send_sem, recv_sem,
):
    i = lax.axis_index("stream")
    j = lax.axis_index("span")
    first = window_start(i, n_stream)
    far = lax.rem(i + n_stream // 2, n_stream)
    near_count = GROUPS * n_span
    far_slot = near_count

    def is_partner(g, jp):
        t = first + g
        return (t >= i - REACH) & (t <= i + REACH) & ((t != i) | (jp != j))

    loads = [
        pltpu.make_async_copy(
            src.at[:, pl.ds(part * CX // PARTS, CX // PARTS)],
            dst.at[:, pl.ds(part * CX // PARTS, CX // PARTS)],
            load_sem.at[2 * part + n],
        )
        for part in range(PARTS)
        for n, (src, dst) in enumerate(((now_hbm, now_ref), (prev_hbm, prev_ref)))
    ]
    others = [
        pltpu.make_async_copy(
            send_hbm.at[pl.ds(first, GROUPS)], picks.at[pl.ds(0, GROUPS)], pick_sem.at[0]
        ),
        pltpu.make_async_copy(
            send_hbm.at[pl.ds(far, 1)], picks.at[pl.ds(GROUPS, 1)], pick_sem.at[1]
        ),
        pltpu.make_async_copy(frac_hbm, frac_ref, pick_sem.at[2]),
    ]
    for copy in loads + others:
        copy.start()

    barrier = pltpu.get_barrier_semaphore()
    for g in range(GROUPS):
        for jp in range(n_span):
            @pl.when(is_partner(g, jp))
            def _():
                pl.semaphore_signal(barrier, inc=1, device_id=(first + g, jp), device_id_type=MESH)
    pl.semaphore_signal(barrier, inc=1, device_id=(far, j), device_id_type=MESH)

    def relayout(xb, carry):
        for dx in range(2):
            for tile in range(CY // 8):
                base = xb * (CY * ROW) + tile * 8 * ROW + dx * CHANS
                for c in range(VARS):
                    packed_ref[pl.ds(base + c, 8, ROW), :] = now_ref[c, 2 * xb + dx, tile * 8:tile * 8 + 8, :]
                    packed_ref[pl.ds(base + VARS + c, 8, ROW), :] = prev_ref[c, 2 * xb + dx, tile * 8:tile * 8 + 8, :]
        return carry

    for part in range(PARTS):
        loads[2 * part].wait()
        loads[2 * part + 1].wait()
        lax.fori_loop(part * BX // PARTS, (part + 1) * BX // PARTS, relayout, 0)
    for copy in others:
        copy.wait()

    half = lanes((ROW, 128)) < 64
    pair = lanes((BRICK, 128)) // 2

    def pack(p, row, start):
        total = jnp.zeros((BRICK, 128), F32)
        for k in range(SLOT):
            brick = jnp.maximum(picks[row, 0, start + k], 0)
            moved = pltpu.roll(
                packed_ref[pl.ds((brick >> 6) * BRICK, BRICK), :], (2 * k - 2 * (brick & 63)) & 127, 1
            )
            total = jnp.where(pair == k, moved, total)
        sending[p] = jnp.where(half, total[:ROW], pltpu.roll(total[ROW:], 64, 1))

    def far_copy():
        return pltpu.make_async_remote_copy(
            src_ref=sending.at[far_slot], dst_ref=arrived.at[far_slot],
            send_sem=send_sem.at[far_slot], recv_sem=recv_sem.at[far_slot],
            device_id=(far, j), device_id_type=MESH,
        )

    def near_copy(p, g, jp):
        t = first + g
        slot = (i - window_start(t, n_stream)) * n_span + j
        slot = jnp.minimum(jnp.maximum(slot, 0), near_count - 1)
        return pltpu.make_async_remote_copy(
            src_ref=sending.at[p], dst_ref=arrived.at[slot],
            send_sem=send_sem.at[p], recv_sem=recv_sem.at[slot],
            device_id=(t, jp), device_id_type=MESH,
        )

    def arrival(p):
        return pltpu.make_async_remote_copy(
            src_ref=sending.at[p], dst_ref=arrived.at[p],
            send_sem=send_sem.at[p], recv_sem=recv_sem.at[p],
            device_id=(first + p // n_span, p % n_span), device_id_type=MESH,
        )

    def start_near(g, jp):
        @pl.when(is_partner(g, jp))
        def _():
            near_copy(g * n_span + jp, g, jp).start()

    rows_near = jnp.minimum(i + REACH, n_stream - 1) - jnp.maximum(i - REACH, 0) + 1

    def column(n):
        return lax.rem(j + jnp.where(n == 0, 2, jnp.where(n == 1, 1, jnp.where(n == 2, 3, 0))), n_span)

    def send(n, carry):
        jp = column(n)
        for g in range(GROUPS):
            pack(g * n_span + jp, g, jp * SLOT)

        @pl.when(n == 0)
        def _():
            pack(far_slot, GROUPS, j * SLOT)

        @pl.when(n == EARLY - 1)
        def _():
            pl.semaphore_wait(barrier, rows_near * n_span)
            for early in range(EARLY):
                for g in (0, 4, 1, 3, 2):
                    start_near(g, column(early))
                if early == 0:
                    far_copy().start()

        @pl.when(n >= EARLY)
        def _():
            for g in (0, 4, 1, 3, 2):
                start_near(g, jp)

        return carry

    lax.fori_loop(0, n_span, send, 0)
    own = (i - first) * n_span + j
    arrived[own] = sending[own]

    near_frac = [frac_ref[d, pl.ds(first, GROUPS), :] for d in range(3)]
    far_frac = [frac_ref[d, pl.ds(far, 1), :] for d in range(3)]
    table = jnp.concatenate([part for d in range(3) for part in (near_frac[d], far_frac[d])], 0)

    def spread(which):
        source = lax.broadcasted_iota(jnp.int32, (128, 128), 0)
        wanted = which * SLOT + lax.rem(lanes((128, 128)), 64) // 2
        chosen = jnp.where(source == wanted, 1.0, 0.0).astype(F32)
        return jnp.dot(table, chosen, precision=lax.Precision.HIGHEST, preferred_element_type=F32)

    spreads = [spread(jp) for jp in range(n_span)]
    far_spread = spread(j)
    even = lanes((CHANS, 128)) % 2 == 0
    low_half = lanes((CHANS, 128)) < 64

    def finish(p, fx, fy, fz):
        block = arrived[p]
        upper = block[CHANS:]
        lower = (1.0 - fx) * block[:CHANS] + fx * upper
        done = []
        for v in (lower, upper):
            v = jnp.where(low_half, (1.0 - fy) * v + fy * pltpu.roll(v, 64, 1), v)
            v = jnp.where(even, (1.0 - fz) * v + fz * pltpu.roll(v, 127, 1), v)
            done.append(v)
        both = jnp.concatenate(done, 0)
        fresh_ref[p, 0:ROW, :] = both
        fresh_ref[p, ROW:BRICK, :] = pltpu.roll(both, 64, 1)

    for p in range(near_count):
        @pl.when(is_partner(p // n_span, p % n_span))
        def _():
            arrival(p).wait_recv()

    far_copy().wait_recv()
    for p in range(near_count):
        g, jp = p // n_span, p % n_span
        finish(p, *(spreads[jp][6 * d + g:6 * d + g + 1] for d in range(3)))
    finish(far_slot, *(far_spread[6 * d + GROUPS:6 * d + GROUPS + 1] for d in range(3)))
    for p in range(near_count):
        @pl.when(is_partner(p // n_span, p % n_span))
        def _():
            arrival(p).wait_send()

    far_copy().wait_send()


def place_kernel(n_stream, n_span, recv_hbm, packed_hbm, fresh_ref, now_ref, prev_ref, targets, work, sem):
    i = lax.axis_index("stream")
    j = lax.axis_index("span")
    first = window_start(i, n_stream)
    far = lax.rem(i + n_stream // 2, n_stream)
    near_count = GROUPS * n_span
    copies = [
        pltpu.make_async_copy(recv_hbm.at[pl.ds(first, GROUPS)], targets.at[pl.ds(0, GROUPS)], sem.at[0]),
        pltpu.make_async_copy(recv_hbm.at[pl.ds(far, 1)], targets.at[pl.ds(GROUPS, 1)], sem.at[1]),
        pltpu.make_async_copy(packed_hbm, work, sem.at[2]),
    ]
    for copy in copies:
        copy.start()
    for copy in copies:
        copy.wait()
    pair = lanes((BRICK, 128)) // 2

    def put(p, row, start):
        block = fresh_ref[p]
        for k in range(SLOT):
            target = targets[row, 0, start + k]
            brick = jnp.maximum(target, 0)
            column = brick & 63
            moved = pltpu.roll(block, (2 * column - 2 * k) & 127, 1)
            mark = jnp.where(target >= 0, column, -1)
            base = pl.multiple_of((brick >> 6) * BRICK, 8)
            pltpu.store(work.at[pl.ds(base, BRICK), :], moved, mask=pair == mark)

    def put_group(g, carry):
        for jp in range(n_span):
            put(g * n_span + jp, g, jp * SLOT)
        return carry

    lax.fori_loop(0, GROUPS, put_group, 0)
    put(near_count, GROUPS, j * SLOT)

    def relayout(xb, carry):
        for dx in range(2):
            for tile in range(CY // 8):
                base = xb * (CY * ROW) + tile * 8 * ROW + dx * CHANS
                for c in range(VARS):
                    now_ref[c, 2 * xb + dx, tile * 8:tile * 8 + 8, :] = work[pl.ds(base + c, 8, ROW), :]
                    prev_ref[c, 2 * xb + dx, tile * 8:tile * 8 + 8, :] = work[pl.ds(base + VARS + c, 8, ROW), :]
        return carry

    lax.fori_loop(0, BX, relayout, 0)


def band(entries):
    source = lax.rem(lax.broadcasted_iota(jnp.int32, (2 * CZ, CZ), 0), CZ)
    away = source - lanes((2 * CZ, CZ))
    total = jnp.zeros((2 * CZ, CZ), F32)
    for offset, weight in entries:
        total = jnp.where(away == offset, weight, total)
    return total.astype(jnp.bfloat16)


def along_z(values, matrix):
    high = values.astype(jnp.bfloat16)
    low = (values - high.astype(F32)).astype(jnp.bfloat16)
    both = jnp.concatenate([high, low], 1)
    return jnp.dot(both, matrix, preferred_element_type=F32)


def advance_kernel(
    n_stream, n_span, jac, q_hbm, old_ref, out_ref,
    wide, pre, y_near_out, y_near_in, y_far_out, y_far_in,
    load_sem, near_send, near_recv, far_send, far_recv,
):
    i = lax.axis_index("stream")
    j = lax.axis_index("span")
    has = (i > 0, i < n_stream - 1, j > 0, j < n_span - 1)
    ids = ((i - 1, j), (i + 1, j), (i, j - 1), (i, j + 1))

    barrier = pltpu.get_barrier_semaphore()
    for side in range(4):
        @pl.when(has[side])
        def _():
            pl.semaphore_signal(barrier, inc=1, device_id=ids[side], device_id_type=MESH)

    load = pltpu.make_async_copy(q_hbm, wide.at[:, NEAR:NEAR + CX, PAD:PAD + CY, :], load_sem)
    load.start()

    for ref, width in ((wide, NEAR), (pre, FAR)):
        planes = CX + 2 * width

        @pl.when(~has[0])
        def _():
            ref[:, 0:width, :, :] = jnp.zeros((VARS, width, WY, CZ), F32)

        @pl.when(~has[1])
        def _():
            ref[:, width + CX:planes, :, :] = jnp.zeros((VARS, width, WY, CZ), F32)

        @pl.when(~has[2])
        def _():
            ref[:, width:width + CX, 0:PAD, :] = jnp.zeros((VARS, CX, PAD, CZ), F32)

        @pl.when(~has[3])
        def _():
            ref[:, width:width + CX, PAD + CY:WY, :] = jnp.zeros((VARS, CX, PAD, CZ), F32)

    load.wait()

    def column(ref, width, c, x, y):
        planes = CX + 2 * width
        flat = ref.reshape(VARS * planes * WY, CZ)
        return flat, pl.ds((c * planes + width + x) * WY + PAD + y, 8, WY)

    def pack(ref, out, width, side):
        for c in range(VARS):
            for m in range(width):
                for x in range(0, CX, 8):
                    flat, rows = column(ref, width, c, x, m if side == 2 else CY - width + m)
                    out[side - 2, c, m, x:x + 8, :] = flat[rows, :]

    def unpack(ref, held, width, side):
        for c in range(VARS):
            for m in range(width):
                for x in range(0, CX, 8):
                    flat, rows = column(ref, width, c, x, m - width if side == 2 else CY + m)
                    flat[rows, :] = held[side - 2, c, m, x:x + 8, :]

    def copy(ref, out, held, width, side, send, recv):
        if side == 0:
            src = ref.at[:, width:2 * width, PAD:PAD + CY, :]
            dst = ref.at[:, width + CX:2 * width + CX, PAD:PAD + CY, :]
        elif side == 1:
            src = ref.at[:, CX:width + CX, PAD:PAD + CY, :]
            dst = ref.at[:, 0:width, PAD:PAD + CY, :]
        else:
            src = out.at[side - 2]
            dst = held.at[3 - side]
        return pltpu.make_async_remote_copy(
            src_ref=src, dst_ref=dst, send_sem=send.at[side], recv_sem=recv.at[side ^ 1],
            device_id=ids[side], device_id_type=MESH,
        )

    def near(side):
        return copy(wide, y_near_out, y_near_in, NEAR, side, near_send, near_recv)

    def far(side):
        return copy(pre, y_far_out, y_far_in, FAR, side, far_send, far_recv)

    def start(make, side):
        @pl.when(has[side])
        def _():
            make(side).start()

    def finish_recv(make, side):
        @pl.when(has[side])
        def _():
            make(side ^ 1).wait_recv()

    def finish_send(make, side):
        @pl.when(has[side])
        def _():
            make(side).wait_send()

    expected = sum(jnp.where(flag, 1, 0) for flag in has)
    pl.semaphore_wait(barrier, expected)
    start(near, 0)
    start(near, 1)
    for side in (2, 3):
        pack(wide, y_near_out, NEAR, side)
        start(near, side)

    slope = band(((1, 8.0), (-1, -8.0), (2, -1.0), (-2, 1.0)))

    def base_plane(x, carry):
        q = wide[:, NEAR + x, PAD:PAD + CY, :]
        dz = along_z(q.reshape(VARS * CY, CZ), slope).reshape(VARS, CY, CZ) * (-1.0 / 36.0)
        for v in range(VARS):
            total = (4.0 * q[v] - old_ref[v, x]) * (1.0 / 3.0)
            for w in range(VARS):
                total = total + jac[50 + 5 * v + w] * dz[w]
            pre[v, FAR + x, PAD:PAD + CY, :] = total
        return carry

    lax.fori_loop(0, CX, base_plane, 0)

    for side in range(4):
        finish_recv(near, side)

    for side in (2, 3):
        @pl.when(has[side])
        def _():
            unpack(wide, y_near_in, NEAR, side)

    def rate_plane(x, carry):
        for tile in range(CY // 8):
            y = PAD + 8 * tile
            dx, dy = [], []
            for w in range(VARS):
                def at(sx, sy):
                    return wide[w, NEAR + x + sx, y + sy:y + sy + 8, :]

                dx.append((at(1, 0) - at(-1, 0)) * (-8.0 / 36.0) + (at(2, 0) - at(-2, 0)) * (1.0 / 36.0))
                dy.append((at(0, 1) - at(0, -1)) * (-8.0 / 36.0) + (at(0, 2) - at(0, -2)) * (1.0 / 36.0))
            for v in range(VARS):
                total = pre[v, FAR + x, y:y + 8, :]
                for w in range(VARS):
                    total = total + jac[5 * v + w] * dx[w]
                    total = total + jac[25 + 5 * v + w] * dy[w]
                pre[v, FAR + x, y:y + 8, :] = total
        return carry

    lax.fori_loop(0, FAR, rate_plane, 0)
    start(far, 0)
    lax.fori_loop(CX - FAR, CX, rate_plane, 0)
    start(far, 1)
    lax.fori_loop(FAR, CX - FAR, rate_plane, 0)
    for side in (2, 3):
        pack(pre, y_far_out, FAR, side)
        start(far, side)

    tenth = band(tuple((o, TAPS[abs(o)]) for o in range(-5, 6)))

    def filter_y(x, c, tile):
        y = PAD + 8 * tile

        def at(sy):
            return pre[c, FAR + x, y + sy:y + sy + 8, :]

        total = (TAPS[0] * SCALE) * at(0)
        for m in range(1, 6):
            total = total + (TAPS[m] * SCALE) * (at(m) + at(-m))
        return total

    def first_plane(x, carry):
        p = pre[:, FAR + x, PAD:PAD + CY, :]
        fz = along_z(p.reshape(VARS * CY, CZ), tenth).reshape(VARS, CY, CZ)
        total = p + SCALE * fz
        for c in range(VARS):
            for tile in range(CY // 8):
                part = total[c, 8 * tile:8 * tile + 8]
                if tile in (1, 2):
                    part = part + filter_y(x, c, tile)
                out_ref[c, x, 8 * tile:8 * tile + 8, :] = part
        return carry

    lax.fori_loop(0, CX, first_plane, 0)

    def filter_x(x, carry):
        for c in range(VARS):
            for tile in range(CY // 8):
                y = PAD + 8 * tile

                def at(sx):
                    return pre[c, FAR + x + sx, y:y + 8, :]

                total = out_ref[c, x, 8 * tile:8 * tile + 8, :] + (TAPS[0] * SCALE) * at(0)
                for m in range(1, 6):
                    total = total + (TAPS[m] * SCALE) * (at(m) + at(-m))
                out_ref[c, x, 8 * tile:8 * tile + 8, :] = total
        return carry

    lax.fori_loop(FAR, CX - FAR, filter_x, 0)
    for side in (0, 1):
        finish_recv(far, side)
    lax.fori_loop(0, FAR, filter_x, 0)
    lax.fori_loop(CX - FAR, CX, filter_x, 0)
    for side in (2, 3):
        finish_recv(far, side)

        @pl.when(has[side])
        def _():
            unpack(pre, y_far_in, FAR, side)

    def edge_plane(x, carry):
        for c in range(VARS):
            for tile in (0, CY // 8 - 1):
                rows = pl.ds(8 * tile, 8)
                out_ref[c, x, rows, :] = out_ref[c, x, rows, :] + filter_y(x, c, tile)
        return carry

    lax.fori_loop(0, CX, edge_plane, 0)
    for side in range(4):
        finish_send(near, side)
        finish_send(far, side)


def per_device(n_stream, n_span, q_now, q_prev, jacobians, fractions, send_blocks, recv_blocks):
    vmem = pl.BlockSpec(memory_space=pltpu.VMEM)
    anywhere = pl.BlockSpec(memory_space=pl.ANY)
    slots = GROUPS * n_span + 1
    width = n_span * SLOT
    sending = send_blocks.reshape(n_stream, 1, width)
    receiving = recv_blocks.reshape(n_stream, 1, width)
    offsets = fractions.reshape(3, n_stream, width)
    limit = 48 * 1024 * 1024
    packed, fresh = pl.pallas_call(
        functools.partial(exchange_kernel, n_stream, n_span),
        name="exchange",
        out_shape=(
            jax.ShapeDtypeStruct((ROWS, CZ), F32),
            jax.ShapeDtypeStruct((slots, BRICK, 128), F32),
        ),
        in_specs=[anywhere] * 4,
        out_specs=(vmem, vmem),
        scratch_shapes=[
            pltpu.SMEM((GROUPS + 1, 1, width), jnp.int32),
            pltpu.VMEM((3, n_stream, width), F32),
            pltpu.VMEM(q_now.shape, F32),
            pltpu.VMEM(q_now.shape, F32),
            pltpu.VMEM((slots, ROW, 128), F32),
            pltpu.VMEM((slots, ROW, 128), F32),
            pltpu.SemaphoreType.DMA((3,)),
            pltpu.SemaphoreType.DMA((2 * PARTS,)),
            pltpu.SemaphoreType.DMA((slots,)),
            pltpu.SemaphoreType.DMA((slots,)),
        ],
        compiler_params=pltpu.CompilerParams(
            collective_id=0, has_side_effects=True, vmem_limit_bytes=48 * 1024 * 1024
        ),
    )(*(pltpu.with_memory_space_constraint(x, pltpu.HBM) for x in (sending, offsets, q_now, q_prev)))
    shape = jax.ShapeDtypeStruct(q_now.shape, F32)
    now, older = pl.pallas_call(
        functools.partial(place_kernel, n_stream, n_span),
        name="place",
        out_shape=(shape, shape),
        in_specs=[anywhere, anywhere, vmem],
        out_specs=(vmem, vmem),
        scratch_shapes=[
            pltpu.SMEM((GROUPS + 1, 1, width), jnp.int32),
            pltpu.VMEM((ROWS, CZ), F32),
            pltpu.SemaphoreType.DMA((3,)),
        ],
        compiler_params=pltpu.CompilerParams(vmem_limit_bytes=limit),
    )(receiving, packed, fresh)
    return pl.pallas_call(
        functools.partial(advance_kernel, n_stream, n_span),
        name="advance",
        out_shape=shape,
        in_specs=[pl.BlockSpec(memory_space=pltpu.SMEM), anywhere, vmem],
        out_specs=vmem,
        scratch_shapes=[
            pltpu.VMEM((VARS, CX + 2 * NEAR, WY, CZ), F32),
            pltpu.VMEM((VARS, CX + 2 * FAR, WY, CZ), F32),
            pltpu.VMEM((2, VARS, NEAR, CX, CZ), F32),
            pltpu.VMEM((2, VARS, NEAR, CX, CZ), F32),
            pltpu.VMEM((2, VARS, FAR, CX, CZ), F32),
            pltpu.VMEM((2, VARS, FAR, CX, CZ), F32),
            pltpu.SemaphoreType.DMA,
            pltpu.SemaphoreType.DMA((4,)),
            pltpu.SemaphoreType.DMA((4,)),
            pltpu.SemaphoreType.DMA((4,)),
            pltpu.SemaphoreType.DMA((4,)),
        ],
        compiler_params=pltpu.CompilerParams(
            collective_id=1, has_side_effects=True, vmem_limit_bytes=limit
        ),
    )(jacobians.reshape(-1), now, older)


def solution(mesh):
    in_specs = (
        P(None, "stream", "span", None),
        P(None, "stream", "span", None),
        P(),
        P(None, ("stream", "span"), None),
        P(("stream", "span"), None),
        P(("stream", "span"), None),
    )
    out_specs = P(None, "stream", "span", None)
    body = functools.partial(per_device, mesh.shape["stream"], mesh.shape["span"])
    return jax.shard_map(
        body, mesh=mesh, in_specs=in_specs, out_specs=out_specs, check_vma=False
    )
```

```python
import functools

import jax
import jax.numpy as jnp
from jax import lax
from jax.experimental import pallas as pl
from jax.experimental.pallas import tpu as pltpu
from jax.sharding import PartitionSpec as P

MESH = pl.DeviceIdType.MESH
F32 = jnp.float32
VARS = 5
CHANS = 10
SLOT = 32
REACH = 2
PARTS = 4
EARLY = 2
BATCH = 4
GROUPS = 2 * REACH + 1
CX, CY, CZ = 16, 32, 128
BX, BY = CX // 2, CY // 2
ROW = 2 * CHANS
BRICK = 2 * ROW
ROWS = BX * CY * ROW
PAD = 8
WY = CY + 2 * PAD
NEAR, FAR = 2, 5
SCALE = 0.6 / 1024.0
TAPS = (-252.0, 210.0, -120.0, 45.0, -10.0, 1.0)


def lanes(shape):
    return lax.broadcasted_iota(jnp.int32, shape, len(shape) - 1)


def window_start(i, n_stream):
    return jnp.minimum(jnp.maximum(i - REACH, 0), n_stream - GROUPS)


def exchange_kernel(
    n_stream, n_span, send_hbm, frac_hbm, now_hbm, prev_hbm, packed_ref, fresh_ref,
    picks, frac_ref, now_ref, prev_ref, sending, arrived, pick_sem, load_sem, send_sem, recv_sem,
):
    i = lax.axis_index("stream")
    j = lax.axis_index("span")
    first = window_start(i, n_stream)
    far = lax.rem(i + n_stream // 2, n_stream)
    near_count = GROUPS * n_span
    far_slot = near_count

    def is_partner(g, jp):
        t = first + g
        return (t >= i - REACH) & (t <= i + REACH) & ((t != i) | (jp != j))

    loads = [
        pltpu.make_async_copy(
            src.at[:, pl.ds(part * CX // PARTS, CX // PARTS)],
            dst.at[:, pl.ds(part * CX // PARTS, CX // PARTS)],
            load_sem.at[2 * part + n],
        )
        for part in range(PARTS)
        for n, (src, dst) in enumerate(((now_hbm, now_ref), (prev_hbm, prev_ref)))
    ]
    others = [
        pltpu.make_async_copy(
            send_hbm.at[pl.ds(first, GROUPS)], picks.at[pl.ds(0, GROUPS)], pick_sem.at[0]
        ),
        pltpu.make_async_copy(
            send_hbm.at[pl.ds(far, 1)], picks.at[pl.ds(GROUPS, 1)], pick_sem.at[1]
        ),
        pltpu.make_async_copy(frac_hbm, frac_ref, pick_sem.at[2]),
    ]
    for copy in loads + others:
        copy.start()

    barrier = pltpu.get_barrier_semaphore()
    for g in range(GROUPS):
        for jp in range(n_span):
            @pl.when(is_partner(g, jp))
            def _():
                pl.semaphore_signal(barrier, inc=1, device_id=(first + g, jp), device_id_type=MESH)
    pl.semaphore_signal(barrier, inc=1, device_id=(far, j), device_id_type=MESH)

    def relayout(xb, carry):
        for dx in range(2):
            for tile in range(CY // 8):
                base = xb * (CY * ROW) + tile * 8 * ROW + dx * CHANS
                for c in range(VARS):
                    packed_ref[pl.ds(base + c, 8, ROW), :] = now_ref[c, 2 * xb + dx, tile * 8:tile * 8 + 8, :]
                    packed_ref[pl.ds(base + VARS + c, 8, ROW), :] = prev_ref[c, 2 * xb + dx, tile * 8:tile * 8 + 8, :]
        return carry

    for part in range(PARTS):
        loads[2 * part].wait()
        loads[2 * part + 1].wait()
        lax.fori_loop(part * BX // PARTS, (part + 1) * BX // PARTS, relayout, 0)
    for copy in others:
        copy.wait()

    half = lanes((ROW, 128)) < 64
    pair = lanes((BRICK, 128)) // 2

    def pack(p, row, start):
        total = jnp.zeros((BRICK, 128), F32)
        for k in range(SLOT):
            brick = jnp.maximum(picks[row, 0, start + k], 0)
            moved = pltpu.roll(
                packed_ref[pl.ds((brick >> 6) * BRICK, BRICK), :], (2 * k - 2 * (brick & 63)) & 127, 1
            )
            total = jnp.where(pair == k, moved, total)
        sending[p] = jnp.where(half, total[:ROW], pltpu.roll(total[ROW:], 64, 1))

    def far_copy():
        return pltpu.make_async_remote_copy(
            src_ref=sending.at[far_slot], dst_ref=arrived.at[far_slot],
            send_sem=send_sem.at[far_slot], recv_sem=recv_sem.at[far_slot],
            device_id=(far, j), device_id_type=MESH,
        )

    def near_copy(p, g, jp):
        t = first + g
        slot = (i - window_start(t, n_stream)) * n_span + j
        slot = jnp.minimum(jnp.maximum(slot, 0), near_count - 1)
        return pltpu.make_async_remote_copy(
            src_ref=sending.at[p], dst_ref=arrived.at[slot],
            send_sem=send_sem.at[p], recv_sem=recv_sem.at[slot],
            device_id=(t, jp), device_id_type=MESH,
        )

    def arrival(p):
        return pltpu.make_async_remote_copy(
            src_ref=sending.at[p], dst_ref=arrived.at[p],
            send_sem=send_sem.at[p], recv_sem=recv_sem.at[p],
            device_id=(first + p // n_span, p % n_span), device_id_type=MESH,
        )

    def start_near(g, jp):
        @pl.when(is_partner(g, jp))
        def _():
            near_copy(g * n_span + jp, g, jp).start()

    rows_near = jnp.minimum(i + REACH, n_stream - 1) - jnp.maximum(i - REACH, 0) + 1

    def column(n):
        return lax.rem(j + jnp.where(n == 0, 2, jnp.where(n == 1, 1, jnp.where(n == 2, 3, 0))), n_span)

    def send(n, carry):
        jp = column(n)
        for g in range(GROUPS):
            pack(g * n_span + jp, g, jp * SLOT)

        @pl.when(n == 0)
        def _():
            pack(far_slot, GROUPS, j * SLOT)

        @pl.when(n == EARLY - 1)
        def _():
            pl.semaphore_wait(barrier, rows_near * n_span)
            for early in range(EARLY):
                for g in (0, 4, 1, 3, 2):
                    start_near(g, column(early))
                if early == 0:
                    far_copy().start()

        @pl.when(n >= EARLY)
        def _():
            for g in (0, 4, 1, 3, 2):
                start_near(g, jp)

        return carry

    lax.fori_loop(0, n_span, send, 0)
    own = (i - first) * n_span + j
    arrived[own] = sending[own]

    near_frac = [frac_ref[d, pl.ds(first, GROUPS), :] for d in range(3)]
    far_frac = [frac_ref[d, pl.ds(far, 1), :] for d in range(3)]
    table = jnp.concatenate([part for d in range(3) for part in (near_frac[d], far_frac[d])], 0)

    def spread(which):
        source = lax.broadcasted_iota(jnp.int32, (128, 128), 0)
        wanted = which * SLOT + lax.rem(lanes((128, 128)), 64) // 2
        chosen = jnp.where(source == wanted, 1.0, 0.0).astype(F32)
        return jnp.dot(table, chosen, precision=lax.Precision.HIGHEST, preferred_element_type=F32)

    spreads = [spread(jp) for jp in range(n_span)]
    far_spread = spread(j)
    even = lanes((CHANS, 128)) % 2 == 0
    low_half = lanes((CHANS, 128)) < 64

    def finish(p, fx, fy, fz):
        block = arrived[p]
        upper = block[CHANS:]
        lower = (1.0 - fx) * block[:CHANS] + fx * upper
        done = []
        for v in (lower, upper):
            v = jnp.where(low_half, (1.0 - fy) * v + fy * pltpu.roll(v, 64, 1), v)
            v = jnp.where(even, (1.0 - fz) * v + fz * pltpu.roll(v, 127, 1), v)
            done.append(v)
        both = jnp.concatenate(done, 0)
        fresh_ref[p, 0:ROW, :] = both
        fresh_ref[p, ROW:BRICK, :] = pltpu.roll(both, 64, 1)

    for p in range(near_count):
        @pl.when(is_partner(p // n_span, p % n_span))
        def _():
            arrival(p).wait_recv()

    far_copy().wait_recv()
    for p in range(near_count):
        g, jp = p // n_span, p % n_span
        finish(p, *(spreads[jp][6 * d + g:6 * d + g + 1] for d in range(3)))
    finish(far_slot, *(far_spread[6 * d + GROUPS:6 * d + GROUPS + 1] for d in range(3)))
    for p in range(near_count):
        @pl.when(is_partner(p // n_span, p % n_span))
        def _():
            arrival(p).wait_send()

    far_copy().wait_send()


def place_kernel(n_stream, n_span, recv_hbm, packed_hbm, fresh_ref, now_ref, prev_ref, targets, work, sem):
    i = lax.axis_index("stream")
    j = lax.axis_index("span")
    first = window_start(i, n_stream)
    far = lax.rem(i + n_stream // 2, n_stream)
    near_count = GROUPS * n_span
    copies = [
        pltpu.make_async_copy(recv_hbm.at[pl.ds(first, GROUPS)], targets.at[pl.ds(0, GROUPS)], sem.at[0]),
        pltpu.make_async_copy(recv_hbm.at[pl.ds(far, 1)], targets.at[pl.ds(GROUPS, 1)], sem.at[1]),
        pltpu.make_async_copy(packed_hbm, work, sem.at[2]),
    ]
    for copy in copies:
        copy.start()
    for copy in copies:
        copy.wait()
    pair = lanes((BRICK, 128)) // 2

    def put(p, row, start):
        block = fresh_ref[p]
        for k in range(SLOT):
            target = targets[row, 0, start + k]
            brick = jnp.maximum(target, 0)
            column = brick & 63
            moved = pltpu.roll(block, (2 * column - 2 * k) & 127, 1)
            mark = jnp.where(target >= 0, column, -1)
            base = pl.multiple_of((brick >> 6) * BRICK, 8)
            pltpu.store(work.at[pl.ds(base, BRICK), :], moved, mask=pair == mark)

    def put_group(g, carry):
        for jp in range(n_span):
            put(g * n_span + jp, g, jp * SLOT)
        return carry

    lax.fori_loop(0, GROUPS, put_group, 0)
    put(near_count, GROUPS, j * SLOT)

    def relayout(xb, carry):
        for dx in range(2):
            for tile in range(CY // 8):
                base = xb * (CY * ROW) + tile * 8 * ROW + dx * CHANS
                for c in range(VARS):
                    now_ref[c, 2 * xb + dx, tile * 8:tile * 8 + 8, :] = work[pl.ds(base + c, 8, ROW), :]
                    prev_ref[c, 2 * xb + dx, tile * 8:tile * 8 + 8, :] = work[pl.ds(base + VARS + c, 8, ROW), :]
        return carry

    lax.fori_loop(0, BX, relayout, 0)


def band(entries):
    source = lax.rem(lax.broadcasted_iota(jnp.int32, (2 * CZ, CZ), 0), CZ)
    away = source - lanes((2 * CZ, CZ))
    total = jnp.zeros((2 * CZ, CZ), F32)
    for offset, weight in entries:
        total = jnp.where(away == offset, weight, total)
    return total.astype(jnp.bfloat16)


def along_z(values, matrix):
    high = values.astype(jnp.bfloat16)
    low = (values - high.astype(F32)).astype(jnp.bfloat16)
    both = jnp.concatenate([high, low], 1)
    return jnp.dot(both, matrix, preferred_element_type=F32)


def advance_kernel(
    n_stream, n_span, jac, q_hbm, old_ref, out_ref,
    wide, pre, y_near_out, y_near_in, y_far_out, y_far_in,
    load_sem, near_send, near_recv, far_send, far_recv,
):
    i = lax.axis_index("stream")
    j = lax.axis_index("span")
    has = (i > 0, i < n_stream - 1, j > 0, j < n_span - 1)
    ids = ((i - 1, j), (i + 1, j), (i, j - 1), (i, j + 1))

    barrier = pltpu.get_barrier_semaphore()
    for side in range(4):
        @pl.when(has[side])
        def _():
            pl.semaphore_signal(barrier, inc=1, device_id=ids[side], device_id_type=MESH)

    load = pltpu.make_async_copy(q_hbm, wide.at[:, NEAR:NEAR + CX, PAD:PAD + CY, :], load_sem)
    load.start()

    for ref, width in ((wide, NEAR), (pre, FAR)):
        planes = CX + 2 * width

        @pl.when(~has[0])
        def _():
            ref[:, 0:width, :, :] = jnp.zeros((VARS, width, WY, CZ), F32)

        @pl.when(~has[1])
        def _():
            ref[:, width + CX:planes, :, :] = jnp.zeros((VARS, width, WY, CZ), F32)

        @pl.when(~has[2])
        def _():
            ref[:, width:width + CX, 0:PAD, :] = jnp.zeros((VARS, CX, PAD, CZ), F32)

        @pl.when(~has[3])
        def _():
            ref[:, width:width + CX, PAD + CY:WY, :] = jnp.zeros((VARS, CX, PAD, CZ), F32)

    load.wait()

    def flat_rows(ref, width, c, x, y, count):
        planes = CX + 2 * width
        flat = ref.reshape(VARS * planes * WY, CZ)
        return flat, pl.ds((c * planes + width + x) * WY + PAD + y, count, WY)

    def pack_near(side):
        for c in range(VARS):
            for m in range(NEAR):
                for x in range(0, CX, 8):
                    flat, rows = flat_rows(wide, NEAR, c, x, m if side == 2 else CY - NEAR + m, 8)
                    y_near_out[side - 2, c, m, x:x + 8, :] = flat[rows, :]

    def unpack_near(side):
        for c in range(VARS):
            for m in range(NEAR):
                for x in range(0, CX, 8):
                    flat, rows = flat_rows(wide, NEAR, c, x, m - NEAR if side == 2 else CY + m, 8)
                    flat[rows, :] = y_near_in[side - 2, c, m, x:x + 8, :]

    pieces = (((4, 8, 0),), ((0, 4, 0), (12, 4, 4)))

    def pack_far(side, part):
        for c in range(VARS):
            for m in range(FAR):
                for x, count, at in pieces[part]:
                    flat, rows = flat_rows(pre, FAR, c, x, m if side == 2 else CY - FAR + m, count)
                    y_far_out[side - 2, part, c, m, at:at + count, :] = flat[rows, :]

    def unpack_far(side, part):
        for c in range(VARS):
            for m in range(FAR):
                for x, count, at in pieces[part]:
                    flat, rows = flat_rows(pre, FAR, c, x, m - FAR if side == 2 else CY + m, count)
                    flat[rows, :] = y_far_in[side - 2, part, c, m, at:at + count, :]

    def near(side, part):
        if side == 0:
            src = wide.at[:, NEAR:2 * NEAR, PAD:PAD + CY, :]
            dst = wide.at[:, NEAR + CX:2 * NEAR + CX, PAD:PAD + CY, :]
        elif side == 1:
            src = wide.at[:, CX:NEAR + CX, PAD:PAD + CY, :]
            dst = wide.at[:, 0:NEAR, PAD:PAD + CY, :]
        else:
            src = y_near_out.at[side - 2]
            dst = y_near_in.at[3 - side]
        return pltpu.make_async_remote_copy(
            src_ref=src, dst_ref=dst, send_sem=near_send.at[side], recv_sem=near_recv.at[side ^ 1],
            device_id=ids[side], device_id_type=MESH,
        )

    inner = (NEAR, FAR)
    outer = (0, NEAR)
    x_parts = ((inner, (8, 24)), (inner, (0, 8)), (inner, (24, CY)), (outer, (0, CY)))

    def far(side, part):
        if side < 2:
            (low, high), (top, bottom) = x_parts[part]
            if side == 1:
                low, high = CX - high, CX - low
            shift = CX if side == 0 else -CX
            rows = slice(PAD + top, PAD + bottom)
            src = pre.at[:, FAR + low:FAR + high, rows, :]
            dst = pre.at[:, FAR + low + shift:FAR + high + shift, rows, :]
        else:
            src = y_far_out.at[side - 2, part]
            dst = y_far_in.at[3 - side, part]
        return pltpu.make_async_remote_copy(
            src_ref=src, dst_ref=dst, send_sem=far_send.at[side, part], recv_sem=far_recv.at[side ^ 1, part],
            device_id=ids[side], device_id_type=MESH,
        )

    def start(make, side, part=0):
        @pl.when(has[side])
        def _():
            make(side, part).start()

    def finish_recv(make, side, part=0):
        @pl.when(has[side])
        def _():
            make(side ^ 1, part).wait_recv()

    def finish_send(make, side, part=0):
        @pl.when(has[side])
        def _():
            make(side, part).wait_send()

    expected = sum(jnp.where(flag, 1, 0) for flag in has)
    for side in (2, 3):
        pack_near(side)
    pl.semaphore_wait(barrier, expected)
    for side in range(4):
        start(near, side)

    slope = band(((1, 8.0), (-1, -8.0), (2, -1.0), (-2, 1.0)))

    def base_planes(n, carry):
        x = n * BATCH
        q = wide[:, pl.ds(NEAR + x, BATCH), PAD:PAD + CY, :]
        dz = along_z(q.reshape(VARS * BATCH * CY, CZ), slope).reshape(VARS, BATCH, CY, CZ)
        dz = dz * (-1.0 / 36.0)
        for v in range(VARS):
            total = (4.0 * q[v] - old_ref[v, pl.ds(x, BATCH)]) * (1.0 / 3.0)
            for w in range(VARS):
                total = total + jac[50 + 5 * v + w] * dz[w]
            pre[v, pl.ds(FAR + x, BATCH), PAD:PAD + CY, :] = total
        return carry

    lax.fori_loop(0, CX // BATCH, base_planes, 0)

    def rate_tile(x, tile):
        y = PAD + 8 * tile
        dx, dy = [], []
        for w in range(VARS):
            def at(sx, sy):
                return wide[w, NEAR + x + sx, y + sy:y + sy + 8, :]

            dx.append((at(1, 0) - at(-1, 0)) * (-8.0 / 36.0) + (at(2, 0) - at(-2, 0)) * (1.0 / 36.0))
            dy.append((at(0, 1) - at(0, -1)) * (-8.0 / 36.0) + (at(0, 2) - at(0, -2)) * (1.0 / 36.0))
        for v in range(VARS):
            total = pre[v, FAR + x, y:y + 8, :]
            for w in range(VARS):
                total = total + jac[5 * v + w] * dx[w]
                total = total + jac[25 + 5 * v + w] * dy[w]
            pre[v, FAR + x, y:y + 8, :] = total

    def middle_planes(tiles):
        def step(n, carry):
            for x in (NEAR + 2 * n, NEAR + 2 * n + 1):
                for tile in tiles:
                    rate_tile(x, tile)
            return carry

        return step

    pairs = CX // 2 - NEAR
    lax.fori_loop(0, pairs, middle_planes((1, 2)), 0)
    start(far, 0, 0)
    start(far, 1, 0)
    for side in (2, 3):
        finish_recv(near, side)

        @pl.when(has[side])
        def _():
            unpack_near(side)

    lax.fori_loop(0, pairs, middle_planes((0, 3)), 0)
    for part in (1, 2):
        start(far, 0, part)
        start(far, 1, part)
    for side in (2, 3):
        pack_far(side, 0)
        start(far, side, 0)
    for side in (0, 1):
        finish_recv(near, side)

    def outer_plane(n, carry):
        for x in (n, CX - NEAR + n):
            for tile in range(CY // 8):
                rate_tile(x, tile)
        return carry

    lax.fori_loop(0, NEAR, outer_plane, 0)
    start(far, 0, 3)
    start(far, 1, 3)
    for side in (2, 3):
        pack_far(side, 1)
        start(far, side, 1)

    tenth = band(tuple((o, TAPS[abs(o)]) for o in range(-5, 6)))

    def filter_y(x, c, tile):
        y = PAD + 8 * tile

        def at(sy):
            return pre[c, FAR + x, y + sy:y + sy + 8, :]

        total = (TAPS[0] * SCALE) * at(0)
        for m in range(1, 6):
            total = total + (TAPS[m] * SCALE) * (at(m) + at(-m))
        return total

    def first_planes(n, carry):
        x = n * BATCH
        p = pre[:, pl.ds(FAR + x, BATCH), PAD:PAD + CY, :]
        fz = along_z(p.reshape(VARS * BATCH * CY, CZ), tenth).reshape(VARS, BATCH, CY, CZ)
        total = p + SCALE * fz
        for c in range(VARS):
            for b in range(BATCH):
                for tile in range(CY // 8):
                    part = total[c, b, 8 * tile:8 * tile + 8]
                    if tile in (1, 2):
                        part = part + filter_y(x + b, c, tile)
                    out_ref[c, x + b, 8 * tile:8 * tile + 8, :] = part
        return carry

    lax.fori_loop(0, CX // BATCH, first_planes, 0)

    def filter_x(x, carry):
        for c in range(VARS):
            for tile in range(CY // 8):
                y = PAD + 8 * tile

                def at(sx):
                    return pre[c, FAR + x + sx, y:y + 8, :]

                total = out_ref[c, x, 8 * tile:8 * tile + 8, :] + (TAPS[0] * SCALE) * at(0)
                for m in range(1, 6):
                    total = total + (TAPS[m] * SCALE) * (at(m) + at(-m))
                out_ref[c, x, 8 * tile:8 * tile + 8, :] = total
        return carry

    lax.fori_loop(FAR, CX - FAR, filter_x, 0)
    for side in (0, 1):
        for part in range(4):
            finish_recv(far, side, part)
    lax.fori_loop(0, FAR, filter_x, 0)
    lax.fori_loop(CX - FAR, CX, filter_x, 0)
    for side in (2, 3):
        for part in range(2):
            finish_recv(far, side, part)

            @pl.when(has[side])
            def _():
                unpack_far(side, part)

    def edge_plane(x, carry):
        for c in range(VARS):
            for tile in (0, CY // 8 - 1):
                rows = pl.ds(8 * tile, 8)
                out_ref[c, x, rows, :] = out_ref[c, x, rows, :] + filter_y(x, c, tile)
        return carry

    lax.fori_loop(0, CX, edge_plane, 0)
    for side in range(4):
        finish_send(near, side)
        for part in range(4 if side < 2 else 2):
            finish_send(far, side, part)


def per_device(n_stream, n_span, q_now, q_prev, jacobians, fractions, send_blocks, recv_blocks):
    vmem = pl.BlockSpec(memory_space=pltpu.VMEM)
    anywhere = pl.BlockSpec(memory_space=pl.ANY)
    slots = GROUPS * n_span + 1
    width = n_span * SLOT
    sending = send_blocks.reshape(n_stream, 1, width)
    receiving = recv_blocks.reshape(n_stream, 1, width)
    offsets = fractions.reshape(3, n_stream, width)
    limit = 48 * 1024 * 1024
    packed, fresh = pl.pallas_call(
        functools.partial(exchange_kernel, n_stream, n_span),
        name="exchange",
        out_shape=(
            jax.ShapeDtypeStruct((ROWS, CZ), F32),
            jax.ShapeDtypeStruct((slots, BRICK, 128), F32),
        ),
        in_specs=[anywhere] * 4,
        out_specs=(vmem, vmem),
        scratch_shapes=[
            pltpu.SMEM((GROUPS + 1, 1, width), jnp.int32),
            pltpu.VMEM((3, n_stream, width), F32),
            pltpu.VMEM(q_now.shape, F32),
            pltpu.VMEM(q_now.shape, F32),
            pltpu.VMEM((slots, ROW, 128), F32),
            pltpu.VMEM((slots, ROW, 128), F32),
            pltpu.SemaphoreType.DMA((3,)),
            pltpu.SemaphoreType.DMA((2 * PARTS,)),
            pltpu.SemaphoreType.DMA((slots,)),
            pltpu.SemaphoreType.DMA((slots,)),
        ],
        compiler_params=pltpu.CompilerParams(
            collective_id=0, has_side_effects=True, vmem_limit_bytes=48 * 1024 * 1024
        ),
    )(*(pltpu.with_memory_space_constraint(x, pltpu.HBM) for x in (sending, offsets, q_now, q_prev)))
    shape = jax.ShapeDtypeStruct(q_now.shape, F32)
    now, older = pl.pallas_call(
        functools.partial(place_kernel, n_stream, n_span),
        name="place",
        out_shape=(shape, shape),
        in_specs=[anywhere, anywhere, vmem],
        out_specs=(vmem, vmem),
        scratch_shapes=[
            pltpu.SMEM((GROUPS + 1, 1, width), jnp.int32),
            pltpu.VMEM((ROWS, CZ), F32),
            pltpu.SemaphoreType.DMA((3,)),
        ],
        compiler_params=pltpu.CompilerParams(vmem_limit_bytes=limit),
    )(receiving, packed, fresh)
    return pl.pallas_call(
        functools.partial(advance_kernel, n_stream, n_span),
        name="advance",
        out_shape=shape,
        in_specs=[pl.BlockSpec(memory_space=pltpu.SMEM), anywhere, vmem],
        out_specs=vmem,
        scratch_shapes=[
            pltpu.VMEM((VARS, CX + 2 * NEAR, WY, CZ), F32),
            pltpu.VMEM((VARS, CX + 2 * FAR, WY, CZ), F32),
            pltpu.VMEM((2, VARS, NEAR, CX, CZ), F32),
            pltpu.VMEM((2, VARS, NEAR, CX, CZ), F32),
            pltpu.VMEM((2, 2, VARS, FAR, CX // 2, CZ), F32),
            pltpu.VMEM((2, 2, VARS, FAR, CX // 2, CZ), F32),
            pltpu.SemaphoreType.DMA,
            pltpu.SemaphoreType.DMA((4,)),
            pltpu.SemaphoreType.DMA((4,)),
            pltpu.SemaphoreType.DMA((4, 4)),
            pltpu.SemaphoreType.DMA((4, 4)),
        ],
        compiler_params=pltpu.CompilerParams(
            collective_id=1, has_side_effects=True, vmem_limit_bytes=limit
        ),
    )(jacobians.reshape(-1), now, older)


def solution(mesh):
    in_specs = (
        P(None, "stream", "span", None),
        P(None, "stream", "span", None),
        P(),
        P(None, ("stream", "span"), None),
        P(("stream", "span"), None),
        P(("stream", "span"), None),
    )
    out_specs = P(None, "stream", "span", None)
    body = functools.partial(per_device, mesh.shape["stream"], mesh.shape["span"])
    return jax.shard_map(
        body, mesh=mesh, in_specs=in_specs, out_specs=out_specs, check_vma=False
    )
```

```python
import functools

import jax
import jax.numpy as jnp
from jax import lax
from jax.experimental import pallas as pl
from jax.experimental.pallas import tpu as pltpu
from jax.sharding import PartitionSpec as P

MESH = pl.DeviceIdType.MESH
F32 = jnp.float32
VARS = 5
CHANS = 10
SLOT = 32
REACH = 2
PARTS = 4
EARLY = 2
BATCH = 4
GROUPS = 2 * REACH + 1
CX, CY, CZ = 16, 32, 128
BX, BY = CX // 2, CY // 2
ROW = 2 * CHANS
BRICK = 2 * ROW
ROWS = BX * CY * ROW
PAD = 8
WY = CY + 2 * PAD
NEAR, FAR = 2, 5
SCALE = 0.6 / 1024.0
TAPS = (-252.0, 210.0, -120.0, 45.0, -10.0, 1.0)


def lanes(shape):
    return lax.broadcasted_iota(jnp.int32, shape, len(shape) - 1)


def window_start(i, n_stream):
    return jnp.minimum(jnp.maximum(i - REACH, 0), n_stream - GROUPS)


def exchange_kernel(
    n_stream, n_span, send_hbm, frac_hbm, now_hbm, prev_hbm, packed_ref, fresh_ref,
    picks, frac_ref, now_ref, prev_ref, sending, arrived, pick_sem, load_sem, send_sem, recv_sem,
):
    i = lax.axis_index("stream")
    j = lax.axis_index("span")
    first = window_start(i, n_stream)
    far = lax.rem(i + n_stream // 2, n_stream)
    near_count = GROUPS * n_span
    far_slot = near_count

    def is_partner(g, jp):
        t = first + g
        return (t >= i - REACH) & (t <= i + REACH) & ((t != i) | (jp != j))

    loads = [
        pltpu.make_async_copy(
            src.at[:, pl.ds(part * CX // PARTS, CX // PARTS)],
            dst.at[:, pl.ds(part * CX // PARTS, CX // PARTS)],
            load_sem.at[2 * part + n],
        )
        for part in range(PARTS)
        for n, (src, dst) in enumerate(((now_hbm, now_ref), (prev_hbm, prev_ref)))
    ]
    others = [
        pltpu.make_async_copy(
            send_hbm.at[pl.ds(first, GROUPS)], picks.at[pl.ds(0, GROUPS)], pick_sem.at[0]
        ),
        pltpu.make_async_copy(
            send_hbm.at[pl.ds(far, 1)], picks.at[pl.ds(GROUPS, 1)], pick_sem.at[1]
        ),
        pltpu.make_async_copy(frac_hbm, frac_ref, pick_sem.at[2]),
    ]
    for copy in loads + others:
        copy.start()

    barrier = pltpu.get_barrier_semaphore()
    for g in range(GROUPS):
        for jp in range(n_span):
            @pl.when(is_partner(g, jp))
            def _():
                pl.semaphore_signal(barrier, inc=1, device_id=(first + g, jp), device_id_type=MESH)
    pl.semaphore_signal(barrier, inc=1, device_id=(far, j), device_id_type=MESH)

    def relayout(xb, carry):
        for dx in range(2):
            for tile in range(CY // 8):
                base = xb * (CY * ROW) + tile * 8 * ROW + dx * CHANS
                for c in range(VARS):
                    packed_ref[pl.ds(base + c, 8, ROW), :] = now_ref[c, 2 * xb + dx, tile * 8:tile * 8 + 8, :]
                    packed_ref[pl.ds(base + VARS + c, 8, ROW), :] = prev_ref[c, 2 * xb + dx, tile * 8:tile * 8 + 8, :]
        return carry

    for part in range(PARTS):
        loads[2 * part].wait()
        loads[2 * part + 1].wait()
        lax.fori_loop(part * BX // PARTS, (part + 1) * BX // PARTS, relayout, 0)
    for copy in others:
        copy.wait()

    half = lanes((ROW, 128)) < 64
    pair = lanes((BRICK, 128)) // 2

    def pack(p, row, start):
        total = jnp.zeros((BRICK, 128), F32)
        for k in range(SLOT):
            brick = jnp.maximum(picks[row, 0, start + k], 0)
            moved = pltpu.roll(
                packed_ref[pl.ds((brick >> 6) * BRICK, BRICK), :], (2 * k - 2 * (brick & 63)) & 127, 1
            )
            total = jnp.where(pair == k, moved, total)
        sending[p] = jnp.where(half, total[:ROW], pltpu.roll(total[ROW:], 64, 1))

    def far_copy():
        return pltpu.make_async_remote_copy(
            src_ref=sending.at[far_slot], dst_ref=arrived.at[far_slot],
            send_sem=send_sem.at[far_slot], recv_sem=recv_sem.at[far_slot],
            device_id=(far, j), device_id_type=MESH,
        )

    def near_copy(p, g, jp):
        t = first + g
        slot = (i - window_start(t, n_stream)) * n_span + j
        slot = jnp.minimum(jnp.maximum(slot, 0), near_count - 1)
        return pltpu.make_async_remote_copy(
            src_ref=sending.at[p], dst_ref=arrived.at[slot],
            send_sem=send_sem.at[p], recv_sem=recv_sem.at[slot],
            device_id=(t, jp), device_id_type=MESH,
        )

    def arrival(p):
        return pltpu.make_async_remote_copy(
            src_ref=sending.at[p], dst_ref=arrived.at[p],
            send_sem=send_sem.at[p], recv_sem=recv_sem.at[p],
            device_id=(first + p // n_span, lax.rem(p, n_span)), device_id_type=MESH,
        )

    def start_near(g, jp):
        @pl.when(is_partner(g, jp))
        def _():
            near_copy(g * n_span + jp, g, jp).start()

    rows_near = jnp.minimum(i + REACH, n_stream - 1) - jnp.maximum(i - REACH, 0) + 1

    def column(n):
        return lax.rem(j + jnp.where(n == 0, 2, jnp.where(n == 1, 1, jnp.where(n == 2, 3, 0))), n_span)

    def send(n, carry):
        jp = column(n)
        for g in range(GROUPS):
            pack(g * n_span + jp, g, jp * SLOT)

        @pl.when(n == 0)
        def _():
            pack(far_slot, GROUPS, j * SLOT)

        @pl.when(n == EARLY - 1)
        def _():
            pl.semaphore_wait(barrier, rows_near * n_span)
            for early in range(EARLY):
                for g in (0, 4, 1, 3, 2):
                    start_near(g, column(early))
                if early == 0:
                    far_copy().start()

        @pl.when(n >= EARLY)
        def _():
            for g in (0, 4, 1, 3, 2):
                start_near(g, jp)

        return carry

    lax.fori_loop(0, n_span, send, 0)
    own = (i - first) * n_span + j
    arrived[own] = sending[own]

    near_frac = [frac_ref[d, pl.ds(first, GROUPS), :] for d in range(3)]
    far_frac = [frac_ref[d, pl.ds(far, 1), :] for d in range(3)]
    table = jnp.concatenate([part for d in range(3) for part in (near_frac[d], far_frac[d])], 0)

    def spread(which):
        source = lax.broadcasted_iota(jnp.int32, (128, 128), 0)
        wanted = which * SLOT + lax.rem(lanes((128, 128)), 64) // 2
        chosen = jnp.where(source == wanted, 1.0, 0.0).astype(F32)
        return jnp.dot(table, chosen, precision=lax.Precision.HIGHEST, preferred_element_type=F32)

    even = lanes((CHANS, 128)) % 2 == 0
    low_half = lanes((CHANS, 128)) < 64

    def finish(p, fx, fy, fz):
        block = arrived[p]
        upper = block[CHANS:]
        lower = (1.0 - fx) * block[:CHANS] + fx * upper
        done = []
        for v in (lower, upper):
            v = jnp.where(low_half, (1.0 - fy) * v + fy * pltpu.roll(v, 64, 1), v)
            v = jnp.where(even, (1.0 - fz) * v + fz * pltpu.roll(v, 127, 1), v)
            done.append(v)
        both = jnp.concatenate(done, 0)
        fresh_ref[p, 0:ROW, :] = both
        fresh_ref[p, ROW:BRICK, :] = pltpu.roll(both, 64, 1)

    for n in range(n_span):
        jp = column(n)
        shares = spread(jp)
        if n == 1:
            far_shares = spread(j)
            far_copy().wait_recv()
            finish(far_slot, *(far_shares[6 * d + GROUPS:6 * d + GROUPS + 1] for d in range(3)))
        for g in range(GROUPS):
            @pl.when(is_partner(g, jp))
            def _():
                arrival(g * n_span + jp).wait_recv()
        for g in range(GROUPS):
            finish(g * n_span + jp, *(shares[6 * d + g:6 * d + g + 1] for d in range(3)))
    for p in range(near_count):
        @pl.when(is_partner(p // n_span, p % n_span))
        def _():
            arrival(p).wait_send()

    far_copy().wait_send()


def place_kernel(n_stream, n_span, recv_hbm, packed_hbm, fresh_ref, now_ref, prev_ref, targets, work, sem):
    i = lax.axis_index("stream")
    j = lax.axis_index("span")
    first = window_start(i, n_stream)
    far = lax.rem(i + n_stream // 2, n_stream)
    near_count = GROUPS * n_span
    copies = [
        pltpu.make_async_copy(recv_hbm.at[pl.ds(first, GROUPS)], targets.at[pl.ds(0, GROUPS)], sem.at[0]),
        pltpu.make_async_copy(recv_hbm.at[pl.ds(far, 1)], targets.at[pl.ds(GROUPS, 1)], sem.at[1]),
        pltpu.make_async_copy(packed_hbm, work, sem.at[2]),
    ]
    for copy in copies:
        copy.start()
    for copy in copies:
        copy.wait()
    pair = lanes((BRICK, 128)) // 2

    def put(p, row, start):
        block = fresh_ref[p]
        for k in range(SLOT):
            target = targets[row, 0, start + k]
            brick = jnp.maximum(target, 0)
            column = brick & 63
            moved = pltpu.roll(block, (2 * column - 2 * k) & 127, 1)
            mark = jnp.where(target >= 0, column, -1)
            base = pl.multiple_of((brick >> 6) * BRICK, 8)
            pltpu.store(work.at[pl.ds(base, BRICK), :], moved, mask=pair == mark)

    def put_group(g, carry):
        for jp in range(n_span):
            put(g * n_span + jp, g, jp * SLOT)
        return carry

    lax.fori_loop(0, GROUPS, put_group, 0)
    put(near_count, GROUPS, j * SLOT)

    def relayout(xb, carry):
        for dx in range(2):
            for tile in range(CY // 8):
                base = xb * (CY * ROW) + tile * 8 * ROW + dx * CHANS
                for c in range(VARS):
                    now_ref[c, 2 * xb + dx, tile * 8:tile * 8 + 8, :] = work[pl.ds(base + c, 8, ROW), :]
                    prev_ref[c, 2 * xb + dx, tile * 8:tile * 8 + 8, :] = work[pl.ds(base + VARS + c, 8, ROW), :]
        return carry

    lax.fori_loop(0, BX, relayout, 0)


def band(entries):
    source = lax.rem(lax.broadcasted_iota(jnp.int32, (2 * CZ, CZ), 0), CZ)
    away = source - lanes((2 * CZ, CZ))
    total = jnp.zeros((2 * CZ, CZ), F32)
    for offset, weight in entries:
        total = jnp.where(away == offset, weight, total)
    return total.astype(jnp.bfloat16)


def along_z(values, matrix):
    high = values.astype(jnp.bfloat16)
    low = (values - high.astype(F32)).astype(jnp.bfloat16)
    both = jnp.concatenate([high, low], 1)
    return jnp.dot(both, matrix, preferred_element_type=F32)


def advance_kernel(
    n_stream, n_span, jac, q_hbm, old_ref, out_ref,
    wide, pre, y_near_out, y_near_in, y_far_out, y_far_in,
    load_sem, near_send, near_recv, far_send, far_recv,
):
    i = lax.axis_index("stream")
    j = lax.axis_index("span")
    has = (i > 0, i < n_stream - 1, j > 0, j < n_span - 1)
    ids = ((i - 1, j), (i + 1, j), (i, j - 1), (i, j + 1))

    barrier = pltpu.get_barrier_semaphore()
    for side in range(4):
        @pl.when(has[side])
        def _():
            pl.semaphore_signal(barrier, inc=1, device_id=ids[side], device_id_type=MESH)

    load = pltpu.make_async_copy(q_hbm, wide.at[:, NEAR:NEAR + CX, PAD:PAD + CY, :], load_sem)
    load.start()

    for ref, width in ((wide, NEAR), (pre, FAR)):
        planes = CX + 2 * width

        @pl.when(~has[0])
        def _():
            ref[:, 0:width, :, :] = jnp.zeros((VARS, width, WY, CZ), F32)

        @pl.when(~has[1])
        def _():
            ref[:, width + CX:planes, :, :] = jnp.zeros((VARS, width, WY, CZ), F32)

    @pl.when(~has[2])
    def _():
        wide[:, NEAR:NEAR + CX, 0:PAD, :] = jnp.zeros((VARS, CX, PAD, CZ), F32)

    @pl.when(~has[3])
    def _():
        wide[:, NEAR:NEAR + CX, PAD + CY:WY, :] = jnp.zeros((VARS, CX, PAD, CZ), F32)

    for edge in (0, PAD + CY):
        pre[:, FAR:FAR + CX, edge:edge + PAD, :] = jnp.zeros((VARS, CX, PAD, CZ), F32)

    load.wait()

    def flat_rows(ref, width, c, x, y, count):
        planes = CX + 2 * width
        flat = ref.reshape(VARS * planes * WY, CZ)
        return flat, pl.ds((c * planes + width + x) * WY + PAD + y, count, WY)

    def pack_near(side):
        for c in range(VARS):
            for m in range(NEAR):
                for x in range(0, CX, 8):
                    flat, rows = flat_rows(wide, NEAR, c, x, m if side == 2 else CY - NEAR + m, 8)
                    y_near_out[side - 2, c, m, x:x + 8, :] = flat[rows, :]

    def unpack_near(side):
        for c in range(VARS):
            for m in range(NEAR):
                for x in range(0, CX, 8):
                    flat, rows = flat_rows(wide, NEAR, c, x, m - NEAR if side == 2 else CY + m, 8)
                    flat[rows, :] = y_near_in[side - 2, c, m, x:x + 8, :]

    pieces = (((4, 8, 0),), ((0, 4, 0), (12, 4, 4)))

    def pack_far(side, part):
        for c in range(VARS):
            for m in range(FAR):
                for x, count, at in pieces[part]:
                    flat, rows = flat_rows(pre, FAR, c, x, m if side == 2 else CY - FAR + m, count)
                    y_far_out[side - 2, part, c, m, at:at + count, :] = flat[rows, :]

    out_rows = out_ref.reshape(VARS * CX * CY, CZ)

    def add_far_y(side, part):
        for c in range(VARS):
            held = [y_far_in[side - 2, part, c, m] for m in range(FAR)]
            for r in range(FAR):
                total = None
                for m in range(r, FAR) if side == 2 else range(r + 1):
                    away = r + FAR - m if side == 2 else FAR + m - r
                    term = (TAPS[away] * SCALE) * held[m]
                    total = term if total is None else total + term
                row = r if side == 2 else CY - FAR + r
                for x, count, at in pieces[part]:
                    rows = pl.ds((c * CX + x) * CY + row, count, CY)
                    out_rows[rows, :] = out_rows[rows, :] + total[at:at + count]

    def add_far_x(side):
        def step(c, carry):
            for tile in range(CY // 8):
                y = PAD + 8 * tile
                first_plane = 0 if side == 0 else FAR + CX
                held = [pre[c, first_plane + m, y:y + 8, :] for m in range(FAR)]
                for r in range(FAR):
                    total = None
                    for m in range(r, FAR) if side == 0 else range(r + 1):
                        away = r + FAR - m if side == 0 else FAR + m - r
                        term = (TAPS[away] * SCALE) * held[m]
                        total = term if total is None else total + term
                    x = r if side == 0 else CX - FAR + r
                    out_ref[c, x, 8 * tile:8 * tile + 8, :] = out_ref[c, x, 8 * tile:8 * tile + 8, :] + total
            return carry

        return step

    def near(side, part):
        if side == 0:
            src = wide.at[:, NEAR:2 * NEAR, PAD:PAD + CY, :]
            dst = wide.at[:, NEAR + CX:2 * NEAR + CX, PAD:PAD + CY, :]
        elif side == 1:
            src = wide.at[:, CX:NEAR + CX, PAD:PAD + CY, :]
            dst = wide.at[:, 0:NEAR, PAD:PAD + CY, :]
        else:
            src = y_near_out.at[side - 2]
            dst = y_near_in.at[3 - side]
        return pltpu.make_async_remote_copy(
            src_ref=src, dst_ref=dst, send_sem=near_send.at[side], recv_sem=near_recv.at[side ^ 1],
            device_id=ids[side], device_id_type=MESH,
        )

    inner = (NEAR, FAR)
    outer = (0, NEAR)
    x_parts = ((inner, (8, 24)), (inner, (0, 8)), (inner, (24, CY)), (outer, (0, CY)))

    def far(side, part):
        if side < 2:
            (low, high), (top, bottom) = x_parts[part]
            if side == 1:
                low, high = CX - high, CX - low
            shift = CX if side == 0 else -CX
            rows = slice(PAD + top, PAD + bottom)
            src = pre.at[:, FAR + low:FAR + high, rows, :]
            dst = pre.at[:, FAR + low + shift:FAR + high + shift, rows, :]
        else:
            src = y_far_out.at[side - 2, part]
            dst = y_far_in.at[3 - side, part]
        return pltpu.make_async_remote_copy(
            src_ref=src, dst_ref=dst, send_sem=far_send.at[side, part], recv_sem=far_recv.at[side ^ 1, part],
            device_id=ids[side], device_id_type=MESH,
        )

    def start(make, side, part=0):
        @pl.when(has[side])
        def _():
            make(side, part).start()

    def finish_recv(make, side, part=0):
        @pl.when(has[side])
        def _():
            make(side ^ 1, part).wait_recv()

    def finish_send(make, side, part=0):
        @pl.when(has[side])
        def _():
            make(side, part).wait_send()

    expected = sum(jnp.where(flag, 1, 0) for flag in has)
    for side in (2, 3):
        pack_near(side)
    pl.semaphore_wait(barrier, expected)
    for side in range(4):
        start(near, side)

    slope = band(((1, 8.0), (-1, -8.0), (2, -1.0), (-2, 1.0)))

    def base_planes(n, carry):
        x = n * BATCH
        q = wide[:, pl.ds(NEAR + x, BATCH), PAD:PAD + CY, :]
        dz = along_z(q.reshape(VARS * BATCH * CY, CZ), slope).reshape(VARS, BATCH, CY, CZ)
        dz = dz * (-1.0 / 36.0)
        for v in range(VARS):
            total = (4.0 * q[v] - old_ref[v, pl.ds(x, BATCH)]) * (1.0 / 3.0)
            for w in range(VARS):
                total = total + jac[50 + 5 * v + w] * dz[w]
            pre[v, pl.ds(FAR + x, BATCH), PAD:PAD + CY, :] = total
        return carry

    lax.fori_loop(0, CX // BATCH, base_planes, 0)

    def rate_tile(x, tile):
        y = PAD + 8 * tile
        dx, dy = [], []
        for w in range(VARS):
            def at(sx, sy):
                return wide[w, NEAR + x + sx, y + sy:y + sy + 8, :]

            dx.append((at(1, 0) - at(-1, 0)) * (-8.0 / 36.0) + (at(2, 0) - at(-2, 0)) * (1.0 / 36.0))
            dy.append((at(0, 1) - at(0, -1)) * (-8.0 / 36.0) + (at(0, 2) - at(0, -2)) * (1.0 / 36.0))
        for v in range(VARS):
            total = pre[v, FAR + x, y:y + 8, :]
            for w in range(VARS):
                total = total + jac[5 * v + w] * dx[w]
                total = total + jac[25 + 5 * v + w] * dy[w]
            pre[v, FAR + x, y:y + 8, :] = total

    def middle_planes(tiles):
        def step(n, carry):
            for x in (NEAR + 2 * n, NEAR + 2 * n + 1):
                for tile in tiles:
                    rate_tile(x, tile)
            return carry

        return step

    pairs = CX // 2 - NEAR
    lax.fori_loop(0, pairs, middle_planes((1, 2)), 0)
    start(far, 0, 0)
    start(far, 1, 0)
    for side in (2, 3):
        finish_recv(near, side)

        @pl.when(has[side])
        def _():
            unpack_near(side)

    lax.fori_loop(0, pairs, middle_planes((0, 3)), 0)
    for part in (1, 2):
        start(far, 0, part)
        start(far, 1, part)
    for side in (2, 3):
        pack_far(side, 0)
        start(far, side, 0)
    for side in (0, 1):
        finish_recv(near, side)

    def outer_plane(n, carry):
        for x in (n, CX - NEAR + n):
            for tile in range(CY // 8):
                rate_tile(x, tile)
        return carry

    lax.fori_loop(0, NEAR, outer_plane, 0)
    start(far, 0, 3)
    start(far, 1, 3)
    for side in (2, 3):
        pack_far(side, 1)
        start(far, side, 1)

    tenth = band(tuple((o, TAPS[abs(o)]) for o in range(-5, 6)))

    def filter_y(x, c, tile):
        y = PAD + 8 * tile

        def at(sy):
            return pre[c, FAR + x, y + sy:y + sy + 8, :]

        total = (TAPS[0] * SCALE) * at(0)
        for m in range(1, 6):
            total = total + (TAPS[m] * SCALE) * (at(m) + at(-m))
        return total

    def first_planes(n, carry):
        x = n * BATCH
        p = pre[:, pl.ds(FAR + x, BATCH), PAD:PAD + CY, :]
        fz = along_z(p.reshape(VARS * BATCH * CY, CZ), tenth).reshape(VARS, BATCH, CY, CZ)
        total = p + SCALE * fz
        for c in range(VARS):
            for b in range(BATCH):
                for tile in range(CY // 8):
                    part = total[c, b, 8 * tile:8 * tile + 8] + filter_y(x + b, c, tile)
                    out_ref[c, x + b, 8 * tile:8 * tile + 8, :] = part
        return carry

    lax.fori_loop(0, CX // BATCH, first_planes, 0)

    def filter_x(c, carry):
        for tile in range(CY // 8):
            y = PAD + 8 * tile
            line = [pre[c, FAR + x, y:y + 8, :] for x in range(CX)]
            for x in range(CX):
                total = out_ref[c, x, 8 * tile:8 * tile + 8, :] + (TAPS[0] * SCALE) * line[x]
                for m in range(1, 6):
                    near_by = [line[x + o] for o in (m, -m) if 0 <= x + o < CX]
                    total = total + (TAPS[m] * SCALE) * sum(near_by[1:], near_by[0])
                out_ref[c, x, 8 * tile:8 * tile + 8, :] = total
        return carry

    lax.fori_loop(0, VARS, filter_x, 0)

    def receive_far_y(part):
        for side in (2, 3):
            finish_recv(far, side, part)

            @pl.when(has[side])
            def _():
                add_far_y(side, part)

    receive_far_y(0)
    for side in (0, 1):
        for part in range(4):
            finish_recv(far, side, part)
        lax.fori_loop(0, VARS, add_far_x(side), 0)
    receive_far_y(1)
    for side in range(4):
        finish_send(near, side)
        for part in range(4 if side < 2 else 2):
            finish_send(far, side, part)


def per_device(n_stream, n_span, q_now, q_prev, jacobians, fractions, send_blocks, recv_blocks):
    vmem = pl.BlockSpec(memory_space=pltpu.VMEM)
    anywhere = pl.BlockSpec(memory_space=pl.ANY)
    slots = GROUPS * n_span + 1
    width = n_span * SLOT
    sending = send_blocks.reshape(n_stream, 1, width)
    receiving = recv_blocks.reshape(n_stream, 1, width)
    offsets = fractions.reshape(3, n_stream, width)
    limit = 48 * 1024 * 1024
    packed, fresh = pl.pallas_call(
        functools.partial(exchange_kernel, n_stream, n_span),
        name="exchange",
        out_shape=(
            jax.ShapeDtypeStruct((ROWS, CZ), F32),
            jax.ShapeDtypeStruct((slots, BRICK, 128), F32),
        ),
        in_specs=[anywhere] * 4,
        out_specs=(vmem, vmem),
        scratch_shapes=[
            pltpu.SMEM((GROUPS + 1, 1, width), jnp.int32),
            pltpu.VMEM((3, n_stream, width), F32),
            pltpu.VMEM(q_now.shape, F32),
            pltpu.VMEM(q_now.shape, F32),
            pltpu.VMEM((slots, ROW, 128), F32),
            pltpu.VMEM((slots, ROW, 128), F32),
            pltpu.SemaphoreType.DMA((3,)),
            pltpu.SemaphoreType.DMA((2 * PARTS,)),
            pltpu.SemaphoreType.DMA((slots,)),
            pltpu.SemaphoreType.DMA((slots,)),
        ],
        compiler_params=pltpu.CompilerParams(
            collective_id=0, has_side_effects=True, vmem_limit_bytes=48 * 1024 * 1024
        ),
    )(*(pltpu.with_memory_space_constraint(x, pltpu.HBM) for x in (sending, offsets, q_now, q_prev)))
    shape = jax.ShapeDtypeStruct(q_now.shape, F32)
    now, older = pl.pallas_call(
        functools.partial(place_kernel, n_stream, n_span),
        name="place",
        out_shape=(shape, shape),
        in_specs=[anywhere, anywhere, vmem],
        out_specs=(vmem, vmem),
        scratch_shapes=[
            pltpu.SMEM((GROUPS + 1, 1, width), jnp.int32),
            pltpu.VMEM((ROWS, CZ), F32),
            pltpu.SemaphoreType.DMA((3,)),
        ],
        compiler_params=pltpu.CompilerParams(vmem_limit_bytes=limit),
    )(receiving, packed, fresh)
    return pl.pallas_call(
        functools.partial(advance_kernel, n_stream, n_span),
        name="advance",
        out_shape=shape,
        in_specs=[pl.BlockSpec(memory_space=pltpu.SMEM), anywhere, vmem],
        out_specs=vmem,
        scratch_shapes=[
            pltpu.VMEM((VARS, CX + 2 * NEAR, WY, CZ), F32),
            pltpu.VMEM((VARS, CX + 2 * FAR, WY, CZ), F32),
            pltpu.VMEM((2, VARS, NEAR, CX, CZ), F32),
            pltpu.VMEM((2, VARS, NEAR, CX, CZ), F32),
            pltpu.VMEM((2, 2, VARS, FAR, CX // 2, CZ), F32),
            pltpu.VMEM((2, 2, VARS, FAR, CX // 2, CZ), F32),
            pltpu.SemaphoreType.DMA,
            pltpu.SemaphoreType.DMA((4,)),
            pltpu.SemaphoreType.DMA((4,)),
            pltpu.SemaphoreType.DMA((4, 4)),
            pltpu.SemaphoreType.DMA((4, 4)),
        ],
        compiler_params=pltpu.CompilerParams(
            collective_id=1, has_side_effects=True, vmem_limit_bytes=limit
        ),
    )(jacobians.reshape(-1), now, older)


def solution(mesh):
    in_specs = (
        P(None, "stream", "span", None),
        P(None, "stream", "span", None),
        P(),
        P(None, ("stream", "span"), None),
        P(("stream", "span"), None),
        P(("stream", "span"), None),
    )
    out_specs = P(None, "stream", "span", None)
    body = functools.partial(per_device, mesh.shape["stream"], mesh.shape["span"])
    return jax.shard_map(
        body, mesh=mesh, in_specs=in_specs, out_specs=out_specs, check_vma=False
    )
```

```python
import functools

import jax
import jax.numpy as jnp
from jax import lax
from jax.experimental import pallas as pl
from jax.experimental.pallas import tpu as pltpu
from jax.sharding import PartitionSpec as P

MESH = pl.DeviceIdType.MESH
F32 = jnp.float32
VARS = 5
CHANS = 10
SLOT = 32
REACH = 2
PARTS = 4
EARLY = 2
BATCH = 4
GROUPS = 2 * REACH + 1
CX, CY, CZ = 16, 32, 128
BX, BY = CX // 2, CY // 2
ROW = 2 * CHANS
BRICK = 2 * ROW
ROWS = BX * CY * ROW
PAD = 8
WY = CY + 2 * PAD
NEAR, FAR = 2, 5
SCALE = 0.6 / 1024.0
TAPS = (-252.0, 210.0, -120.0, 45.0, -10.0, 1.0)


def lanes(shape):
    return lax.broadcasted_iota(jnp.int32, shape, len(shape) - 1)


def window_start(i, n_stream):
    return jnp.minimum(jnp.maximum(i - REACH, 0), n_stream - GROUPS)


def exchange_kernel(
    n_stream, n_span, send_hbm, frac_hbm, now_hbm, prev_hbm, packed_ref, fresh_ref,
    picks, frac_ref, now_ref, prev_ref, sending, arrived, pick_sem, load_sem, send_sem, recv_sem,
):
    i = lax.axis_index("stream")
    j = lax.axis_index("span")
    first = window_start(i, n_stream)
    far = lax.rem(i + n_stream // 2, n_stream)
    near_count = GROUPS * n_span
    far_slot = near_count

    def is_partner(g, jp):
        t = first + g
        return (t >= i - REACH) & (t <= i + REACH) & ((t != i) | (jp != j))

    loads = [
        pltpu.make_async_copy(
            src.at[:, pl.ds(part * CX // PARTS, CX // PARTS)],
            dst.at[:, pl.ds(part * CX // PARTS, CX // PARTS)],
            load_sem.at[2 * part + n],
        )
        for part in range(PARTS)
        for n, (src, dst) in enumerate(((now_hbm, now_ref), (prev_hbm, prev_ref)))
    ]
    others = [
        pltpu.make_async_copy(
            send_hbm.at[pl.ds(first, GROUPS)], picks.at[pl.ds(0, GROUPS)], pick_sem.at[0]
        ),
        pltpu.make_async_copy(
            send_hbm.at[pl.ds(far, 1)], picks.at[pl.ds(GROUPS, 1)], pick_sem.at[1]
        ),
        pltpu.make_async_copy(frac_hbm, frac_ref, pick_sem.at[2]),
    ]
    for copy in loads + others:
        copy.start()

    barrier = pltpu.get_barrier_semaphore()
    for g in range(GROUPS):
        for jp in range(n_span):
            @pl.when(is_partner(g, jp))
            def _():
                pl.semaphore_signal(barrier, inc=1, device_id=(first + g, jp), device_id_type=MESH)
    pl.semaphore_signal(barrier, inc=1, device_id=(far, j), device_id_type=MESH)

    def relayout(xb, carry):
        for dx in range(2):
            for tile in range(CY // 8):
                base = xb * (CY * ROW) + tile * 8 * ROW + dx * CHANS
                for c in range(VARS):
                    packed_ref[pl.ds(base + c, 8, ROW), :] = now_ref[c, 2 * xb + dx, tile * 8:tile * 8 + 8, :]
                    packed_ref[pl.ds(base + VARS + c, 8, ROW), :] = prev_ref[c, 2 * xb + dx, tile * 8:tile * 8 + 8, :]
        return carry

    for part in range(PARTS):
        loads[2 * part].wait()
        loads[2 * part + 1].wait()
        lax.fori_loop(part * BX // PARTS, (part + 1) * BX // PARTS, relayout, 0)
    for copy in others:
        copy.wait()

    half = lanes((ROW, 128)) < 64
    pair = lanes((BRICK, 128)) // 2

    def pack(p, row, start):
        total = jnp.zeros((BRICK, 128), F32)
        for k in range(SLOT):
            brick = jnp.maximum(picks[row, 0, start + k], 0)
            moved = pltpu.roll(
                packed_ref[pl.ds((brick >> 6) * BRICK, BRICK), :], (2 * k - 2 * (brick & 63)) & 127, 1
            )
            total = jnp.where(pair == k, moved, total)
        sending[p] = jnp.where(half, total[:ROW], pltpu.roll(total[ROW:], 64, 1))

    def far_copy():
        return pltpu.make_async_remote_copy(
            src_ref=sending.at[far_slot], dst_ref=arrived.at[far_slot],
            send_sem=send_sem.at[far_slot], recv_sem=recv_sem.at[far_slot],
            device_id=(far, j), device_id_type=MESH,
        )

    def near_copy(p, g, jp):
        t = first + g
        slot = (i - window_start(t, n_stream)) * n_span + j
        slot = jnp.minimum(jnp.maximum(slot, 0), near_count - 1)
        return pltpu.make_async_remote_copy(
            src_ref=sending.at[p], dst_ref=arrived.at[slot],
            send_sem=send_sem.at[p], recv_sem=recv_sem.at[slot],
            device_id=(t, jp), device_id_type=MESH,
        )

    def arrival(p):
        return pltpu.make_async_remote_copy(
            src_ref=sending.at[p], dst_ref=arrived.at[p],
            send_sem=send_sem.at[p], recv_sem=recv_sem.at[p],
            device_id=(first + p // n_span, lax.rem(p, n_span)), device_id_type=MESH,
        )

    def start_near(g, jp):
        @pl.when(is_partner(g, jp))
        def _():
            near_copy(g * n_span + jp, g, jp).start()

    rows_near = jnp.minimum(i + REACH, n_stream - 1) - jnp.maximum(i - REACH, 0) + 1

    def column(n):
        return lax.rem(j + jnp.where(n == 0, 2, jnp.where(n == 1, 1, jnp.where(n == 2, 3, 0))), n_span)

    def send(n, carry):
        jp = column(n)
        for g in range(GROUPS):
            pack(g * n_span + jp, g, jp * SLOT)

        @pl.when(n == 0)
        def _():
            pack(far_slot, GROUPS, j * SLOT)

        @pl.when(n == EARLY - 1)
        def _():
            pl.semaphore_wait(barrier, rows_near * n_span)
            for early in range(EARLY):
                for g in (0, 4, 1, 3, 2):
                    start_near(g, column(early))
                if early == 0:
                    far_copy().start()

        @pl.when(n >= EARLY)
        def _():
            for g in (0, 4, 1, 3, 2):
                start_near(g, jp)

        return carry

    lax.fori_loop(0, n_span, send, 0)
    own = (i - first) * n_span + j
    arrived[own] = sending[own]

    near_frac = [frac_ref[d, pl.ds(first, GROUPS), :] for d in range(3)]
    far_frac = [frac_ref[d, pl.ds(far, 1), :] for d in range(3)]
    table = jnp.concatenate([part for d in range(3) for part in (near_frac[d], far_frac[d])], 0)

    def spread(which):
        source = lax.broadcasted_iota(jnp.int32, (128, 128), 0)
        wanted = which * SLOT + lax.rem(lanes((128, 128)), 64) // 2
        chosen = jnp.where(source == wanted, 1.0, 0.0).astype(F32)
        return jnp.dot(table, chosen, precision=lax.Precision.HIGHEST, preferred_element_type=F32)

    even = lanes((CHANS, 128)) % 2 == 0
    low_half = lanes((CHANS, 128)) < 64

    def finish(p, fx, fy, fz):
        block = arrived[p]
        upper = block[CHANS:]
        lower = (1.0 - fx) * block[:CHANS] + fx * upper
        done = []
        for v in (lower, upper):
            v = jnp.where(low_half, (1.0 - fy) * v + fy * pltpu.roll(v, 64, 1), v)
            v = jnp.where(even, (1.0 - fz) * v + fz * pltpu.roll(v, 127, 1), v)
            done.append(v)
        both = jnp.concatenate(done, 0)
        fresh_ref[p, 0:ROW, :] = both
        fresh_ref[p, ROW:BRICK, :] = pltpu.roll(both, 64, 1)

    for n in range(n_span):
        jp = column(n)
        shares = spread(jp)
        if n == 1:
            far_shares = spread(j)
            far_copy().wait_recv()
            finish(far_slot, *(far_shares[6 * d + GROUPS:6 * d + GROUPS + 1] for d in range(3)))
        for g in range(GROUPS):
            @pl.when(is_partner(g, jp))
            def _():
                arrival(g * n_span + jp).wait_recv()
        for g in range(GROUPS):
            finish(g * n_span + jp, *(shares[6 * d + g:6 * d + g + 1] for d in range(3)))
    for p in range(near_count):
        @pl.when(is_partner(p // n_span, p % n_span))
        def _():
            arrival(p).wait_send()

    far_copy().wait_send()


def place_kernel(n_stream, n_span, recv_hbm, packed_hbm, fresh_ref, now_ref, prev_ref, targets, work, sem):
    i = lax.axis_index("stream")
    j = lax.axis_index("span")
    first = window_start(i, n_stream)
    far = lax.rem(i + n_stream // 2, n_stream)
    near_count = GROUPS * n_span
    copies = [
        pltpu.make_async_copy(recv_hbm.at[pl.ds(first, GROUPS)], targets.at[pl.ds(0, GROUPS)], sem.at[0]),
        pltpu.make_async_copy(recv_hbm.at[pl.ds(far, 1)], targets.at[pl.ds(GROUPS, 1)], sem.at[1]),
        pltpu.make_async_copy(packed_hbm, work, sem.at[2]),
    ]
    for copy in copies:
        copy.start()
    for copy in copies:
        copy.wait()
    pair = lanes((BRICK, 128)) // 2

    def put(p, row, start):
        block = fresh_ref[p]
        for k in range(SLOT):
            target = targets[row, 0, start + k]
            brick = jnp.maximum(target, 0)
            column = brick & 63
            moved = pltpu.roll(block, (2 * column - 2 * k) & 127, 1)
            mark = jnp.where(target >= 0, column, -1)
            base = pl.multiple_of((brick >> 6) * BRICK, 8)
            pltpu.store(work.at[pl.ds(base, BRICK), :], moved, mask=pair == mark)

    def put_group(g, carry):
        for jp in range(n_span):
            put(g * n_span + jp, g, jp * SLOT)
        return carry

    lax.fori_loop(0, GROUPS, put_group, 0)
    put(near_count, GROUPS, j * SLOT)

    def relayout(xb, carry):
        for dx in range(2):
            for tile in range(CY // 8):
                base = xb * (CY * ROW) + tile * 8 * ROW + dx * CHANS
                for c in range(VARS):
                    now_ref[c, 2 * xb + dx, tile * 8:tile * 8 + 8, :] = work[pl.ds(base + c, 8, ROW), :]
                    prev_ref[c, 2 * xb + dx, tile * 8:tile * 8 + 8, :] = work[pl.ds(base + VARS + c, 8, ROW), :]
        return carry

    lax.fori_loop(0, BX, relayout, 0)


def band(entries):
    source = lax.rem(lax.broadcasted_iota(jnp.int32, (2 * CZ, CZ), 0), CZ)
    away = source - lanes((2 * CZ, CZ))
    total = jnp.zeros((2 * CZ, CZ), F32)
    for offset, weight in entries:
        total = jnp.where(away == offset, weight, total)
    return total.astype(jnp.bfloat16)


def along_z(values, matrix):
    high = values.astype(jnp.bfloat16)
    low = (values - high.astype(F32)).astype(jnp.bfloat16)
    both = jnp.concatenate([high, low], 1)
    return jnp.dot(both, matrix, preferred_element_type=F32)


def advance_kernel(
    n_stream, n_span, jac, q_hbm, old_ref, out_ref,
    wide, pre, y_near_out, y_near_in, y_far_out, y_far_in,
    load_sem, near_send, near_recv, far_send, far_recv,
):
    i = lax.axis_index("stream")
    j = lax.axis_index("span")
    has = (i > 0, i < n_stream - 1, j > 0, j < n_span - 1)
    ids = ((i - 1, j), (i + 1, j), (i, j - 1), (i, j + 1))

    barrier = pltpu.get_barrier_semaphore()
    for side in range(4):
        @pl.when(has[side])
        def _():
            pl.semaphore_signal(barrier, inc=1, device_id=ids[side], device_id_type=MESH)

    load = pltpu.make_async_copy(q_hbm, wide.at[:, NEAR:NEAR + CX, PAD:PAD + CY, :], load_sem)
    load.start()

    for ref, width in ((wide, NEAR), (pre, FAR)):
        planes = CX + 2 * width

        @pl.when(~has[0])
        def _():
            ref[:, 0:width, :, :] = jnp.zeros((VARS, width, WY, CZ), F32)

        @pl.when(~has[1])
        def _():
            ref[:, width + CX:planes, :, :] = jnp.zeros((VARS, width, WY, CZ), F32)

    for edge in (0, PAD + CY):
        wide[:, NEAR:NEAR + CX, edge:edge + PAD, :] = jnp.zeros((VARS, CX, PAD, CZ), F32)
        pre[:, FAR:FAR + CX, edge:edge + PAD, :] = jnp.zeros((VARS, CX, PAD, CZ), F32)

    load.wait()

    def flat_rows(ref, width, c, x, y, count):
        planes = CX + 2 * width
        flat = ref.reshape(VARS * planes * WY, CZ)
        return flat, pl.ds((c * planes + width + x) * WY + PAD + y, count, WY)

    def pack_near(side):
        for c in range(VARS):
            for m in range(NEAR):
                for x in range(0, CX, 8):
                    flat, rows = flat_rows(wide, NEAR, c, x, m if side == 2 else CY - NEAR + m, 8)
                    y_near_out[side - 2, c, m, x:x + 8, :] = flat[rows, :]

    def near_terms(low, inner, outer):
        edge = inner * (8.0 / 36.0) - outer * (1.0 / 36.0)
        second = inner * (-1.0 / 36.0)
        return (edge, second) if low else (-edge, -second)

    def add_near_y(side):
        for x in range(0, CX, 8):
            terms = []
            for w in range(VARS):
                held = [y_near_in[side - 2, w, m, x:x + 8, :] for m in range(NEAR)]
                terms.append(near_terms(side == 2, *(reversed(held) if side == 2 else held)))
            for k in range(NEAR):
                for v in range(VARS):
                    flat, rows = flat_rows(pre, FAR, v, x, k if side == 2 else CY - 1 - k, 8)
                    total = flat[rows, :]
                    for w in range(VARS):
                        total = total + jac[25 + 5 * v + w] * terms[w][k]
                    flat[rows, :] = total

    def add_near_x(side):
        def step(tile, carry):
            rows = pl.ds(PAD + 8 * tile, 8)
            terms = []
            for w in range(VARS):
                held = [wide[w, m if side == 0 else NEAR + CX + m, rows, :] for m in range(NEAR)]
                terms.append(near_terms(side == 0, *(reversed(held) if side == 0 else held)))
            for k in range(NEAR):
                x = k if side == 0 else CX - 1 - k
                for v in range(VARS):
                    total = pre[v, FAR + x, rows, :]
                    for w in range(VARS):
                        total = total + jac[5 * v + w] * terms[w][k]
                    pre[v, FAR + x, rows, :] = total
            return carry

        return step

    inner_x, outer_x = ((4, 8, 0),), ((0, 4, 0), (12, 4, 4))
    y_order = {2: (2, 3, 4, 0, 1), 3: (0, 1, 2, 3, 4)}
    y_parts = ((0, 3), (3, 5), (5, 10))

    def pack_far(side, part):
        for at_plane in range(*y_parts[part]):
            m = y_order[side][at_plane] if part < 2 else at_plane - FAR
            for c in range(VARS):
                for x, count, at in inner_x if part < 2 else outer_x:
                    flat, rows = flat_rows(pre, FAR, c, x, m if side == 2 else CY - FAR + m, count)
                    y_far_out[side - 2, at_plane, c, at:at + count, :] = flat[rows, :]

    out_rows = out_ref.reshape(VARS * CX * CY, CZ)

    def add_far_y(side, outer):
        for c in range(VARS):
            order = y_order[side ^ 1]
            held = [y_far_in[side - 2, FAR + m if outer else order.index(m), c] for m in range(FAR)]
            for r in range(FAR):
                total = None
                for m in range(r, FAR) if side == 2 else range(r + 1):
                    away = r + FAR - m if side == 2 else FAR + m - r
                    term = (TAPS[away] * SCALE) * held[m]
                    total = term if total is None else total + term
                row = r if side == 2 else CY - FAR + r
                for x, count, at in outer_x if outer else inner_x:
                    rows = pl.ds((c * CX + x) * CY + row, count, CY)
                    out_rows[rows, :] = out_rows[rows, :] + total[at:at + count]

    def add_far_x(side):
        def step(c, carry):
            for tile in range(CY // 8):
                y = PAD + 8 * tile
                first_plane = 0 if side == 0 else FAR + CX
                held = [pre[c, first_plane + m, y:y + 8, :] for m in range(FAR)]
                for r in range(FAR):
                    total = None
                    for m in range(r, FAR) if side == 0 else range(r + 1):
                        away = r + FAR - m if side == 0 else FAR + m - r
                        term = (TAPS[away] * SCALE) * held[m]
                        total = term if total is None else total + term
                    x = r if side == 0 else CX - FAR + r
                    out_ref[c, x, 8 * tile:8 * tile + 8, :] = out_ref[c, x, 8 * tile:8 * tile + 8, :] + total
            return carry

        return step

    def near(side, part):
        if side == 0:
            src = wide.at[:, NEAR:2 * NEAR, PAD:PAD + CY, :]
            dst = wide.at[:, NEAR + CX:2 * NEAR + CX, PAD:PAD + CY, :]
        elif side == 1:
            src = wide.at[:, CX:NEAR + CX, PAD:PAD + CY, :]
            dst = wide.at[:, 0:NEAR, PAD:PAD + CY, :]
        else:
            src = y_near_out.at[side - 2]
            dst = y_near_in.at[3 - side]
        return pltpu.make_async_remote_copy(
            src_ref=src, dst_ref=dst, send_sem=near_send.at[side], recv_sem=near_recv.at[side ^ 1],
            device_id=ids[side], device_id_type=MESH,
        )

    inner = (NEAR, FAR)
    outer = (0, NEAR)
    x_parts = ((inner, (8, 24)), (inner, (0, 8)), (inner, (24, CY)), (outer, (0, CY)))

    def far(side, part):
        if side < 2:
            (low, high), (top, bottom) = x_parts[part]
            if side == 1:
                low, high = CX - high, CX - low
            shift = CX if side == 0 else -CX
            rows = slice(PAD + top, PAD + bottom)
            src = pre.at[:, FAR + low:FAR + high, rows, :]
            dst = pre.at[:, FAR + low + shift:FAR + high + shift, rows, :]
        else:
            low, high = y_parts[part]
            src = y_far_out.at[side - 2, low:high]
            dst = y_far_in.at[3 - side, low:high]
        return pltpu.make_async_remote_copy(
            src_ref=src, dst_ref=dst, send_sem=far_send.at[side, part], recv_sem=far_recv.at[side ^ 1, part],
            device_id=ids[side], device_id_type=MESH,
        )

    def start(make, side, part=0):
        @pl.when(has[side])
        def _():
            make(side, part).start()

    def finish_recv(make, side, part=0):
        @pl.when(has[side])
        def _():
            make(side ^ 1, part).wait_recv()

    def finish_send(make, side, part=0):
        @pl.when(has[side])
        def _():
            make(side, part).wait_send()

    expected = sum(jnp.where(flag, 1, 0) for flag in has)
    for side in (2, 3):
        pack_near(side)
    pl.semaphore_wait(barrier, expected)
    for side in range(4):
        start(near, side)

    slope = band(((1, 8.0), (-1, -8.0), (2, -1.0), (-2, 1.0)))

    def base_planes(n, carry):
        x = n * BATCH
        q = wide[:, pl.ds(NEAR + x, BATCH), PAD:PAD + CY, :]
        dz = along_z(q.reshape(VARS * BATCH * CY, CZ), slope).reshape(VARS, BATCH, CY, CZ)
        dz = dz * (-1.0 / 36.0)
        for v in range(VARS):
            total = (4.0 * q[v] - old_ref[v, pl.ds(x, BATCH)]) * (1.0 / 3.0)
            for w in range(VARS):
                total = total + jac[50 + 5 * v + w] * dz[w]
            pre[v, pl.ds(FAR + x, BATCH), PAD:PAD + CY, :] = total
        return carry

    lax.fori_loop(0, CX // BATCH, base_planes, 0)

    def rate_tile(x, y, offsets):
        dx, dy = [], []
        for w in range(VARS):
            def at(sx, sy):
                return wide[w, NEAR + x + sx, pl.ds(y + sy, 8), :]

            parts = [
                at(o, 0) * ((-8.0 if abs(o) == 1 else 1.0) * (1.0 if o > 0 else -1.0) / 36.0) for o in offsets
            ]
            dx.append(sum(parts[1:], parts[0]))
            dy.append((at(0, 1) - at(0, -1)) * (-8.0 / 36.0) + (at(0, 2) - at(0, -2)) * (1.0 / 36.0))
        for v in range(VARS):
            total = pre[v, FAR + x, pl.ds(y, 8), :]
            for w in range(VARS):
                total = total + jac[5 * v + w] * dx[w]
                total = total + jac[25 + 5 * v + w] * dy[w]
            pre[v, FAR + x, pl.ds(y, 8), :] = total

    def middle_planes(tiles):
        def step(n, carry):
            for x in (NEAR + 2 * n, NEAR + 2 * n + 1):
                for tile in tiles:
                    rate_tile(x, PAD + 8 * tile, (-2, -1, 1, 2))
            return carry

        return step

    def outer_planes(tile, carry):
        y = pl.multiple_of(PAD + 8 * tile, 8)
        for x in (0, 1, CX - 2, CX - 1):
            rate_tile(x, y, [o for o in (-2, -1, 1, 2) if 0 <= x + o < CX])
        return carry

    pairs = CX // 2 - NEAR
    lax.fori_loop(0, pairs, middle_planes((1, 2)), 0)
    start(far, 0, 0)
    start(far, 1, 0)
    lax.fori_loop(0, pairs, middle_planes((0, 3)), 0)
    for side in (2, 3):
        pack_far(side, 0)
        start(far, side, 0)
    lax.fori_loop(0, CY // 8, outer_planes, 0)
    for side in (2, 3):
        finish_recv(near, side)

        @pl.when(has[side])
        def _():
            add_near_y(side)

        pack_far(side, 1)
        start(far, side, 1)
    for part in (1, 2):
        start(far, 0, part)
        start(far, 1, part)
    for side in (0, 1):
        finish_recv(near, side)
        lax.fori_loop(0, CY // 8, add_near_x(side), 0)
        start(far, side, 3)
    for side in (2, 3):
        pack_far(side, 2)
        start(far, side, 2)

    tenth = band(tuple((o, TAPS[abs(o)]) for o in range(-5, 6)))

    def filter_y(x, c, tile):
        y = PAD + 8 * tile

        def at(sy):
            return pre[c, FAR + x, y + sy:y + sy + 8, :]

        total = (TAPS[0] * SCALE) * at(0)
        for m in range(1, 6):
            total = total + (TAPS[m] * SCALE) * (at(m) + at(-m))
        return total

    def first_planes(n, carry):
        x = n * BATCH
        p = pre[:, pl.ds(FAR + x, BATCH), PAD:PAD + CY, :]
        fz = along_z(p.reshape(VARS * BATCH * CY, CZ), tenth).reshape(VARS, BATCH, CY, CZ)
        total = p + SCALE * fz
        for c in range(VARS):
            for b in range(BATCH):
                for tile in range(CY // 8):
                    part = total[c, b, 8 * tile:8 * tile + 8] + filter_y(x + b, c, tile)
                    out_ref[c, x + b, 8 * tile:8 * tile + 8, :] = part
        return carry

    lax.fori_loop(0, CX // BATCH, first_planes, 0)

    def filter_x(c, carry):
        for tile in range(CY // 8):
            y = PAD + 8 * tile
            line = [pre[c, FAR + x, y:y + 8, :] for x in range(CX)]
            for x in range(CX):
                total = out_ref[c, x, 8 * tile:8 * tile + 8, :] + (TAPS[0] * SCALE) * line[x]
                for m in range(1, 6):
                    near_by = [line[x + o] for o in (m, -m) if 0 <= x + o < CX]
                    total = total + (TAPS[m] * SCALE) * sum(near_by[1:], near_by[0])
                out_ref[c, x, 8 * tile:8 * tile + 8, :] = total
        return carry

    lax.fori_loop(0, VARS, filter_x, 0)

    def receive_far_y(parts, outer):
        for side in (2, 3):
            for part in parts:
                finish_recv(far, side, part)

            @pl.when(has[side])
            def _():
                add_far_y(side, outer)

    receive_far_y((0, 1), False)
    for side in (0, 1):
        for part in range(4):
            finish_recv(far, side, part)
        lax.fori_loop(0, VARS, add_far_x(side), 0)
    receive_far_y((2,), True)
    for side in range(4):
        finish_send(near, side)
        for part in range(4 if side < 2 else 3):
            finish_send(far, side, part)


def per_device(n_stream, n_span, q_now, q_prev, jacobians, fractions, send_blocks, recv_blocks):
    vmem = pl.BlockSpec(memory_space=pltpu.VMEM)
    anywhere = pl.BlockSpec(memory_space=pl.ANY)
    slots = GROUPS * n_span + 1
    width = n_span * SLOT
    sending = send_blocks.reshape(n_stream, 1, width)
    receiving = recv_blocks.reshape(n_stream, 1, width)
    offsets = fractions.reshape(3, n_stream, width)
    limit = 48 * 1024 * 1024
    packed, fresh = pl.pallas_call(
        functools.partial(exchange_kernel, n_stream, n_span),
        name="exchange",
        out_shape=(
            jax.ShapeDtypeStruct((ROWS, CZ), F32),
            jax.ShapeDtypeStruct((slots, BRICK, 128), F32),
        ),
        in_specs=[anywhere] * 4,
        out_specs=(vmem, vmem),
        scratch_shapes=[
            pltpu.SMEM((GROUPS + 1, 1, width), jnp.int32),
            pltpu.VMEM((3, n_stream, width), F32),
            pltpu.VMEM(q_now.shape, F32),
            pltpu.VMEM(q_now.shape, F32),
            pltpu.VMEM((slots, ROW, 128), F32),
            pltpu.VMEM((slots, ROW, 128), F32),
            pltpu.SemaphoreType.DMA((3,)),
            pltpu.SemaphoreType.DMA((2 * PARTS,)),
            pltpu.SemaphoreType.DMA((slots,)),
            pltpu.SemaphoreType.DMA((slots,)),
        ],
        compiler_params=pltpu.CompilerParams(
            collective_id=0, has_side_effects=True, vmem_limit_bytes=48 * 1024 * 1024
        ),
    )(*(pltpu.with_memory_space_constraint(x, pltpu.HBM) for x in (sending, offsets, q_now, q_prev)))
    shape = jax.ShapeDtypeStruct(q_now.shape, F32)
    now, older = pl.pallas_call(
        functools.partial(place_kernel, n_stream, n_span),
        name="place",
        out_shape=(shape, shape),
        in_specs=[anywhere, anywhere, vmem],
        out_specs=(vmem, vmem),
        scratch_shapes=[
            pltpu.SMEM((GROUPS + 1, 1, width), jnp.int32),
            pltpu.VMEM((ROWS, CZ), F32),
            pltpu.SemaphoreType.DMA((3,)),
        ],
        compiler_params=pltpu.CompilerParams(vmem_limit_bytes=limit),
    )(receiving, packed, fresh)
    return pl.pallas_call(
        functools.partial(advance_kernel, n_stream, n_span),
        name="advance",
        out_shape=shape,
        in_specs=[pl.BlockSpec(memory_space=pltpu.SMEM), anywhere, vmem],
        out_specs=vmem,
        scratch_shapes=[
            pltpu.VMEM((VARS, CX + 2 * NEAR, WY, CZ), F32),
            pltpu.VMEM((VARS, CX + 2 * FAR, WY, CZ), F32),
            pltpu.VMEM((2, VARS, NEAR, CX, CZ), F32),
            pltpu.VMEM((2, VARS, NEAR, CX, CZ), F32),
            pltpu.VMEM((2, 2 * FAR, VARS, CX // 2, CZ), F32),
            pltpu.VMEM((2, 2 * FAR, VARS, CX // 2, CZ), F32),
            pltpu.SemaphoreType.DMA,
            pltpu.SemaphoreType.DMA((4,)),
            pltpu.SemaphoreType.DMA((4,)),
            pltpu.SemaphoreType.DMA((4, 4)),
            pltpu.SemaphoreType.DMA((4, 4)),
        ],
        compiler_params=pltpu.CompilerParams(
            collective_id=1, has_side_effects=True, vmem_limit_bytes=limit
        ),
    )(jacobians.reshape(-1), now, older)


def solution(mesh):
    in_specs = (
        P(None, "stream", "span", None),
        P(None, "stream", "span", None),
        P(),
        P(None, ("stream", "span"), None),
        P(("stream", "span"), None),
        P(("stream", "span"), None),
    )
    out_specs = P(None, "stream", "span", None)
    body = functools.partial(per_device, mesh.shape["stream"], mesh.shape["span"])
    return jax.shard_map(
        body, mesh=mesh, in_specs=in_specs, out_specs=out_specs, check_vma=False
    )
```

```python
import functools

import jax
import jax.numpy as jnp
from jax import lax
from jax.experimental import pallas as pl
from jax.experimental.pallas import tpu as pltpu
from jax.sharding import PartitionSpec as P

MESH = pl.DeviceIdType.MESH
F32 = jnp.float32
VARS = 5
CHANS = 10
SLOT = 32
REACH = 2
PARTS = 4
EARLY = 2
BATCH = 4
GROUPS = 2 * REACH + 1
CX, CY, CZ = 16, 32, 128
BX, BY = CX // 2, CY // 2
ROW = 2 * CHANS
BRICK = 2 * ROW
ROWS = BX * CY * ROW
PAD = 8
WY = CY + 2 * PAD
NEAR, FAR = 2, 5
SCALE = 0.6 / 1024.0
TAPS = (-252.0, 210.0, -120.0, 45.0, -10.0, 1.0)


def lanes(shape):
    return lax.broadcasted_iota(jnp.int32, shape, len(shape) - 1)


def window_start(i, n_stream):
    return jnp.minimum(jnp.maximum(i - REACH, 0), n_stream - GROUPS)


def exchange_kernel(
    n_stream, n_span, send_hbm, frac_hbm, now_hbm, prev_hbm, packed_ref, fresh_ref,
    picks, frac_ref, now_ref, prev_ref, sending, arrived, pick_sem, load_sem, send_sem, recv_sem,
):
    i = lax.axis_index("stream")
    j = lax.axis_index("span")
    first = window_start(i, n_stream)
    far = lax.rem(i + n_stream // 2, n_stream)
    near_count = GROUPS * n_span
    far_slot = near_count

    def is_partner(g, jp):
        t = first + g
        return (t >= i - REACH) & (t <= i + REACH) & ((t != i) | (jp != j))

    loads = [
        pltpu.make_async_copy(
            src.at[:, pl.ds(part * CX // PARTS, CX // PARTS)],
            dst.at[:, pl.ds(part * CX // PARTS, CX // PARTS)],
            load_sem.at[2 * part + n],
        )
        for part in range(PARTS)
        for n, (src, dst) in enumerate(((now_hbm, now_ref), (prev_hbm, prev_ref)))
    ]
    others = [
        pltpu.make_async_copy(
            send_hbm.at[pl.ds(first, GROUPS)], picks.at[pl.ds(0, GROUPS)], pick_sem.at[0]
        ),
        pltpu.make_async_copy(
            send_hbm.at[pl.ds(far, 1)], picks.at[pl.ds(GROUPS, 1)], pick_sem.at[1]
        ),
        pltpu.make_async_copy(frac_hbm, frac_ref, pick_sem.at[2]),
    ]
    for copy in loads + others:
        copy.start()

    barrier = pltpu.get_barrier_semaphore()
    for g in range(GROUPS):
        for jp in range(n_span):
            @pl.when(is_partner(g, jp))
            def _():
                pl.semaphore_signal(barrier, inc=1, device_id=(first + g, jp), device_id_type=MESH)
    pl.semaphore_signal(barrier, inc=1, device_id=(far, j), device_id_type=MESH)

    def relayout(xb, carry):
        for dx in range(2):
            for tile in range(CY // 8):
                base = xb * (CY * ROW) + tile * 8 * ROW + dx * CHANS
                for c in range(VARS):
                    packed_ref[pl.ds(base + c, 8, ROW), :] = now_ref[c, 2 * xb + dx, tile * 8:tile * 8 + 8, :]
                    packed_ref[pl.ds(base + VARS + c, 8, ROW), :] = prev_ref[c, 2 * xb + dx, tile * 8:tile * 8 + 8, :]
        return carry

    for part in range(PARTS):
        loads[2 * part].wait()
        loads[2 * part + 1].wait()
        lax.fori_loop(part * BX // PARTS, (part + 1) * BX // PARTS, relayout, 0)
    for copy in others:
        copy.wait()

    half = lanes((ROW, 128)) < 64
    pair = lanes((BRICK, 128)) // 2

    def pack(p, row, start):
        total = jnp.zeros((BRICK, 128), F32)
        for k in range(SLOT):
            brick = jnp.maximum(picks[row, 0, start + k], 0)
            moved = pltpu.roll(
                packed_ref[pl.ds((brick >> 6) * BRICK, BRICK), :], (2 * k - 2 * (brick & 63)) & 127, 1
            )
            total = jnp.where(pair == k, moved, total)
        sending[p] = jnp.where(half, total[:ROW], pltpu.roll(total[ROW:], 64, 1))

    def far_copy():
        return pltpu.make_async_remote_copy(
            src_ref=sending.at[far_slot], dst_ref=arrived.at[far_slot],
            send_sem=send_sem.at[far_slot], recv_sem=recv_sem.at[far_slot],
            device_id=(far, j), device_id_type=MESH,
        )

    def near_copy(p, g, jp):
        t = first + g
        slot = (i - window_start(t, n_stream)) * n_span + j
        slot = jnp.minimum(jnp.maximum(slot, 0), near_count - 1)
        return pltpu.make_async_remote_copy(
            src_ref=sending.at[p], dst_ref=arrived.at[slot],
            send_sem=send_sem.at[p], recv_sem=recv_sem.at[slot],
            device_id=(t, jp), device_id_type=MESH,
        )

    def arrival(p):
        return pltpu.make_async_remote_copy(
            src_ref=sending.at[p], dst_ref=arrived.at[p],
            send_sem=send_sem.at[p], recv_sem=recv_sem.at[p],
            device_id=(first + p // n_span, lax.rem(p, n_span)), device_id_type=MESH,
        )

    def start_near(g, jp):
        @pl.when(is_partner(g, jp))
        def _():
            near_copy(g * n_span + jp, g, jp).start()

    rows_near = jnp.minimum(i + REACH, n_stream - 1) - jnp.maximum(i - REACH, 0) + 1

    def column(n):
        return lax.rem(j + jnp.where(n == 0, 2, jnp.where(n == 1, 1, jnp.where(n == 2, 3, 0))), n_span)

    def send(n, carry):
        jp = column(n)
        for g in range(GROUPS):
            pack(g * n_span + jp, g, jp * SLOT)

        @pl.when(n == 0)
        def _():
            pack(far_slot, GROUPS, j * SLOT)

        @pl.when(n == EARLY - 1)
        def _():
            pl.semaphore_wait(barrier, rows_near * n_span)
            for early in range(EARLY):
                for g in (0, 4, 1, 3, 2):
                    start_near(g, column(early))
                if early == 0:
                    far_copy().start()

        @pl.when(n >= EARLY)
        def _():
            for g in (0, 4, 1, 3, 2):
                start_near(g, jp)

        return carry

    lax.fori_loop(0, n_span, send, 0)
    own = (i - first) * n_span + j
    arrived[own] = sending[own]

    near_frac = [frac_ref[d, pl.ds(first, GROUPS), :] for d in range(3)]
    far_frac = [frac_ref[d, pl.ds(far, 1), :] for d in range(3)]
    table = jnp.concatenate([part for d in range(3) for part in (near_frac[d], far_frac[d])], 0)

    def spread(which):
        source = lax.broadcasted_iota(jnp.int32, (128, 128), 0)
        wanted = which * SLOT + lax.rem(lanes((128, 128)), 64) // 2
        chosen = jnp.where(source == wanted, 1.0, 0.0).astype(F32)
        return jnp.dot(table, chosen, precision=lax.Precision.HIGHEST, preferred_element_type=F32)

    even = lanes((CHANS, 128)) % 2 == 0
    low_half = lanes((CHANS, 128)) < 64

    def finish(p, fx, fy, fz):
        block = arrived[p]
        upper = block[CHANS:]
        lower = (1.0 - fx) * block[:CHANS] + fx * upper
        done = []
        for v in (lower, upper):
            v = jnp.where(low_half, (1.0 - fy) * v + fy * pltpu.roll(v, 64, 1), v)
            v = jnp.where(even, (1.0 - fz) * v + fz * pltpu.roll(v, 127, 1), v)
            done.append(v)
        both = jnp.concatenate(done, 0)
        fresh_ref[p, 0:ROW, :] = both
        fresh_ref[p, ROW:BRICK, :] = pltpu.roll(both, 64, 1)

    all_shares = [spread(column(n)) for n in range(n_span)]
    far_shares = all_shares[n_span - 1]
    for n in range(n_span):
        jp = column(n)
        shares = all_shares[n]
        if n == 1:
            far_copy().wait_recv()
            finish(far_slot, *(far_shares[6 * d + GROUPS:6 * d + GROUPS + 1] for d in range(3)))
        for g in range(GROUPS):
            @pl.when(is_partner(g, jp))
            def _():
                arrival(g * n_span + jp).wait_recv()
        for g in range(GROUPS):
            finish(g * n_span + jp, *(shares[6 * d + g:6 * d + g + 1] for d in range(3)))
    for p in range(near_count):
        @pl.when(is_partner(p // n_span, p % n_span))
        def _():
            arrival(p).wait_send()

    far_copy().wait_send()


def place_kernel(n_stream, n_span, recv_hbm, packed_hbm, fresh_ref, now_ref, prev_ref, targets, work, sem):
    i = lax.axis_index("stream")
    j = lax.axis_index("span")
    first = window_start(i, n_stream)
    far = lax.rem(i + n_stream // 2, n_stream)
    near_count = GROUPS * n_span
    copies = [
        pltpu.make_async_copy(recv_hbm.at[pl.ds(first, GROUPS)], targets.at[pl.ds(0, GROUPS)], sem.at[0]),
        pltpu.make_async_copy(recv_hbm.at[pl.ds(far, 1)], targets.at[pl.ds(GROUPS, 1)], sem.at[1]),
        pltpu.make_async_copy(packed_hbm, work, sem.at[2]),
    ]
    for copy in copies:
        copy.start()
    for copy in copies:
        copy.wait()
    pair = lanes((BRICK, 128)) // 2

    def put(p, row, start):
        block = fresh_ref[p]
        for k in range(SLOT):
            target = targets[row, 0, start + k]
            brick = jnp.maximum(target, 0)
            column = brick & 63
            moved = pltpu.roll(block, (2 * column - 2 * k) & 127, 1)
            mark = jnp.where(target >= 0, column, -1)
            base = pl.multiple_of((brick >> 6) * BRICK, 8)
            pltpu.store(work.at[pl.ds(base, BRICK), :], moved, mask=pair == mark)

    for g in range(GROUPS):
        for jp in range(n_span):
            put(g * n_span + jp, g, jp * SLOT)
    put(near_count, GROUPS, j * SLOT)

    def relayout(xb, carry):
        for dx in range(2):
            for tile in range(CY // 8):
                base = xb * (CY * ROW) + tile * 8 * ROW + dx * CHANS
                for c in range(VARS):
                    now_ref[c, 2 * xb + dx, tile * 8:tile * 8 + 8, :] = work[pl.ds(base + c, 8, ROW), :]
                    prev_ref[c, 2 * xb + dx, tile * 8:tile * 8 + 8, :] = work[pl.ds(base + VARS + c, 8, ROW), :]
        return carry

    lax.fori_loop(0, BX, relayout, 0)


def band(entries):
    source = lax.rem(lax.broadcasted_iota(jnp.int32, (2 * CZ, CZ), 0), CZ)
    away = source - lanes((2 * CZ, CZ))
    total = jnp.zeros((2 * CZ, CZ), F32)
    for offset, weight in entries:
        total = jnp.where(away == offset, weight, total)
    return total.astype(jnp.bfloat16)


def along_z(values, matrix):
    high = values.astype(jnp.bfloat16)
    low = (values - high.astype(F32)).astype(jnp.bfloat16)
    both = jnp.concatenate([high, low], 1)
    return jnp.dot(both, matrix, preferred_element_type=F32)


def advance_kernel(
    n_stream, n_span, jac, q_hbm, old_ref, out_ref,
    wide, pre, y_near_out, y_near_in, y_far_out, y_far_in,
    load_sem, near_send, near_recv, far_send, far_recv,
):
    i = lax.axis_index("stream")
    j = lax.axis_index("span")
    has = (i > 0, i < n_stream - 1, j > 0, j < n_span - 1)
    ids = ((i - 1, j), (i + 1, j), (i, j - 1), (i, j + 1))

    barrier = pltpu.get_barrier_semaphore()
    for side in range(4):
        @pl.when(has[side])
        def _():
            pl.semaphore_signal(barrier, inc=1, device_id=ids[side], device_id_type=MESH)

    load = pltpu.make_async_copy(q_hbm, wide.at[:, NEAR:NEAR + CX, PAD:PAD + CY, :], load_sem)
    load.start()

    for ref, width in ((wide, NEAR), (pre, FAR)):
        planes = CX + 2 * width

        @pl.when(~has[0])
        def _():
            ref[:, 0:width, :, :] = jnp.zeros((VARS, width, WY, CZ), F32)

        @pl.when(~has[1])
        def _():
            ref[:, width + CX:planes, :, :] = jnp.zeros((VARS, width, WY, CZ), F32)

    for edge in (0, PAD + CY):
        wide[:, NEAR:NEAR + CX, edge:edge + PAD, :] = jnp.zeros((VARS, CX, PAD, CZ), F32)
        pre[:, FAR:FAR + CX, edge:edge + PAD, :] = jnp.zeros((VARS, CX, PAD, CZ), F32)

    load.wait()

    def flat_rows(ref, width, c, x, y, count):
        planes = CX + 2 * width
        flat = ref.reshape(VARS * planes * WY, CZ)
        return flat, pl.ds((c * planes + width + x) * WY + PAD + y, count, WY)

    def pack_near(side):
        for c in range(VARS):
            for m in range(NEAR):
                for x in range(0, CX, 8):
                    flat, rows = flat_rows(wide, NEAR, c, x, m if side == 2 else CY - NEAR + m, 8)
                    y_near_out[side - 2, c, m, x:x + 8, :] = flat[rows, :]

    def near_terms(low, inner, outer):
        edge = inner * (8.0 / 36.0) - outer * (1.0 / 36.0)
        second = inner * (-1.0 / 36.0)
        return (edge, second) if low else (-edge, -second)

    def add_near_y(side):
        for x in range(0, CX, 8):
            terms = []
            for w in range(VARS):
                held = [y_near_in[side - 2, w, m, x:x + 8, :] for m in range(NEAR)]
                terms.append(near_terms(side == 2, *(reversed(held) if side == 2 else held)))
            for k in range(NEAR):
                for v in range(VARS):
                    flat, rows = flat_rows(pre, FAR, v, x, k if side == 2 else CY - 1 - k, 8)
                    total = flat[rows, :]
                    for w in range(VARS):
                        total = total + jac[25 + 5 * v + w] * terms[w][k]
                    flat[rows, :] = total

    def add_near_x(side):
        def step(tile, carry):
            rows = pl.ds(PAD + 8 * tile, 8)
            terms = []
            for w in range(VARS):
                held = [wide[w, m if side == 0 else NEAR + CX + m, rows, :] for m in range(NEAR)]
                terms.append(near_terms(side == 0, *(reversed(held) if side == 0 else held)))
            for k in range(NEAR):
                x = k if side == 0 else CX - 1 - k
                for v in range(VARS):
                    total = pre[v, FAR + x, rows, :]
                    for w in range(VARS):
                        total = total + jac[5 * v + w] * terms[w][k]
                    pre[v, FAR + x, rows, :] = total
            return carry

        return step

    inner_x, outer_x = ((4, 8, 0),), ((0, 4, 0), (12, 4, 4))
    y_order = {2: (2, 3, 4, 0, 1), 3: (0, 1, 2, 3, 4)}
    y_parts = ((0, 3), (3, 5), (5, 10))

    def pack_far(side, part):
        for at_plane in range(*y_parts[part]):
            m = y_order[side][at_plane] if part < 2 else at_plane - FAR
            for c in range(VARS):
                for x, count, at in inner_x if part < 2 else outer_x:
                    flat, rows = flat_rows(pre, FAR, c, x, m if side == 2 else CY - FAR + m, count)
                    y_far_out[side - 2, at_plane, c, at:at + count, :] = flat[rows, :]

    out_rows = out_ref.reshape(VARS * CX * CY, CZ)

    def add_far_y(side, outer):
        for c in range(VARS):
            order = y_order[side ^ 1]
            held = [y_far_in[side - 2, FAR + m if outer else order.index(m), c] for m in range(FAR)]
            for r in range(FAR):
                total = None
                for m in range(r, FAR) if side == 2 else range(r + 1):
                    away = r + FAR - m if side == 2 else FAR + m - r
                    term = (TAPS[away] * SCALE) * held[m]
                    total = term if total is None else total + term
                row = r if side == 2 else CY - FAR + r
                for x, count, at in outer_x if outer else inner_x:
                    rows = pl.ds((c * CX + x) * CY + row, count, CY)
                    out_rows[rows, :] = out_rows[rows, :] + total[at:at + count]

    def add_far_x(side):
        def step(c, carry):
            for tile in range(CY // 8):
                y = PAD + 8 * tile
                first_plane = 0 if side == 0 else FAR + CX
                held = [pre[c, first_plane + m, y:y + 8, :] for m in range(FAR)]
                for r in range(FAR):
                    total = None
                    for m in range(r, FAR) if side == 0 else range(r + 1):
                        away = r + FAR - m if side == 0 else FAR + m - r
                        term = (TAPS[away] * SCALE) * held[m]
                        total = term if total is None else total + term
                    x = r if side == 0 else CX - FAR + r
                    out_ref[c, x, 8 * tile:8 * tile + 8, :] = out_ref[c, x, 8 * tile:8 * tile + 8, :] + total
            return carry

        return step

    def near(side, part):
        if side == 0:
            src = wide.at[:, NEAR:2 * NEAR, PAD:PAD + CY, :]
            dst = wide.at[:, NEAR + CX:2 * NEAR + CX, PAD:PAD + CY, :]
        elif side == 1:
            src = wide.at[:, CX:NEAR + CX, PAD:PAD + CY, :]
            dst = wide.at[:, 0:NEAR, PAD:PAD + CY, :]
        else:
            src = y_near_out.at[side - 2]
            dst = y_near_in.at[3 - side]
        return pltpu.make_async_remote_copy(
            src_ref=src, dst_ref=dst, send_sem=near_send.at[side], recv_sem=near_recv.at[side ^ 1],
            device_id=ids[side], device_id_type=MESH,
        )

    inner = (NEAR, FAR)
    outer = (0, NEAR)
    x_parts = ((inner, (8, 24)), (inner, (0, 8)), (inner, (24, CY)), (outer, (0, CY)))

    def far(side, part):
        if side < 2:
            (low, high), (top, bottom) = x_parts[part]
            if side == 1:
                low, high = CX - high, CX - low
            shift = CX if side == 0 else -CX
            rows = slice(PAD + top, PAD + bottom)
            src = pre.at[:, FAR + low:FAR + high, rows, :]
            dst = pre.at[:, FAR + low + shift:FAR + high + shift, rows, :]
        else:
            low, high = y_parts[part]
            src = y_far_out.at[side - 2, low:high]
            dst = y_far_in.at[3 - side, low:high]
        return pltpu.make_async_remote_copy(
            src_ref=src, dst_ref=dst, send_sem=far_send.at[side, part], recv_sem=far_recv.at[side ^ 1, part],
            device_id=ids[side], device_id_type=MESH,
        )

    def start(make, side, part=0):
        @pl.when(has[side])
        def _():
            make(side, part).start()

    def finish_recv(make, side, part=0):
        @pl.when(has[side])
        def _():
            make(side ^ 1, part).wait_recv()

    def finish_send(make, side, part=0):
        @pl.when(has[side])
        def _():
            make(side, part).wait_send()

    expected = sum(jnp.where(flag, 1, 0) for flag in has)
    for side in (2, 3):
        pack_near(side)
    pl.semaphore_wait(barrier, expected)
    for side in range(4):
        start(near, side)

    slope = band(((1, 8.0), (-1, -8.0), (2, -1.0), (-2, 1.0)))

    def base_planes(n, carry):
        x = n * BATCH
        q = wide[:, pl.ds(NEAR + x, BATCH), PAD:PAD + CY, :]
        dz = along_z(q.reshape(VARS * BATCH * CY, CZ), slope).reshape(VARS, BATCH, CY, CZ)
        dz = dz * (-1.0 / 36.0)
        for v in range(VARS):
            total = (4.0 * q[v] - old_ref[v, pl.ds(x, BATCH)]) * (1.0 / 3.0)
            for w in range(VARS):
                total = total + jac[50 + 5 * v + w] * dz[w]
            pre[v, pl.ds(FAR + x, BATCH), PAD:PAD + CY, :] = total
        return carry

    lax.fori_loop(0, CX // BATCH, base_planes, 0)

    def rate_tile(x, y, offsets):
        dx, dy = [], []
        for w in range(VARS):
            def at(sx, sy):
                return wide[w, NEAR + x + sx, pl.ds(y + sy, 8), :]

            parts = [
                at(o, 0) * ((-8.0 if abs(o) == 1 else 1.0) * (1.0 if o > 0 else -1.0) / 36.0) for o in offsets
            ]
            dx.append(sum(parts[1:], parts[0]))
            dy.append((at(0, 1) - at(0, -1)) * (-8.0 / 36.0) + (at(0, 2) - at(0, -2)) * (1.0 / 36.0))
        for v in range(VARS):
            total = pre[v, FAR + x, pl.ds(y, 8), :]
            for w in range(VARS):
                total = total + jac[5 * v + w] * dx[w]
                total = total + jac[25 + 5 * v + w] * dy[w]
            pre[v, FAR + x, pl.ds(y, 8), :] = total

    def middle_planes(tiles):
        def step(n, carry):
            for x in (NEAR + 2 * n, NEAR + 2 * n + 1):
                for tile in tiles:
                    rate_tile(x, PAD + 8 * tile, (-2, -1, 1, 2))
            return carry

        return step

    def outer_planes(tile, carry):
        y = pl.multiple_of(PAD + 8 * tile, 8)
        for x in (0, 1, CX - 2, CX - 1):
            rate_tile(x, y, [o for o in (-2, -1, 1, 2) if 0 <= x + o < CX])
        return carry

    pairs = CX // 2 - NEAR
    lax.fori_loop(0, pairs, middle_planes((1, 2)), 0)
    start(far, 0, 0)
    start(far, 1, 0)
    lax.fori_loop(0, pairs, middle_planes((0, 3)), 0)
    for side in (2, 3):
        pack_far(side, 0)
        start(far, side, 0)
    lax.fori_loop(0, CY // 8, outer_planes, 0)
    for side in (2, 3):
        finish_recv(near, side)

        @pl.when(has[side])
        def _():
            add_near_y(side)

        pack_far(side, 1)
        start(far, side, 1)
    for part in (1, 2):
        start(far, 0, part)
        start(far, 1, part)
    for side in (0, 1):
        finish_recv(near, side)
        lax.fori_loop(0, CY // 8, add_near_x(side), 0)
        start(far, side, 3)
    for side in (2, 3):
        pack_far(side, 2)
        start(far, side, 2)

    tenth = band(tuple((o, TAPS[abs(o)]) for o in range(-5, 6)))

    def filter_y(x, c, tile):
        y = PAD + 8 * tile

        def at(sy):
            return pre[c, FAR + x, y + sy:y + sy + 8, :]

        total = (TAPS[0] * SCALE) * at(0)
        for m in range(1, 6):
            total = total + (TAPS[m] * SCALE) * (at(m) + at(-m))
        return total

    def first_planes(n, carry):
        x = n * BATCH
        p = pre[:, pl.ds(FAR + x, BATCH), PAD:PAD + CY, :]
        fz = along_z(p.reshape(VARS * BATCH * CY, CZ), tenth).reshape(VARS, BATCH, CY, CZ)
        total = p + SCALE * fz
        for c in range(VARS):
            for b in range(BATCH):
                for tile in range(CY // 8):
                    part = total[c, b, 8 * tile:8 * tile + 8] + filter_y(x + b, c, tile)
                    out_ref[c, x + b, 8 * tile:8 * tile + 8, :] = part
        return carry

    lax.fori_loop(0, CX // BATCH, first_planes, 0)

    def filter_x(c, carry):
        for tile in range(CY // 8):
            y = PAD + 8 * tile
            line = [pre[c, FAR + x, y:y + 8, :] for x in range(CX)]
            for x in range(CX):
                total = out_ref[c, x, 8 * tile:8 * tile + 8, :] + (TAPS[0] * SCALE) * line[x]
                for m in range(1, 6):
                    near_by = [line[x + o] for o in (m, -m) if 0 <= x + o < CX]
                    total = total + (TAPS[m] * SCALE) * sum(near_by[1:], near_by[0])
                out_ref[c, x, 8 * tile:8 * tile + 8, :] = total
        return carry

    lax.fori_loop(0, VARS, filter_x, 0)

    def receive_far_y(parts, outer):
        for side in (2, 3):
            for part in parts:
                finish_recv(far, side, part)

            @pl.when(has[side])
            def _():
                add_far_y(side, outer)

    receive_far_y((0, 1), False)
    for side in (0, 1):
        for part in range(4):
            finish_recv(far, side, part)
        lax.fori_loop(0, VARS, add_far_x(side), 0)
    receive_far_y((2,), True)
    for side in range(4):
        finish_send(near, side)
        for part in range(4 if side < 2 else 3):
            finish_send(far, side, part)


def per_device(n_stream, n_span, q_now, q_prev, jacobians, fractions, send_blocks, recv_blocks):
    vmem = pl.BlockSpec(memory_space=pltpu.VMEM)
    anywhere = pl.BlockSpec(memory_space=pl.ANY)
    slots = GROUPS * n_span + 1
    width = n_span * SLOT
    sending = send_blocks.reshape(n_stream, 1, width)
    receiving = recv_blocks.reshape(n_stream, 1, width)
    offsets = fractions.reshape(3, n_stream, width)
    limit = 48 * 1024 * 1024
    packed, fresh = pl.pallas_call(
        functools.partial(exchange_kernel, n_stream, n_span),
        name="exchange",
        out_shape=(
            jax.ShapeDtypeStruct((ROWS, CZ), F32),
            jax.ShapeDtypeStruct((slots, BRICK, 128), F32),
        ),
        in_specs=[anywhere] * 4,
        out_specs=(vmem, vmem),
        scratch_shapes=[
            pltpu.SMEM((GROUPS + 1, 1, width), jnp.int32),
            pltpu.VMEM((3, n_stream, width), F32),
            pltpu.VMEM(q_now.shape, F32),
            pltpu.VMEM(q_now.shape, F32),
            pltpu.VMEM((slots, ROW, 128), F32),
            pltpu.VMEM((slots, ROW, 128), F32),
            pltpu.SemaphoreType.DMA((3,)),
            pltpu.SemaphoreType.DMA((2 * PARTS,)),
            pltpu.SemaphoreType.DMA((slots,)),
            pltpu.SemaphoreType.DMA((slots,)),
        ],
        compiler_params=pltpu.CompilerParams(
            collective_id=0, has_side_effects=True, vmem_limit_bytes=48 * 1024 * 1024
        ),
    )(*(pltpu.with_memory_space_constraint(x, pltpu.HBM) for x in (sending, offsets, q_now, q_prev)))
    shape = jax.ShapeDtypeStruct(q_now.shape, F32)
    now, older = pl.pallas_call(
        functools.partial(place_kernel, n_stream, n_span),
        name="place",
        out_shape=(shape, shape),
        in_specs=[anywhere, anywhere, vmem],
        out_specs=(vmem, vmem),
        scratch_shapes=[
            pltpu.SMEM((GROUPS + 1, 1, width), jnp.int32),
            pltpu.VMEM((ROWS, CZ), F32),
            pltpu.SemaphoreType.DMA((3,)),
        ],
        compiler_params=pltpu.CompilerParams(vmem_limit_bytes=limit),
    )(receiving, packed, fresh)
    return pl.pallas_call(
        functools.partial(advance_kernel, n_stream, n_span),
        name="advance",
        out_shape=shape,
        in_specs=[pl.BlockSpec(memory_space=pltpu.SMEM), anywhere, vmem],
        out_specs=vmem,
        scratch_shapes=[
            pltpu.VMEM((VARS, CX + 2 * NEAR, WY, CZ), F32),
            pltpu.VMEM((VARS, CX + 2 * FAR, WY, CZ), F32),
            pltpu.VMEM((2, VARS, NEAR, CX, CZ), F32),
            pltpu.VMEM((2, VARS, NEAR, CX, CZ), F32),
            pltpu.VMEM((2, 2 * FAR, VARS, CX // 2, CZ), F32),
            pltpu.VMEM((2, 2 * FAR, VARS, CX // 2, CZ), F32),
            pltpu.SemaphoreType.DMA,
            pltpu.SemaphoreType.DMA((4,)),
            pltpu.SemaphoreType.DMA((4,)),
            pltpu.SemaphoreType.DMA((4, 4)),
            pltpu.SemaphoreType.DMA((4, 4)),
        ],
        compiler_params=pltpu.CompilerParams(
            collective_id=1, has_side_effects=True, vmem_limit_bytes=limit
        ),
    )(jacobians.reshape(-1), now, older)


def solution(mesh):
    in_specs = (
        P(None, "stream", "span", None),
        P(None, "stream", "span", None),
        P(),
        P(None, ("stream", "span"), None),
        P(("stream", "span"), None),
        P(("stream", "span"), None),
    )
    out_specs = P(None, "stream", "span", None)
    body = functools.partial(per_device, mesh.shape["stream"], mesh.shape["span"])
    return jax.shard_map(
        body, mesh=mesh, in_specs=in_specs, out_specs=out_specs, check_vma=False
    )
```
